32 devices in a mesh: dp: 4 (over y, x), seq: 8 (over z, core).
Axes of the slice: x: 2, y: 2, z: 4, core: 2. Of those that a mesh axis runs over, the one named last changes fastest.
Arguments:
- conv_input: bfloat16 [4096, 5376], P(('dp', 'seq')), may hold values from -6 to 6
- doc_start: int32 [4096], P(('dp', 'seq')), may hold values 0 or 1
- conv_weight: float32 [4, 5376], replicated, may hold values from -3 to 3
- conv_bias: float32 [5376], replicated, may hold values from -0.5 to 0.5
- dt_raw: float32 [4096, 80], P(('dp', 'seq')), may hold values from -3 to 3
- dt_bias: float32 [80], replicated, may hold values from -5.5 to -4.2
- a_log: float32 [80], replicated, may hold values from -9 to 2, as said below
- skip_gain: float32 [80], replicated, may hold values from 0.5 to 1.5
- cotangent: bfloat16 [4096, 5120], P(('dp', 'seq')), may hold values from -6 to 6
Outputs:
- ssm_output: bfloat16 [4096, 5120], P(('dp', 'seq'))
- grad_input: bfloat16 [4096, 5376], P(('dp', 'seq'))
- grad_conv_weight: float32 [4, 5376], replicated
- grad_conv_bias: float32 [5376], replicated
- grad_dt_bias: float32 [80], replicated
- grad_a_log: float32 [80], replicated
- grad_skip_gain: float32 [80], replicated
The draws below stay inside these ranges and needn't reach their ends.
Inputs may be any that keep to these rules, and one draw needn't show every extreme that they name: `doc_start`: 1 marks the first token of a document; documents may cross shard boundaries. One value per head; exp(a_log) lies between 25 / 1024 and 4.2, so that the per-token decay rates exp(a_log) * steps_dt run from under 1 / 1024 to about 1.1.
All inputs are finite; a program needn't handle non-finite values.
Results may differ from the reference program's by a relative error of at most 0.00115.
Values may be sent and summed in bfloat16 or wider, within the bound.
No kernel may reach another device: no remote copies, remote signals or barrier semaphores. Data moves between devices by JAX's collectives and lax.ppermute only.
A program may use at most 320 MiB of HBM per device.

```python
import math
import jax
import jax.numpy as jnp
from jax import lax

HEADS = 80
HEAD_DIM = 64
STATE = 128
CONV = 4
BLOCK = 64
LOCAL = 128
INNER = 5120
CH = 5376
CHAIN = 1024
TOKENS = 4096
N_DP = 4


def draw_a_log(key, part):
    key_pick, key_slow, key_fast = jax.random.split(key, 3)
    slow_share = 0.5
    picked = jax.random.uniform(key_pick, (HEADS,), jnp.float32) < slow_share
    slow_rate = jax.random.uniform(key_slow, (HEADS,), jnp.float32, math.log(0.2 / CHAIN), math.log(2.0 / CHAIN))
    fast_rate = jax.random.uniform(key_fast, (HEADS,), jnp.float32, math.log(2.0 / CHAIN), math.log(1.0 / 30.0))
    return jnp.where(picked, slow_rate, fast_rate) - math.log(0.008)


def with_ends(array, key, least, high):
    index_at = [jax.random.randint(jax.random.fold_in(key, axis), (), 0, length) for axis, length in enumerate(array.shape)]
    longest = array.shape.index(max(array.shape))
    neighbour = index_at[:longest] + [(index_at[longest] + 1) % array.shape[longest]] + index_at[longest + 1:]
    return array.at[tuple(index_at)].set(least).at[tuple(neighbour)].set(high)


def steps_of(own_key, shape, shards, smallest, high):
    gain, own = 1.0, jax.random.fold_in(own_key, 6)
    for dim, shards_of in shards:
        draws = jnp.exp(jax.random.uniform(jax.random.fold_in(own, dim), (shards_of,), jnp.float32, smallest / len(shards), high / len(shards)))
        gain = gain * jnp.repeat(draws, shape[dim] // shards_of).reshape([-1 if axis == dim else 1 for axis in range(len(shape))])
    return gain


def gaussian(own_key, dims, scale, bound, cuts=(), held_as=jnp.bfloat16):
    factor_of = steps_of(own_key, dims, cuts, -0.22, 0.18) if cuts else 1.0
    entries = jax.random.normal(own_key, dims, jnp.float32) * scale * factor_of
    return jnp.minimum(jnp.maximum(entries, -bound), bound).astype(held_as)


def setup_inputs(seed: int = 0) -> dict:
    keys = jax.random.split(jax.random.key(seed), 10)
    return {
        "conv_input": gaussian(keys[0], (TOKENS, CH), 1.0, 6.0, ((0, 32),)),
        "doc_start": with_ends((jax.random.randint(keys[1], (TOKENS,), 0, 4 * LOCAL) < 1).astype(jnp.int32), jax.random.fold_in(keys[1], 1), 0, 1),
        "conv_weight": gaussian(keys[2], (CONV, CH), CONV ** -0.5, 3.0, (), jnp.float32),
        "conv_bias": jnp.clip(jax.random.uniform(keys[3], (CH,), jnp.float32, -0.5, 0.5), -0.5, 0.5),
        "dt_raw": gaussian(keys[4], (TOKENS, HEADS), 0.5, 3.0, ((0, 32),), jnp.float32),
        "dt_bias": jnp.clip(jax.random.uniform(keys[5], (HEADS,), jnp.float32, -5.5, -4.2), -5.5, -4.2),
        "a_log": draw_a_log(jax.random.fold_in(keys[9], 71), 0),
        "skip_gain": jnp.clip(jax.random.uniform(keys[7], (HEADS,), jnp.float32, 0.5, 1.5), 0.5, 1.5),
        "cotangent": gaussian(keys[8], (TOKENS, INNER), 1.0, 6.0, ((0, 32),)),
    }


exact_mode = lax.Precision.HIGHEST

def prepare_inputs(tail_rows, conv_input, doc_start, conv_weight, conv_bias, dt_raw, dt_bias, a_log):
    row_count = conv_input.shape[0]
    extended = jnp.concatenate([tail_rows, conv_input], axis=0)
    resets = doc_start.astype(jnp.float32)
    segment = jnp.cumsum(resets)
    padded = jnp.concatenate([jnp.zeros((CONV - 1,), jnp.float32), segment])
    convolved = conv_bias[None, :] + conv_weight[CONV - 1][None, :] * extended[CONV - 1:]
    for offset in range(1, CONV):
        first_row = CONV - 1 - offset
        tap_valid = (padded[first_row:first_row + row_count] == segment).astype(jnp.float32)
        convolved = convolved + conv_weight[first_row][None, :] * extended[first_row:first_row + row_count] * tap_valid[:, None]
    activated = jax.nn.silu(convolved)
    values_x = activated[:, :INNER].reshape(row_count, HEADS, HEAD_DIM)
    keys_b = activated[:, INNER:INNER + STATE]
    reads_c = activated[:, INNER + STATE:]
    steps_dt = jax.nn.softplus(dt_raw + dt_bias[None, :])
    log_decay = -jnp.exp(a_log)[None, :] * steps_dt
    return (values_x, keys_b, reads_c, steps_dt, log_decay)

def scan_block(carry, block_data):
    carry_state, skip_gain = carry
    values_x, keys_b, reads_c, steps_dt, log_decay, resets = block_data
    length = values_x.shape[0]
    segment = jnp.cumsum(resets)
    running = jnp.cumsum(log_decay, axis=0)
    positions = jnp.arange(length)
    causal = (positions[:, None] >= positions[None, :]) & (segment[:, None] == segment[None, :])
    spread_log = running.T[:, :, None] - running.T[:, None, :]
    within = jnp.where(causal[None], jnp.exp(jnp.where(causal[None], spread_log, 0.0)), 0.0)
    scores = jnp.dot(reads_c, keys_b.T, precision=exact_mode)
    weights = within * scores[None] * steps_dt.T[:, None, :]
    output = jnp.einsum('hts,shp->thp', weights, values_x, precision=exact_mode)
    untouched = (segment == 0).astype(running.dtype)
    entry_weight = jnp.exp(running) * untouched[:, None]
    output = output + jnp.einsum('tn,hpn->thp', reads_c, carry_state, precision=exact_mode) * entry_weight[:, :, None]
    output = output + skip_gain[None, :, None] * values_x
    last_segment = (segment == segment[length - 1]).astype(running.dtype)
    leave_weight = jnp.exp(running[length - 1][None, :] - running) * last_segment[:, None] * steps_dt
    through = jnp.exp(running[length - 1]) * untouched[length - 1]
    added = jnp.einsum('shp,sn->hpn', leave_weight[:, :, None] * values_x, keys_b, precision=exact_mode)
    carry_state = carry_state * through[:, None, None] + added
    return ((carry_state, skip_gain), output)

def chain_blocks(values_x, keys_b, reads_c, steps_dt, log_decay, resets, skip_gain, start_state):
    row_count = values_x.shape[0]
    block_count = row_count // BLOCK
    pieces = tuple((member.reshape((block_count, BLOCK) + member.shape[1:]) for member in (values_x, keys_b, reads_c, steps_dt, log_decay, resets)))
    stepper = jax.checkpoint(scan_block)
    (final_state, _), outputs = lax.scan(stepper, (start_state, skip_gain), pieces)
    return (outputs.reshape(row_count, INNER), final_state)

def reference(conv_input, doc_start, conv_weight, conv_bias, dt_raw, dt_bias, a_log, skip_gain, cotangent):
    zero_tail = jnp.zeros((CONV - 1, CH), jnp.float32)
    zero_state = jnp.zeros((HEADS, HEAD_DIM, STATE), jnp.float32)
    outputs = []
    grads_in = []
    totals = (jnp.zeros((CONV, CH), jnp.float32), jnp.zeros((CH,), jnp.float32), jnp.zeros((HEADS,), jnp.float32), jnp.zeros((HEADS,), jnp.float32), jnp.zeros((HEADS,), jnp.float32))
    for group in range(N_DP):
        first_row = group * CHAIN
        rows_in = conv_input[first_row:first_row + CHAIN].astype(jnp.float32)
        starts = doc_start[first_row:first_row + CHAIN]
        raw_steps = dt_raw[first_row:first_row + CHAIN]
        upstream = cotangent[first_row:first_row + CHAIN].astype(jnp.float32)

        def forward(rows_value, weight_value, bias_value, dtb_value, alog_value, gain_value):
            values_x, keys_b, reads_c, steps_dt, log_decay = prepare_inputs(zero_tail, rows_value, starts, weight_value, bias_value, raw_steps, dtb_value, alog_value)
            result, _ = chain_blocks(values_x, keys_b, reads_c, steps_dt, log_decay, starts.astype(jnp.float32), gain_value, zero_state)
            return result
        result, pull_back = jax.vjp(forward, rows_in, conv_weight, conv_bias, dt_bias, a_log, skip_gain)
        grads = pull_back(upstream)
        outputs.append(result.astype(jnp.bfloat16))
        grads_in.append(grads[0].astype(jnp.bfloat16))
        totals = tuple((before + extra for before, extra in zip(totals, grads[1:])))
    scale = float(TOKENS) ** (-0.5)
    return (jnp.concatenate(outputs, axis=0), jnp.concatenate(grads_in, axis=0), totals[0] * scale, totals[1] * scale, totals[2] * scale, totals[3] * scale, totals[4] * scale)
```

```python
import functools

import jax
import jax.numpy as jnp
from jax import lax
from jax.experimental import pallas as pl
from jax.experimental.pallas import tpu as pltpu
from jax.sharding import PartitionSpec as P

HEADS = 80
HEAD_DIM = 64
STATE = 128
CONV = 4
INNER = 5120
CH = 5376

PIECES = 4
PIECE_HEADS = HEADS // PIECES
WIDTH = PIECE_HEADS * HEAD_DIM
PAIR = 2 * HEAD_DIM
CHUNK = 256
BC = 2 * STATE
STREAMS = 2
FAR = -1e30

F32 = jnp.float32
BF16 = jnp.bfloat16
EXACT = lax.Precision.HIGHEST
VMEM_LIMIT = 48 * 1024 * 1024


def params():
    return pltpu.CompilerParams(vmem_limit_bytes=VMEM_LIMIT)


def iota(shape, dim):
    return lax.broadcasted_iota(jnp.int32, shape, dim)


def mm(a, b, contract=((1,), (0,))):
    return lax.dot_general(a, b, (contract, ((), ())), preferred_element_type=F32)


def halves(value):
    high = value.astype(BF16)
    return high, (value - high.astype(F32)).astype(BF16)


def lanes(*parts):
    return jnp.concatenate(parts, axis=1)


def rows(*parts):
    return jnp.concatenate(parts, axis=0)


def by_head(table, first, count):
    out = []
    for head in range(first, first + count, 2):
        shape = (table.shape[0], PAIR)
        left = jnp.broadcast_to(table[:, head : head + 1], shape)
        right = jnp.broadcast_to(table[:, head + 1 : head + 2], shape)
        out.append(jnp.where(iota(shape, 1) < HEAD_DIM, left, right))
    return lanes(*out)


def taps_of(ext_ref, cols, count, mask):
    taps = []
    for tap in range(CONV):
        back = CONV - 1 - tap
        value = ext_ref[8 - back : 8 - back + count, cols]
        taps.append(value if back == 0 else value * mask[back])
    return taps


def fill_ext(ext_ref, x_ref, halo_ref, count):
    ext_ref[8 : 8 + count, :] = x_ref[...].astype(F32)
    ext_ref[8 - CONV + 1 : 8, :] = halo_ref[...].astype(F32)


def columns(ref, count, width):
    table = ref[...]
    return [jnp.broadcast_to(table[:, i : i + 1], (count, width)) for i in range(CONV)]


def activate(taps, cols, w_ref, b_ref):
    v = b_ref[:, cols] + w_ref[CONV - 1 : CONV, cols] * taps[CONV - 1]
    for tap in range(CONV - 2, -1, -1):
        v = v + w_ref[tap : tap + 1, cols] * taps[tap]
    gate = 1.0 / (1.0 + jnp.exp(-v))
    return v * gate, gate * (1.0 + v * (1.0 - gate))


def prep_kernel(
    doc_ref, raw_ref, dtb_ref, alog_ref,
    mask_ref, smask_ref, far_ref, run_ref, entry_ref, leave_ref, dt_ref, row_ref,
):
    count = raw_ref.shape[0]
    resets = doc_ref[...].astype(F32)
    t, s = iota((count, count), 0), iota((count, count), 1)

    def total(keep, shape):
        return jnp.sum(jnp.where(keep, jnp.broadcast_to(resets, shape), 0.0), axis=1, keepdims=True)

    square = (count, count)
    lane = iota((count, 128), 1)
    table = jnp.ones((count, 128), F32)
    for back in range(1, CONV):
        fits = (total((s <= t) & (s > t - back), square) == 0.0).astype(F32)
        table = jnp.where(lane == back, fits, table)
    mask_ref[...] = table
    wide = (count + 8, count)
    at, s_wide = iota(wide, 0) - 8, iota(wide, 1)
    lane, place = iota((count + 8, 128), 1), iota((count + 8, 128), 0) - 8
    table = jnp.zeros((count + 8, 128), F32)
    for ahead in range(CONV):
        fits = (total((s_wide > at) & (s_wide <= at + ahead), wide) == 0.0).astype(F32)
        fits = jnp.where((place + ahead >= 0) & (place + ahead < count), fits, 0.0)
        table = jnp.where(lane == ahead, fits, table)
    smask_ref[...] = table
    segment = total(s <= t, square)
    reset_col = total(s == t, square)
    segment_row = jnp.sum(
        jnp.where(t <= s, jnp.broadcast_to(reset_col, square), 0.0), axis=0, keepdims=True
    )
    causal = (s <= t) & (segment == segment_row)
    far_ref[...] = jnp.where(causal, 0.0, FAR)
    v = raw_ref[...] + dtb_ref[...]
    dt = jnp.maximum(v, 0.0) + jnp.log1p(jnp.exp(-jnp.abs(v)))
    decay = -jnp.exp(alog_ref[...]) * dt
    run = jnp.dot((s <= t).astype(F32), decay, precision=EXACT, preferred_element_type=F32)
    end = run[count - 1 : count, :]
    run_ref[...] = run
    dt_ref[...] = dt
    entry_ref[...] = jnp.where(segment == 0.0, jnp.exp(run), 0.0)
    last = segment == segment[count - 1 : count, :]
    leave_ref[...] = jnp.where(last, jnp.exp(end - run) * dt, 0.0)
    row = lanes(jnp.log(dt) - run, jnp.zeros((count, 128 - HEADS), F32))
    row_ref[...] = row.T[:HEADS, :]


def bc_kernel(x_ref, halo_ref, w_ref, b_ref, mask_ref, act_ref, slope_ref, turned_ref, scores_ref, ext_ref):
    count = x_ref.shape[0]
    fill_ext(ext_ref, x_ref, halo_ref, count)
    cols = slice(0, BC)
    taps = taps_of(ext_ref, cols, count, columns(mask_ref, count, BC))
    act, slope = activate(taps, cols, w_ref, b_ref)
    act_ref[...] = act
    slope_ref[...] = slope
    keys, reads = act[:, :STATE], act[:, STATE:]
    turned_ref[:STATE, :] = keys.T
    turned_ref[STATE:, :] = reads.T
    scores_ref[...] = lax.dot_general(
        reads, keys, (((1,), (1,)), ((), ())), precision=EXACT, preferred_element_type=F32
    )


def local_kernel(
    piece, flag_ref, x_ref, halo_ref, w_ref, b_ref, cot_ref, mask_ref, entry_ref, leave_ref, turned_ref,
    act_ref, slope_ref, send_ref, mine_ref, ext_ref,
):
    count = x_ref.shape[0]
    fill_ext(ext_ref, x_ref, halo_ref, count)
    keys = halves(turned_ref[:STATE, :])
    reads = halves(turned_ref[STATE:, :])
    keys_both, reads_both = lanes(*keys), lanes(*reads)
    entry, leave = entry_ref[...], leave_ref[...]
    first_core = flag_ref[0] == 0
    mask = columns(mask_ref, count, CHUNK)
    for start in range(0, WIDTH, CHUNK):
        cols = slice(start, start + CHUNK)
        head = piece * PIECE_HEADS + start // HEAD_DIM
        act, slope = activate(taps_of(ext_ref, cols, count, mask), cols, w_ref, b_ref)
        act_ref[:, cols] = act
        slope_ref[:, cols] = slope
        e = by_head(entry, head, CHUNK // HEAD_DIM)
        lx_high, lx_low = halves(act * by_head(leave, head, CHUNK // HEAD_DIM))
        ey_high, ey_low = halves(cot_ref[:, cols].astype(F32) * e)
        state = mm(keys_both, rows(lx_high, lx_high)) + mm(keys[0], lx_low)
        adjoint = mm(reads_both, rows(ey_high, ey_high)) + mm(reads[0], ey_low)
        send_ref[:STATE, cols] = jnp.where(first_core, state, adjoint)
        mine_ref[:, cols] = jnp.where(first_core, adjoint, state)
        send_ref[STATE:, cols] = jnp.broadcast_to(e[count - 1 : count, :], (8, CHUNK))


def within_kernel(
    piece, act_ref, cot_ref, run_ref, row_ref, far_ref, scores_ref, y_ref, dx_ref, dscores_ref
):
    count = act_ref.shape[0]
    run = run_ref[...]
    far, scores = far_ref[...], scores_ref[...]
    left = iota((count, PAIR), 1) < HEAD_DIM
    total = jnp.zeros((count, count), F32)
    zero = jnp.zeros((count, PAIR), BF16)
    for pair in range(PIECE_HEADS // 2):
        cols = slice(pair * PAIR, (pair + 1) * PAIR)
        x_high, x_low = halves(act_ref[:, cols])
        upstream = cot_ref[:, cols]
        upstream_turned = upstream.astype(F32).T.astype(BF16)
        spread, weights = [], []
        for side in range(2):
            head = piece * PIECE_HEADS + 2 * pair + side
            within = jnp.exp(run[:, head : head + 1] + row_ref[head : head + 1, :] + far)
            spread.append(within)
            weights.append(lanes(*halves(within * scores)))
        out = mm(rows(*weights), rows(lanes(x_high, x_low), lanes(x_high, zero)))
        out = out[:, :PAIR] + out[:, PAIR:]
        y_ref[:, cols] = jnp.where(left, out[:count], out[count:])
        parts = []
        for side in range(2):
            mine = upstream_turned[side * HEAD_DIM : (side + 1) * HEAD_DIM, :]
            pushed = rows(weights[side][:, :count], weights[side][:, count:])
            parts.append(mm(lanes(mine, mine), pushed))
        dx_ref[:, cols] = rows(*parts).T
        up_left, up_right = jnp.where(left, upstream, zero), jnp.where(left, zero, upstream)
        lhs = rows(lanes(up_left, up_left), lanes(up_right, up_right))
        products = mm(lhs, lanes(x_high, x_low), ((1,), (1,)))
        total = total + spread[0] * products[:count] + spread[1] * products[count:]
    dscores_ref[...] = total


def conv_back(dconv, taps, cols, w_ref, z_ref, smask, misc_ref, gin_ref, count):
    z_ref[8 : 8 + count, cols] = dconv
    grad = jnp.zeros((count + 8, dconv.shape[1]), F32)
    for ahead in range(CONV):
        tap = CONV - 1 - ahead
        shifted = z_ref[ahead : ahead + count + 8, cols]
        grad = grad + w_ref[tap : tap + 1, cols] * (shifted * smask[ahead])
    misc_ref[0:8, cols] = grad[:8]
    misc_ref[8:16, cols] = grad[count:]
    gin_ref[:, cols] = grad[8:].astype(BF16)
    sums = [jnp.sum(dconv * tap, axis=0, keepdims=True) for tap in taps]
    sums.append(jnp.sum(dconv, axis=0, keepdims=True))
    sums.append(jnp.zeros((3, dconv.shape[1]), F32))
    misc_ref[16:24, cols] = rows(*sums)


def clear_edges(z_ref, count):
    z_ref[0:8, :] = jnp.zeros((8, z_ref.shape[1]), F32)
    z_ref[8 + count : 16 + count, :] = jnp.zeros((8, z_ref.shape[1]), F32)


def finish_kernel(
    piece, flag_ref, inc_ref, met_ref, exch_ref, act_ref, slope_ref, y_ref, dx_ref, cot_ref,
    x_ref, halo_ref, w_ref, mask_ref, smask_ref, entry_ref, leave_ref, dt_ref, raw_ref, dtb_ref,
    alog_ref, skip_ref, bc_ref, *refs,
):
    out_ref, gin_ref, misc_ref, dreads_ref, dkeys_ref, scal_ref, ext_ref, z_ref = refs[-8:]
    count = x_ref.shape[0]
    fill_ext(ext_ref, x_ref, halo_ref, count)
    clear_edges(z_ref, count)
    keys = halves(bc_ref[:, :STATE])
    reads = halves(bc_ref[:, STATE:])
    keys_both, reads_both = lanes(*keys), lanes(*reads)
    entry, leave, skip = entry_ref[...], leave_ref[...], skip_ref[...]
    first_core = flag_ref[0] == 0
    mask = columns(mask_ref, count, CHUNK)
    smask = columns(smask_ref, count + 8, CHUNK)
    dreads = jnp.zeros((count, STATE), F32)
    dkeys = jnp.zeros((count, STATE), F32)
    sums = jnp.zeros((4 * count + 16, HEADS), F32)
    per = CHUNK // HEAD_DIM
    for start in range(0, WIDTH, CHUNK):
        cols = slice(start, start + CHUNK)
        head = piece * PIECE_HEADS + start // HEAD_DIM
        inc, exch = inc_ref[:, cols], exch_ref[:, cols]
        mine = met_ref[STATE : STATE + 1, cols] * inc + met_ref[:STATE, cols]
        state = jnp.where(first_core, exch, mine)
        adjoint = jnp.where(first_core, mine, exch)
        s_high, s_low = halves(state)
        a_high, a_low = halves(adjoint)
        e, leaving = by_head(entry, head, per), by_head(leave, head, per)
        act, up = act_ref[:, cols], cot_ref[:, cols].astype(F32)
        carried = mm(reads_both, rows(s_high, s_high)) + mm(reads[0], s_low)
        y = y_ref[:, cols] + e * carried
        back = mm(keys_both, rows(a_high, a_high)) + mm(keys[0], a_low)
        back = leaving * back
        dx = dx_ref[:, cols] + back
        gain = by_head(skip, head, per)
        out_ref[:, cols] = (y + gain * act).astype(BF16)
        ey_high, ey_low = halves(up * e)
        lx_high, lx_low = halves(act * leaving)
        across = ((1,), (1,))
        dreads = dreads + mm(lanes(ey_high, ey_high, ey_low), lanes(s_high, s_low, s_high), across)
        dkeys = dkeys + mm(lanes(lx_high, lx_high, lx_low), lanes(a_high, a_low, a_high), across)
        through = e[count - 1 : count, :]
        end = jnp.sum(act * back, axis=0, keepdims=True)
        end = end + through * jnp.sum(state * adjoint, axis=0, keepdims=True)
        direct = jnp.sum(up * act, axis=0, keepdims=True)
        received = act * dx
        small = halves(rows(end, direct, jnp.zeros((6, CHUNK), F32)))
        stack = halves(up * y - received) + halves(received)
        pick = (iota((CHUNK, HEADS), 1) == head + iota((CHUNK, HEADS), 0) // HEAD_DIM).astype(BF16)
        sums = sums + mm(rows(*stack, rows(*small)), pick)
        dconv = (dx + gain * up) * slope_ref[:, cols]
        taps = taps_of(ext_ref, cols, count, mask)
        conv_back(dconv, taps, cols, w_ref, z_ref, smask, misc_ref, gin_ref, count)
    dreads_ref[...] = dreads
    dkeys_ref[...] = dkeys
    drun = sums[:count] + sums[count : 2 * count]
    received = sums[2 * count : 3 * count] + sums[3 * count : 4 * count]
    small = sums[4 * count : 4 * count + 8] + sums[4 * count + 8 :]
    drun = drun + jnp.where(iota((count, HEADS), 0) == count - 1, small[0:1, :], 0.0)
    later = (iota((count, count), 1) >= iota((count, count), 0)).astype(F32)
    ddecay = jnp.dot(later, drun, precision=EXACT, preferred_element_type=F32)
    rate = -jnp.exp(alog_ref[...])
    dt = dt_ref[...]
    ddt = received / dt + ddecay * rate
    v = raw_ref[...] + dtb_ref[...]
    ddtb = jnp.sum(ddt / (1.0 + jnp.exp(-v)), axis=0, keepdims=True)
    dalog = jnp.sum(ddecay * (rate * dt), axis=0, keepdims=True)
    scal = rows(ddtb, dalog, small[1:2, :], jnp.zeros((5, HEADS), F32))
    scal_ref[...] = lanes(scal, jnp.zeros((8, 128 - HEADS), F32))


def final_kernel(x_ref, halo_ref, w_ref, mask_ref, smask_ref, bc_ref, slope_ref, *refs):
    gin_ref, misc_ref, ext_ref, z_ref = refs[-4:]
    parts = refs[: 4 * PIECES]
    count = x_ref.shape[0]
    fill_ext(ext_ref, x_ref, halo_ref, count)
    clear_edges(z_ref, count)
    total = []
    for kind in range(4):
        value = parts[kind * PIECES][...]
        for piece in range(1, PIECES):
            value = value + parts[kind * PIECES + piece][...]
        total.append(value)
    dreads, dkeys, dscores, scal = total
    keys, reads = bc_ref[:, :STATE], bc_ref[:, STATE:]
    dreads = dreads + jnp.dot(dscores, keys, precision=EXACT, preferred_element_type=F32)
    dkeys = dkeys + jnp.dot(dscores.T, reads, precision=EXACT, preferred_element_type=F32)
    cols = slice(0, BC)
    dconv = lanes(dkeys, dreads) * slope_ref[...]
    taps = taps_of(ext_ref, cols, count, columns(mask_ref, count, BC))
    smask = columns(smask_ref, count + 8, BC)
    conv_back(dconv, taps, cols, w_ref, z_ref, smask, misc_ref, gin_ref, count)
    misc_ref[16 + CONV + 1 : 24, :128] = scal[:3, :]


def whole(shape):
    return pl.BlockSpec(shape, lambda i: (0,) * len(shape))


def part(shape, index):
    return pl.BlockSpec(shape, lambda i: (0, index))


def call(kernel, ins, specs, outs, out_specs, scratch=(), aliases=None):
    return pl.pallas_call(
        kernel,
        grid=(1,),
        in_specs=specs,
        out_specs=out_specs,
        out_shape=[jax.ShapeDtypeStruct(shape, dtype) for shape, dtype in outs],
        scratch_shapes=list(scratch),
        input_output_aliases=aliases or {},
        compiler_params=params(),
    )(*ins)


def full_specs(arrays):
    return [whole(a.shape) for a in arrays]


def permute(value, axis, target):
    size = lax.axis_size(axis)
    return lax.ppermute(value, axis, [(i, target(i)) for i in range(size)])


def along(size):
    def target(i):
        if i % 2 == 1:
            return i + 2 if i + 2 < size else i - 1
        return i - 2 if i >= 2 else i + 1

    return target


def xor_sum(value, axis, low):
    size = lax.axis_size(axis)
    bit = low
    while bit < size:
        if 2 * bit < size:
            one = permute(value, axis, lambda i: i ^ bit)
            two = permute(value, axis, lambda i: i ^ (2 * bit))
            three = permute(value, axis, lambda i: i ^ (3 * bit))
            value = (value + one) + (two + three)
            bit *= 4
        else:
            value = value + permute(value, axis, lambda i: i ^ bit)
            bit *= 2
    return value


def chain(pieces, own_through, size, place):
    hops = size // 2 - 1
    count = len(pieces)
    received = []
    previous = None
    for turn in range(count + hops - 1):
        value = None
        for j in reversed(range(count)):
            mine = pieces[j]
            if previous is not None:
                mine = mine + own_through[j] * previous
            value = mine if value is None else jnp.where(turn - place <= j, mine, value)
        got = permute(value, "seq", along(size))
        received.append(got)
        previous = jnp.where(place == 0, 0.0, got)
    entering = []
    for j in range(count):
        value = jnp.zeros_like(pieces[j])
        for at in range(1, hops + 1):
            value = jnp.where(place == at, received[j + at - 1], value)
        entering.append(value)
    return entering


def on_device(
    conv_input, doc_start, conv_weight, conv_bias, dt_raw, dt_bias, a_log, skip_gain, cotangent
):
    count = conv_input.shape[0]
    size = lax.axis_size("seq")
    index = lax.axis_index("seq")
    core = lax.rem(index, 2)
    chip = lax.div(index, 2)
    chips = size // 2
    place = jnp.where(core == 1, chip, chips - 1 - chip)
    flag = core.reshape((1,)).astype(jnp.int32)

    resets = doc_start[count - CONV + 2 :].astype(BF16)
    keep = [jnp.ones((1,), BF16)]
    for i in reversed(range(CONV - 2)):
        keep.insert(0, keep[0] * (1.0 - resets[i : i + 1]))
    keep_rows = jnp.concatenate(keep)[:, None]
    tail_out = conv_input[count - CONV + 1 :] * keep_rows
    halo = lax.ppermute(tail_out, "seq", [(i, i + 1) for i in range(size - 1)])

    bias = conv_bias[None, :]
    dtb, alog, skip = dt_bias[None, :], a_log[None, :], skip_gain[None, :]
    per_head = (count, HEADS)
    square = (count, count)
    prep_in = (doc_start[None, :], dt_raw, dtb, alog)
    prep_out = [
        ((count, 128), F32), ((count + 8, 128), F32), (square, F32), (per_head, F32),
        (per_head, F32), (per_head, F32), (per_head, F32), ((HEADS, count), F32),
    ]
    mask, smask, far, run, entry, leave, dt, row = call(
        prep_kernel, prep_in, full_specs(prep_in), prep_out, [whole(s) for s, _ in prep_out]
    )

    bc_at = INNER // BC
    bc_common = [part((count, BC), bc_at), part((CONV - 1, BC), bc_at), part((CONV, BC), bc_at)]
    bc_out = [((count, BC), F32), ((count, BC), F32), ((BC, count), F32), (square, F32)]
    bc_act, bc_slope, turned, scores = call(
        bc_kernel,
        (conv_input, halo, conv_weight, bias, mask),
        bc_common + [part((1, BC), bc_at), whole(mask.shape)],
        bc_out,
        [whole(s) for s, _ in bc_out],
        [pltpu.VMEM((count + 8, BC), F32)],
    )

    smem = pl.BlockSpec(memory_space=pltpu.SMEM)
    block = (count, WIDTH)
    ext = pltpu.VMEM((count + 8, WIDTH), F32)
    acts, slopes, sends, mines = [], [], [], []
    for j in range(PIECES):
        small = (mask, entry, leave, turned)
        specs = [smem, part(block, j), part((CONV - 1, WIDTH), j), part((CONV, WIDTH), j)]
        specs += [part((1, WIDTH), j), part(block, j)] + full_specs(small)
        outs = [(block, F32), (block, F32), ((STATE + 8, WIDTH), F32), ((STATE, WIDTH), F32)]
        act, slope, send, mine = call(
            functools.partial(local_kernel, j),
            (flag, conv_input, halo, conv_weight, bias, cotangent) + small,
            specs,
            outs,
            [whole(s) for s, _ in outs],
            [ext],
        )
        acts.append(act)
        slopes.append(slope)
        sends.append(send)
        mines.append(mine)

    met, chip_state, chip_through = [], [], []
    for j in range(PIECES):
        other = permute(sends[j], "seq", lambda i: i ^ 1)
        own = sends[j][STATE : STATE + 1]
        met.append(other)
        chip_state.append(own * other[:STATE] + mines[j])
        chip_through.append(own * other[STATE : STATE + 1])

    ys, dxs, dscores = [], [], []
    for j in range(PIECES):
        small = (run, row, far, scores)
        outs = [(block, F32), (block, F32), (square, F32)]
        y, dx, dscore = call(
            functools.partial(within_kernel, j),
            (acts[j], cotangent) + small,
            [whole(block), part(block, j)] + full_specs(small),
            outs,
            [whole(s) for s, _ in outs],
        )
        ys.append(y)
        dxs.append(dx)
        dscores.append(dscore)

    entering = [None] * PIECES
    for stream in range(STREAMS):
        members = list(range(stream, PIECES, STREAMS))
        values = chain(
            [chip_state[j] for j in members], [chip_through[j] for j in members], size, place
        )
        for j, value in zip(members, values):
            entering[j] = value

    order = [j for stream in range(PIECES // STREAMS) for j in range(stream * STREAMS, stream * STREAMS + STREAMS)]
    shared = None
    dreads, dkeys, scals = [None] * PIECES, [None] * PIECES, [None] * PIECES
    shared_out = [((count, INNER), BF16), ((count, CH), BF16), ((24, CH), F32)]
    for j in order:
        exch = permute(entering[j], "seq", lambda i: i ^ 1)
        state = (STATE, WIDTH)
        small = (mask, smask, entry, leave, dt, dt_raw, dtb, alog, skip, bc_act)
        ins = (flag, entering[j], met[j], exch, acts[j], slopes[j], ys[j], dxs[j], cotangent)
        ins += (conv_input, halo, conv_weight) + small
        specs = [smem, whole(state), whole((STATE + 8, WIDTH)), whole(state)]
        specs += [whole(block)] * 4 + [part(block, j)] * 2
        specs += [part((CONV - 1, WIDTH), j), part((CONV, WIDTH), j)] + full_specs(small)
        aliases = None
        if shared is not None:
            aliases = {len(ins) + i: i for i in range(3)}
            ins += tuple(shared)
            specs += [pl.BlockSpec(memory_space=pl.ANY)] * 3
        outs = shared_out + [((count, STATE), F32), ((count, STATE), F32), ((8, 128), F32)]
        *shared, dreads[j], dkeys[j], scals[j] = call(
            functools.partial(finish_kernel, j),
            ins,
            specs,
            outs,
            [part(block, j), part(block, j), part((24, WIDTH), j)] + [whole(s) for s, _ in outs[3:]],
            [ext, pltpu.VMEM((count + 16, WIDTH), F32)],
            aliases,
        )
    output, gin, misc = shared

    small = (mask, smask, bc_act, bc_slope, *dreads, *dkeys, *dscores, *scals)
    ins = (conv_input, halo, conv_weight) + small + (gin, misc)
    gin, misc = call(
        final_kernel,
        ins,
        bc_common + full_specs(small) + [pl.BlockSpec(memory_space=pl.ANY)] * 2,
        shared_out[1:],
        [part((count, BC), bc_at), part((24, BC), bc_at)],
        [pltpu.VMEM((count + 8, BC), F32), pltpu.VMEM((count + 16, BC), F32)],
        {len(ins) - 2: 0, len(ins) - 1: 1},
    )

    returned = lax.ppermute(
        misc[8 - CONV + 1 : 8], "seq", [(i, i - 1) for i in range(1, size)]
    )
    last = misc[16 - CONV + 1 : 16] + returned * keep_rows.astype(F32)
    grad_input = lax.dynamic_update_slice(gin, last.astype(BF16), (count - CONV + 1, 0))

    half = CH // 2
    lower, upper = misc[16:24, :half], misc[16:24, half:]
    first = core == 0
    value = jnp.where(first, lower, upper)
    value = value + permute(jnp.where(first, upper, lower), "seq", lambda i: i ^ 1)
    value = xor_sum(value, "dp", 1)
    value = xor_sum(value, "seq", 2)
    value = value * float(lax.axis_size("dp") * size * count) ** (-0.5)
    other = permute(value, "seq", lambda i: i ^ 1)
    lower = jnp.where(first, value, other)
    upper = jnp.where(first, other, value)
    summed = jnp.concatenate([lower, upper], axis=1)
    scal = summed[CONV + 1 :, INNER : INNER + HEADS]
    return (output, grad_input, summed[:CONV], summed[CONV], scal[0], scal[1], scal[2])


def solution(mesh):
    return jax.shard_map(
        on_device,
        mesh=mesh,
        in_specs=(
            P(("dp", "seq"), None),
            P(("dp", "seq")),
            P(),
            P(),
            P(("dp", "seq"), None),
            P(),
            P(),
            P(),
            P(("dp", "seq"), None),
        ),
        out_specs=(P(("dp", "seq"), None), P(("dp", "seq"), None), P(), P(), P(), P(), P()),
        check_vma=False,
    )
```

```python
import functools

import jax
import jax.numpy as jnp
from jax import lax
from jax.experimental import pallas as pl
from jax.experimental.pallas import tpu as pltpu
from jax.sharding import PartitionSpec as P

HEADS = 80
HEAD_DIM = 64
STATE = 128
CONV = 4
INNER = 5120
CH = 5376

STREAMS = 2
TURNS = 2
PIECES = STREAMS * TURNS
PIECE_HEADS = HEADS // PIECES
WIDTH = PIECE_HEADS * HEAD_DIM
SPAN = TURNS * WIDTH
PAIR = 2 * HEAD_DIM
CHUNK = 256
BC = 2 * STATE
BC_AT = INNER // BC
FAR = -1e30
CODE = 32766.0
PER = CHUNK // HEAD_DIM

F32 = jnp.float32
BF16 = jnp.bfloat16
I16 = jnp.int16
EXACT = lax.Precision.HIGHEST
ACROSS = ((1,), (1,))
ANY = pl.BlockSpec(memory_space=pl.ANY)
SMEM = pl.BlockSpec(memory_space=pltpu.SMEM)
VMEM_LIMIT = 64 * 1024 * 1024

MASK, ENTRY, LEAVE, PULL, RATE, DECAY, RUN, FAR_AT, ROW, SMASK = range(0, 1280, 128)
SKIP = ROW + HEADS
TABLE = SMASK + 136


def iota(shape, dim):
    return lax.broadcasted_iota(jnp.int32, shape, dim)


def mm(a, b, contract=((1,), (0,))):
    return lax.dot_general(a, b, (contract, ((), ())), preferred_element_type=F32)


def halves(value):
    high = value.astype(BF16)
    return high, (value - high.astype(F32)).astype(BF16)


def lanes(*parts):
    return jnp.concatenate(parts, axis=1)


def rows(*parts):
    return jnp.concatenate(parts, axis=0)


def by_head(table, first, count):
    out = []
    for head in range(first, first + count, 2):
        shape = (table.shape[0], PAIR)
        left = jnp.broadcast_to(table[:, head : head + 1], shape)
        right = jnp.broadcast_to(table[:, head + 1 : head + 2], shape)
        out.append(jnp.where(iota(shape, 1) < HEAD_DIM, left, right))
    return lanes(*out)


def taps_of(ext_ref, cols, count, mask):
    taps = []
    for tap in range(CONV):
        back = CONV - 1 - tap
        value = ext_ref[8 - back : 8 - back + count, cols]
        taps.append(value if back == 0 else value * mask[back])
    return taps


def columns(table, width):
    shape = (table.shape[0], width)
    return [jnp.broadcast_to(table[:, i : i + 1], shape) for i in range(CONV)]


def activate(taps, cols, w_ref, b_ref):
    v = b_ref[:, cols] + w_ref[CONV - 1 : CONV, cols] * taps[CONV - 1]
    for tap in range(CONV - 2, -1, -1):
        v = v + w_ref[tap : tap + 1, cols] * taps[tap]
    gate = 1.0 / (1.0 + jnp.exp(-v))
    return v * gate, gate * (1.0 + v * (1.0 - gate))


class Flow:
    def __init__(self, sems):
        self.sems = sems
        self.used = 0

    def copy(self, source, target):
        made = pltpu.make_async_copy(source, target, self.sems.at[self.used])
        self.used += 1
        return made


def at(first, width=CHUNK):
    return slice(first, first + width)


def tail_kernel(x_ref, doc_ref, out_ref):
    count = doc_ref.shape[1]
    edge = x_ref.shape[0] - CONV + 1
    cut = jnp.zeros((1, 1), F32)
    for back in range(CONV - 1):
        row = edge + CONV - 2 - back
        if back:
            cut = cut + doc_ref[:, count - back : count - back + 1].astype(F32)
        keep = (cut == 0.0).astype(F32)
        value = x_ref[row : row + 1, :].astype(F32) * keep
        out_ref[CONV - 2 - back : CONV - 1 - back, :] = value.astype(BF16)


def edge_kernel(gin_ref, misc_ref, back_ref, doc_ref, out_ref):
    count = doc_ref.shape[1]
    size = gin_ref.shape[0]
    cut = jnp.zeros((1, 1), F32)
    keeps = []
    for back in range(CONV - 1):
        if back:
            cut = cut + doc_ref[:, count - back : count - back + 1].astype(F32)
        keeps.insert(0, (cut == 0.0).astype(F32))
    place = iota((8, 1), 0)
    value = misc_ref[...]
    for i in range(CONV - 1):
        row = 8 - CONV + 1 + i
        value = value + jnp.where(place == row, back_ref[i : i + 1, :] * keeps[i], 0.0)
    out_ref[...] = gin_ref[...]
    out_ref[size - 8 :, :] = value.astype(BF16)


def prep_kernel(doc_ref, raw_ref, dtb_ref, alog_ref, skip_ref, tab_ref):
    count = raw_ref.shape[0]
    resets = doc_ref[...].astype(F32)
    t, s = iota((count, count), 0), iota((count, count), 1)

    def total(keep, shape):
        return jnp.sum(jnp.where(keep, jnp.broadcast_to(resets, shape), 0.0), axis=1, keepdims=True)

    square = (count, count)
    lane = iota((count, 128), 1)
    table = jnp.ones((count, 128), F32)
    for back in range(1, CONV):
        fits = (total((s <= t) & (s > t - back), square) == 0.0).astype(F32)
        table = jnp.where(lane == back, fits, table)
    tab_ref[MASK : MASK + count, :] = table
    wide = (count + 8, count)
    at, s_wide = iota(wide, 0) - 8, iota(wide, 1)
    lane, place = iota((count + 8, 128), 1), iota((count + 8, 128), 0) - 8
    table = jnp.zeros((count + 8, 128), F32)
    for ahead in range(CONV):
        fits = (total((s_wide > at) & (s_wide <= at + ahead), wide) == 0.0).astype(F32)
        fits = jnp.where((place + ahead >= 0) & (place + ahead < count), fits, 0.0)
        table = jnp.where(lane == ahead, fits, table)
    tab_ref[SMASK : SMASK + count + 8, :] = table
    segment = total(s <= t, square)
    reset_col = total(s == t, square)
    segment_row = jnp.sum(
        jnp.where(t <= s, jnp.broadcast_to(reset_col, square), 0.0), axis=0, keepdims=True
    )
    causal = (s <= t) & (segment == segment_row)
    tab_ref[FAR_AT : FAR_AT + count, :] = jnp.where(causal, 0.0, FAR)
    v = raw_ref[...] + dtb_ref[...]
    dt = jnp.maximum(v, 0.0) + jnp.log1p(jnp.exp(-jnp.abs(v)))
    rate = -jnp.exp(alog_ref[...])
    decay = rate * dt
    run = jnp.dot((s <= t).astype(F32), decay, precision=EXACT, preferred_element_type=F32)
    end = run[count - 1 : count, :]
    last = segment == segment[count - 1 : count, :]
    gate = 1.0 / (1.0 + jnp.exp(-v))
    fill = jnp.zeros((count, 128 - HEADS), F32)

    def put(where, value):
        tab_ref[where : where + count, :] = lanes(value, fill)

    put(ENTRY, jnp.where(segment == 0.0, jnp.exp(run), 0.0))
    put(LEAVE, jnp.where(last, jnp.exp(end - run) * dt, 0.0))
    put(PULL, gate / dt)
    put(RATE, rate * gate)
    put(DECAY, decay)
    put(RUN, run)
    tab_ref[ROW : ROW + 128, :] = lanes(jnp.log(dt) - run, fill).T
    tab_ref[SKIP : SKIP + 1, :] = lanes(skip_ref[...], fill[:1])


def scores_of(act):
    keys, reads = act[:, :STATE], act[:, STATE:]
    return lax.dot_general(
        reads, keys, (ACROSS, ((), ())), precision=EXACT, preferred_element_type=F32
    )


def local_kernel(stream, flag_ref, x_ref, halo_ref, w_ref, b_ref, cot_ref, tab_ref, *refs):
    lead = stream == 0
    if lead:
        act_ref, slope_ref, send_ref, mine_ref, bca_ref, bcs_ref, turned_ref, scores_ref = refs[:8]
    else:
        turned_ref, act_ref, slope_ref, send_ref, mine_ref = refs[:5]
    xb, cb, ab, sb, nb, mb, ext_ref, bx, in_sems, out_sems = refs[-10:]
    count = xb.shape[0]
    base = stream * SPAN
    come, go = Flow(in_sems), Flow(out_sems)
    if lead:
        first = come.copy(x_ref.at[:, at(INNER, BC)], bx)
        first.start()
    arriving = []
    for start in range(0, SPAN, CHUNK):
        pair = (
            come.copy(x_ref.at[:, at(base + start)], xb.at[:, at(start)]),
            come.copy(cot_ref.at[:, at(base + start)], cb.at[:, at(start)]),
        )
        for copy in pair:
            copy.start()
        arriving.append(pair)
    tab = tab_ref
    mask = columns(tab[MASK : MASK + count, :], CHUNK)

    def load(cols, source, whole_cols):
        ext_ref[8 : 8 + count, cols] = source.astype(F32)
        ext_ref[8 - CONV + 1 : 8, cols] = halo_ref[:, whole_cols].astype(F32)
        return taps_of(ext_ref, cols, count, mask)

    def weights(whole_cols):
        return w_ref[:, whole_cols], b_ref[:, whole_cols]

    if lead:
        first.wait()
        cols = at(0, BC)
        act, slope = activate(load(cols, bx[...], at(INNER, BC)), cols, *weights(at(INNER, BC)))
        bca_ref[...] = act
        bcs_ref[...] = slope
        turned = rows(act[:, :STATE].T, act[:, STATE:].T)
        turned_ref[...] = turned
        scores_ref[...] = scores_of(act)
    else:
        turned = turned_ref[...]
    keys, reads = halves(turned[:STATE, :]), halves(turned[STATE:, :])
    keys_both, reads_both = lanes(*keys), lanes(*reads)
    entry, leave = tab[ENTRY : ENTRY + count, :], tab[LEAVE : LEAVE + count, :]
    first_core = flag_ref[0] == 0
    leaving = []
    for start, pair in zip(range(0, SPAN, CHUNK), arriving):
        cols = at(start)
        head = (base + start) // HEAD_DIM
        for copy in pair:
            copy.wait()
        taps = load(cols, xb[:, cols], at(base + start))
        act, slope = activate(taps, at(0), *weights(at(base + start)))
        ab[:, cols] = act
        sb[:, cols] = slope
        e = by_head(entry, head, PER)
        lx_high, lx_low = halves(act * by_head(leave, head, PER))
        ey_high, ey_low = halves(cb[:, cols].astype(F32) * e)
        state = mm(keys_both, rows(lx_high, lx_high)) + mm(keys[0], lx_low)
        adjoint = mm(reads_both, rows(ey_high, ey_high)) + mm(reads[0], ey_low)
        nb[:STATE, cols] = jnp.where(first_core, state, adjoint)
        mb[:, cols] = jnp.where(first_core, adjoint, state)
        nb[STATE:, cols] = jnp.broadcast_to(e[count - 1 : count, :], (8, CHUNK))
        for source, target in ((nb, send_ref), (mb, mine_ref), (ab, act_ref), (sb, slope_ref)):
            copy = go.copy(source.at[:, cols], target.at[:, cols])
            copy.start()
            leaving.append(copy)
    for copy in leaving:
        copy.wait()


def decode(codes):
    scale = jnp.exp2(codes[STATE : STATE + 1, :].astype(F32) * (1.0 / 256.0)) * (1.0 / CODE)
    return codes[:STATE, :].astype(F32) * scale


def encode(value):
    most = jnp.max(jnp.abs(value), axis=0, keepdims=True)
    power = jnp.ceil(jnp.log2(jnp.maximum(most, 1e-30)) * 256.0)
    scale = jnp.exp2(power * (1.0 / 256.0)) * (1.0 / CODE)
    codes = jnp.floor(value * (1.0 / scale) + 0.5).astype(jnp.int32)
    tail = jnp.broadcast_to(power.astype(jnp.int32), (16, value.shape[1]))
    return rows(codes, tail).astype(I16)


def hop_kernel(has_previous, pick_ref, mine_ref, met_ref, own_ref, *refs):
    out_ref, mb, eb, ob, pb, qb, sems, out_sems = refs[-8:]
    come, go = Flow(sems), Flow(out_sems)
    base = pl.multiple_of(pick_ref[0] * WIDTH, 128)
    arriving = []
    for start in range(0, WIDTH, CHUNK):
        cols, wide = at(start), pl.ds(base + start, CHUNK)
        group = [
            come.copy(mine_ref.at[:, wide], mb.at[:, cols]),
            come.copy(met_ref.at[:, wide], eb.at[:, cols]),
            come.copy(own_ref.at[pl.ds(STATE, 8), wide], ob.at[:, cols]),
        ]
        if has_previous:
            group.append(come.copy(refs[0].at[:, cols], pb.at[:, cols]))
        for copy in group:
            copy.start()
        arriving.append(group)
    leaving = []
    for start, group in zip(range(0, WIDTH, CHUNK), arriving):
        cols = at(start)
        for copy in group:
            copy.wait()
        value = eb[:STATE, cols]
        if has_previous:
            before = jnp.where(pick_ref[1] == 0, 0.0, decode(pb[:, cols]))
            value = value + eb[STATE : STATE + 1, cols] * before
        value = mb[:, cols] + ob[0:1, cols] * value
        qb[:, cols] = encode(value)
        copy = go.copy(qb.at[:, cols], out_ref.at[:, cols])
        copy.start()
        leaving.append(copy)
    for copy in leaving:
        copy.wait()


def within_kernel(piece, act_ref, cot_ref, tab_ref, scores_ref, y_ref, dx_ref, dscores_ref, *refs):
    ab, cb, yb, db, in_sems, out_sems = refs
    count = ab.shape[0]
    come, go = Flow(in_sems), Flow(out_sems)
    base = (piece % TURNS) * WIDTH
    arriving, leaving = [], []
    for start in range(0, WIDTH, CHUNK):
        pair = (
            come.copy(act_ref.at[:, at(base + start)], ab.at[:, at(start)]),
            come.copy(cot_ref.at[:, at(piece * WIDTH + start)], cb.at[:, at(start)]),
        )
        for copy in pair:
            copy.start()
        arriving.append(pair)
    run = tab_ref[RUN : RUN + count, :]
    far, scores = tab_ref[FAR_AT : FAR_AT + count, :], scores_ref[...]
    left = iota((count, PAIR), 1) < HEAD_DIM
    total = jnp.zeros((count, count), F32)
    zero = jnp.zeros((count, PAIR), BF16)
    for pair in range(PIECE_HEADS // 2):
        if pair * PAIR % CHUNK == 0:
            for copy in arriving[pair * PAIR // CHUNK]:
                copy.wait()
        cols = at(pair * PAIR, PAIR)
        x_high, x_low = halves(ab[:, cols])
        upstream = cb[:, cols]
        upstream_turned = upstream.astype(F32).T.astype(BF16)
        spread, weights = [], []
        for side in range(2):
            head = piece * PIECE_HEADS + 2 * pair + side
            row = tab_ref[ROW + head : ROW + head + 1, :]
            within = jnp.exp(run[:, head : head + 1] + row + far)
            spread.append(within)
            weights.append(lanes(*halves(within * scores)))
        out = mm(rows(*weights), rows(lanes(x_high, x_low), lanes(x_high, zero)))
        out = out[:, :PAIR] + out[:, PAIR:]
        yb[:, cols] = jnp.where(left, out[:count], out[count:])
        parts = []
        for side in range(2):
            mine = upstream_turned[side * HEAD_DIM : (side + 1) * HEAD_DIM, :]
            pushed = rows(weights[side][:, :count], weights[side][:, count:])
            parts.append(mm(lanes(mine, mine), pushed))
        db[:, cols] = rows(*parts).T
        up_left, up_right = jnp.where(left, upstream, zero), jnp.where(left, zero, upstream)
        lhs = rows(lanes(up_left, up_left), lanes(up_right, up_right))
        products = mm(lhs, lanes(x_high, x_low), ACROSS)
        total = total + spread[0] * products[:count] + spread[1] * products[count:]
        if (pair + 1) * PAIR % CHUNK == 0:
            cols = at((pair + 1) * PAIR - CHUNK)
            for source, target in ((yb, y_ref), (db, dx_ref)):
                copy = go.copy(source.at[:, cols], target.at[:, cols])
                copy.start()
                leaving.append(copy)
    dscores_ref[...] = total
    for copy in leaving:
        copy.wait()


def conv_back(dconv, taps, w, z_ref, z_cols, smask):
    count, width = dconv.shape
    z_ref[8 : 8 + count, z_cols] = dconv
    grad = jnp.zeros((count + 8, width), F32)
    for ahead in range(CONV):
        tap = CONV - 1 - ahead
        shifted = z_ref[ahead : ahead + count + 8, z_cols]
        grad = grad + w[tap : tap + 1, :] * (shifted * smask[ahead])
    sums = [jnp.sum(dconv * tap, axis=0, keepdims=True) for tap in taps]
    sums.append(jnp.sum(dconv, axis=0, keepdims=True))
    sums.append(jnp.zeros((3, width), F32))
    return grad[8:].astype(BF16), rows(grad[:8], grad[count:], *sums)


def clear_edges(z_ref, count):
    z_ref[0:8, :] = jnp.zeros((8, z_ref.shape[1]), F32)
    z_ref[8 + count : 16 + count, :] = jnp.zeros((8, z_ref.shape[1]), F32)


def finish_kernel(piece, hops, flag_ref, *refs):
    incs, exchs = refs[:hops], refs[hops : 2 * hops]
    refs = refs[2 * hops :]
    met_ref, act_ref, slope_ref, y_ref, dx_ref, cot_ref, x_ref, halo_ref, w_ref, tab_ref, bc_ref = refs[:11]
    out_ref, gin_ref, misc_ref, dreads_ref, dkeys_ref, scal_ref = refs[-22:-16]
    ib, hb, eb, ab, sb, yb, db, cb, xb, ob, gb, nb, ext_ref, z_ref, in_sems, out_sems = refs[-16:]
    count = xb.shape[0]
    come, go = Flow(in_sems), Flow(out_sems)
    within, base = (piece % TURNS) * WIDTH, piece * WIDTH
    place = flag_ref[1]
    choices = []
    for here, sources, buffer in ((place, incs, ib), (hops - place, exchs, hb)):
        sem = come.used
        come.used += 1
        for i, source in enumerate(sources):
            choices.append((here == i + 1, pltpu.make_async_copy(source, buffer, come.sems.at[sem])))

        @pl.when(here == 0)
        def _():
            buffer[...] = jnp.zeros(buffer.shape, I16)

    for chosen, copy in choices:
        pl.when(chosen)(copy.start)
    arriving, leaving = [], []
    for start in range(0, WIDTH, CHUNK):
        cols, stream_cols, whole_cols = at(start), at(within + start), at(base + start)
        group = [
            come.copy(met_ref.at[:, stream_cols], eb.at[:, cols]),
            come.copy(act_ref.at[:, stream_cols], ab.at[:, cols]),
            come.copy(slope_ref.at[:, stream_cols], sb.at[:, cols]),
            come.copy(y_ref.at[:, cols], yb.at[:, cols]),
            come.copy(dx_ref.at[:, cols], db.at[:, cols]),
            come.copy(cot_ref.at[:, whole_cols], cb.at[:, cols]),
            come.copy(x_ref.at[:, whole_cols], xb.at[:, cols]),
        ]
        for copy in group:
            copy.start()
        arriving.append(group)
    clear_edges(z_ref, count)
    keys, reads = halves(bc_ref[:, :STATE]), halves(bc_ref[:, STATE:])
    keys_both, reads_both = lanes(*keys), lanes(*reads)
    entry, leave = tab_ref[ENTRY : ENTRY + count, :], tab_ref[LEAVE : LEAVE + count, :]
    skip = tab_ref[SKIP : SKIP + 1, :]
    first_core = flag_ref[0] == 0
    mask = columns(tab_ref[MASK : MASK + count, :], CHUNK)
    smask = columns(tab_ref[SMASK : SMASK + count + 8, :], CHUNK)
    dreads = jnp.zeros((count, STATE), F32)
    dkeys = jnp.zeros((count, STATE), F32)
    sums = jnp.zeros((4 * count + 16, 128), F32)
    for chosen, copy in choices:
        pl.when(chosen)(copy.wait)
    for start, group in zip(range(0, WIDTH, CHUNK), arriving):
        cols, whole_cols = at(start), at(base + start)
        head = (base + start) // HEAD_DIM
        for copy in group:
            copy.wait()
        inc, exch = decode(ib[:, cols]), decode(hb[:, cols])
        mine = eb[STATE : STATE + 1, cols] * inc + eb[:STATE, cols]
        state = jnp.where(first_core, exch, mine)
        adjoint = jnp.where(first_core, mine, exch)
        s_high, s_low = halves(state)
        a_high, a_low = halves(adjoint)
        e, leaves = by_head(entry, head, PER), by_head(leave, head, PER)
        act, up = ab[:, cols], cb[:, cols].astype(F32)
        carried = mm(reads_both, rows(s_high, s_high)) + mm(reads[0], s_low)
        y = yb[:, cols] + e * carried
        back = mm(keys_both, rows(a_high, a_high)) + mm(keys[0], a_low)
        back = leaves * back
        dx = db[:, cols] + back
        gain = by_head(skip, head, PER)
        ob[:, cols] = (y + gain * act).astype(BF16)
        ey_high, ey_low = halves(up * e)
        lx_high, lx_low = halves(act * leaves)
        dreads = dreads + mm(lanes(ey_high, ey_high, ey_low), lanes(s_high, s_low, s_high), ACROSS)
        dkeys = dkeys + mm(lanes(lx_high, lx_high, lx_low), lanes(a_high, a_low, a_high), ACROSS)
        through = e[count - 1 : count, :]
        end = jnp.sum(act * back, axis=0, keepdims=True)
        end = end + through * jnp.sum(state * adjoint, axis=0, keepdims=True)
        direct = jnp.sum(up * act, axis=0, keepdims=True)
        received = act * dx
        small = halves(rows(end, direct, jnp.zeros((6, CHUNK), F32)))
        stack = halves(up * y - received) + halves(received)
        pick = (iota((CHUNK, 128), 1) == head + iota((CHUNK, 128), 0) // HEAD_DIM).astype(BF16)
        sums = sums + mm(rows(*stack, rows(*small)), pick)
        dconv = (dx + gain * up) * sb[:, cols]
        ext_ref[8 : 8 + count, cols] = xb[:, cols].astype(F32)
        ext_ref[8 - CONV + 1 : 8, cols] = halo_ref[:, whole_cols].astype(F32)
        taps = taps_of(ext_ref, cols, count, mask)
        gb[:, cols], nb[:, cols] = conv_back(dconv, taps, w_ref[:, whole_cols], z_ref, cols, smask)
        for source, target in ((ob, out_ref), (gb, gin_ref), (nb, misc_ref)):
            copy = go.copy(source.at[:, cols], target.at[:, whole_cols])
            copy.start()
            leaving.append(copy)
    dreads_ref[...] = dreads
    dkeys_ref[...] = dkeys
    drun = sums[:count] + sums[count : 2 * count]
    received = sums[2 * count : 3 * count] + sums[3 * count : 4 * count]
    small = sums[4 * count : 4 * count + 8] + sums[4 * count + 8 :]
    drun = drun + jnp.where(iota((count, 128), 0) == count - 1, small[0:1, :], 0.0)
    later = (iota((count, count), 1) >= iota((count, count), 0)).astype(F32)
    ddecay = jnp.dot(later, drun, precision=EXACT, preferred_element_type=F32)
    pull, rate = tab_ref[PULL : PULL + count, :], tab_ref[RATE : RATE + count, :]
    ddtb = jnp.sum(received * pull + ddecay * rate, axis=0, keepdims=True)
    dalog = jnp.sum(ddecay * tab_ref[DECAY : DECAY + count, :], axis=0, keepdims=True)
    scal_ref[...] = rows(ddtb, dalog, small[1:2, :], jnp.zeros((5, 128), F32))
    for copy in leaving:
        copy.wait()


def final_kernel(x_ref, halo_ref, w_ref, tab_ref, bc_ref, slope_ref, *refs):
    gin_ref, misc_ref, ext_ref, z_ref = refs[-4:]
    parts = refs[: 4 * PIECES]
    count = x_ref.shape[0]
    ext_ref[8 : 8 + count, :] = x_ref[...].astype(F32)
    ext_ref[8 - CONV + 1 : 8, :] = halo_ref[...].astype(F32)
    clear_edges(z_ref, count)
    total = []
    for kind in range(4):
        value = parts[kind * PIECES][...]
        for piece in range(1, PIECES):
            value = value + parts[kind * PIECES + piece][...]
        total.append(value)
    dreads, dkeys, dscores, scal = total
    keys, reads = bc_ref[:, :STATE], bc_ref[:, STATE:]
    dreads = dreads + jnp.dot(dscores, keys, precision=EXACT, preferred_element_type=F32)
    dkeys = dkeys + jnp.dot(dscores.T, reads, precision=EXACT, preferred_element_type=F32)
    cols = slice(0, BC)
    dconv = lanes(dkeys, dreads) * slope_ref[...]
    taps = taps_of(ext_ref, cols, count, columns(tab_ref[MASK : MASK + count, :], BC))
    smask = columns(tab_ref[SMASK : SMASK + count + 8, :], BC)
    gin_ref[...], misc = conv_back(dconv, taps, w_ref[...], z_ref, cols, smask)
    misc_ref[...] = misc
    misc_ref[16 + CONV + 1 : 24, :128] = scal[:3, :]


def whole(shape):
    return pl.BlockSpec(shape, lambda *_: (0,) * len(shape))


def part(shape, *index):
    return pl.BlockSpec(shape, lambda *_: index)


def full(*arrays):
    return [whole(a.shape) for a in arrays]


def call(kernel, ins, specs, outs, out_specs, scratch=(), aliases=None, us=1.0):
    return pl.pallas_call(
        kernel,
        grid=(1,),
        in_specs=specs,
        out_specs=out_specs,
        out_shape=[jax.ShapeDtypeStruct(shape, dtype) for shape, dtype in outs],
        scratch_shapes=list(scratch),
        input_output_aliases=aliases or {},
        compiler_params=pltpu.CompilerParams(vmem_limit_bytes=VMEM_LIMIT),
        cost_estimate=pl.CostEstimate(
            flops=0, bytes_accessed=int(us * 3.5e6), transcendentals=0
        ),
    )(*ins)


def vmem(rows_, cols, dtype=F32):
    return pltpu.VMEM((rows_, cols), dtype)


def sems(count):
    return pltpu.SemaphoreType.DMA((count,))


def permute(value, axis, target):
    size = lax.axis_size(axis)
    return lax.ppermute(value, axis, [(i, target(i)) for i in range(size)])


def other_core(value):
    return permute(value, "seq", lambda i: i ^ 1)


def along(size):
    def target(i):
        if i % 2 == 1:
            return i + 2 if i + 2 < size else i - 1
        return i - 2 if i >= 2 else i + 1

    return target


def xor_sum(value, axis, low):
    size = lax.axis_size(axis)
    bit = low
    while bit < size:
        if 2 * bit < size:
            one = permute(value, axis, lambda i: i ^ bit)
            two = permute(value, axis, lambda i: i ^ (2 * bit))
            three = permute(value, axis, lambda i: i ^ (3 * bit))
            value = (value + one) + (two + three)
            bit *= 4
        else:
            value = value + permute(value, axis, lambda i: i ^ bit)
            bit *= 2
    return value


def hop(pick, mine, met, own, previous):
    ins = [pick, mine, met, own]
    payload = (STATE + 16, WIDTH)
    chunks = WIDTH // CHUNK
    if previous is not None:
        ins.append(previous)
    return call(
        functools.partial(hop_kernel, previous is not None),
        ins,
        [SMEM] + [ANY] * (len(ins) - 1),
        [(payload, I16)],
        [ANY],
        [
            vmem(STATE, WIDTH), vmem(STATE + 8, WIDTH), vmem(8, WIDTH), vmem(*payload, I16),
            vmem(*payload, I16), sems(4 * chunks), sems(chunks),
        ],
        us=2.0,
    )[0]


def on_device(
    conv_input, doc_start, conv_weight, conv_bias, dt_raw, dt_bias, a_log, skip_gain, cotangent
):
    count = conv_input.shape[0]
    size = lax.axis_size("seq")
    index = lax.axis_index("seq")
    core = lax.rem(index, 2)
    chip = lax.div(index, 2)
    hops = size // 2 - 1
    place = jnp.where(core == 1, chip, hops - chip)
    flag = jnp.stack([core, place]).astype(jnp.int32)
    docs = doc_start[None, :]
    edge = part((16, CH), count // 16 - 1, 0)

    tail_out = call(
        tail_kernel, (conv_input, docs), [edge, whole(docs.shape)],
        [((CONV - 1, CH), BF16)], [whole((CONV - 1, CH))],
    )[0]
    halo = lax.ppermute(tail_out, "seq", [(i, i + 1) for i in range(size - 1)])

    bias = conv_bias[None, :]
    prep_in = (docs, dt_raw, dt_bias[None, :], a_log[None, :], skip_gain[None, :])
    table = (TABLE, 128)
    tab = call(prep_kernel, prep_in, full(*prep_in), [(table, F32)], [whole(table)])[0]

    square = (count, count)
    bc_out = [((count, BC), F32), ((count, BC), F32), ((BC, count), F32), (square, F32)]
    locals_ = []
    for stream in range(STREAMS):
        lead = stream == 0
        ins = [flag, conv_input, halo, conv_weight, bias, cotangent, tab]
        specs = [SMEM, ANY, *full(halo, conv_weight, bias), ANY, whole(table)]
        if not lead:
            ins.append(turned)
            specs.append(whole(turned.shape))
        outs = [((count, SPAN), F32), ((count, SPAN), F32), ((STATE + 8, SPAN), F32), ((STATE, SPAN), F32)]
        out_specs = [ANY] * 4
        if lead:
            outs = outs + bc_out
            out_specs = out_specs + [whole(shape) for shape, _ in bc_out]
        chunks = SPAN // CHUNK
        got = call(
            functools.partial(local_kernel, stream),
            ins,
            specs,
            outs,
            out_specs,
            [
                vmem(count, SPAN, BF16), vmem(count, SPAN, BF16), vmem(count, SPAN),
                vmem(count, SPAN), vmem(STATE + 8, SPAN), vmem(STATE, SPAN),
                vmem(count + 8, SPAN), vmem(count, BC, BF16), sems(2 * chunks + 1), sems(4 * chunks),
            ],
            us=5.0,
        )
        locals_.append(got[:4])
        if lead:
            bc_act, bc_slope, turned, scores = got[4:]
    mets = [other_core(send) for _, _, send, _ in locals_]

    received = [[] for _ in range(STREAMS)]
    swapped = [[] for _ in range(STREAMS)]
    previous = [None] * STREAMS
    for turn in range(TURNS + hops - 1):
        piece = jnp.clip(turn - place, 0, TURNS - 1)
        pick = jnp.stack([piece, place]).astype(jnp.int32)
        for stream, (_, _, send, mine) in enumerate(locals_):
            sent = hop(pick, mine, mets[stream], send, previous[stream])
            got = permute(sent, "seq", along(size))
            received[stream].append(got)
            swapped[stream].append(other_core(got))
            previous[stream] = got

    shape = (count, WIDTH)
    chunks = WIDTH // CHUNK
    withins = []
    for j in range(PIECES):
        ins = (locals_[j // TURNS][0], cotangent, tab, scores)
        withins.append(
            call(
                functools.partial(within_kernel, j),
                ins,
                [ANY, ANY, *full(tab, scores)],
                [(shape, F32), (shape, F32), (square, F32)],
                [ANY, ANY, whole(square)],
                [
                    vmem(*shape), vmem(*shape, BF16), vmem(*shape), vmem(*shape),
                    sems(2 * chunks), sems(2 * chunks),
                ],
                us=3.0,
            )
        )

    shared = None
    dreads, dkeys, scals = [None] * PIECES, [None] * PIECES, [None] * PIECES
    shared_out = [((count, INNER), BF16), ((count, CH), BF16), ((24, CH), F32)]
    small_out = [((count, STATE), F32), ((count, STATE), F32), ((8, 128), F32)]
    for turn in range(TURNS):
        for stream in range(STREAMS):
            j = stream * TURNS + turn
            act, slope, _, _ = locals_[stream]
            y, dx, _ = withins[j]
            ins = [flag, *received[stream][turn : turn + hops], *swapped[stream][turn : turn + hops]]
            ins += [mets[stream], act, slope, y, dx, cotangent, conv_input]
            specs = [SMEM] + [ANY] * (len(ins) - 1) + full(halo, conv_weight, tab, bc_act)
            ins += [halo, conv_weight, tab, bc_act]
            aliases = None
            if shared is not None:
                aliases = {len(ins) + i: i for i in range(3)}
                ins += shared
                specs += [ANY] * 3
            payload = (STATE + 16, WIDTH)
            *shared, dreads[j], dkeys[j], scals[j] = call(
                functools.partial(finish_kernel, j, hops),
                ins,
                specs,
                shared_out + small_out,
                [ANY] * 3 + [whole(s) for s, _ in small_out],
                [
                    vmem(*payload, I16), vmem(*payload, I16), vmem(STATE + 8, WIDTH),
                    vmem(*shape), vmem(*shape), vmem(*shape), vmem(*shape), vmem(*shape, BF16),
                    vmem(*shape, BF16), vmem(*shape, BF16), vmem(*shape, BF16), vmem(24, WIDTH),
                    vmem(count + 8, WIDTH), vmem(count + 16, WIDTH),
                    sems(2 + 7 * chunks), sems(3 * chunks),
                ],
                aliases,
                us=5.0,
            )
    output, gin, misc = shared

    dscores = [group[2] for group in withins]
    small = (tab, bc_act, bc_slope, *dreads, *dkeys, *dscores, *scals)
    ins = (conv_input, halo, conv_weight) + small + (gin, misc)
    bc_common = [part((count, BC), 0, BC_AT), part((CONV - 1, BC), 0, BC_AT), part((CONV, BC), 0, BC_AT)]
    gin, misc = call(
        final_kernel,
        ins,
        bc_common + full(*small) + [ANY] * 2,
        shared_out[1:],
        [part((count, BC), 0, BC_AT), part((24, BC), 0, BC_AT)],
        [vmem(count + 8, BC), vmem(count + 16, BC)],
        {len(ins) - 2: 0, len(ins) - 1: 1},
    )

    returned = lax.ppermute(
        misc[8 - CONV + 1 : 8], "seq", [(i, i - 1) for i in range(1, size)]
    )
    grad_input = call(
        edge_kernel,
        (gin, misc, returned, docs),
        [edge, part((8, CH), 1, 0), *full(returned, docs)],
        [((count, CH), BF16)],
        [edge],
        aliases={0: 0},
    )[0]

    half = CH // 2
    lower, upper = misc[16:24, :half], misc[16:24, half:]
    first = core == 0
    value = jnp.where(first, lower, upper)
    value = value + other_core(jnp.where(first, upper, lower))
    value = xor_sum(value, "dp", 1)
    value = xor_sum(value, "seq", 2)
    value = value * float(lax.axis_size("dp") * size * count) ** (-0.5)
    other = other_core(value)
    lower = jnp.where(first, value, other)
    upper = jnp.where(first, other, value)
    summed = jnp.concatenate([lower, upper], axis=1)
    scal = summed[CONV + 1 :, INNER : INNER + HEADS]
    return (output, grad_input, summed[:CONV], summed[CONV], scal[0], scal[1], scal[2])


def solution(mesh):
    return jax.shard_map(
        on_device,
        mesh=mesh,
        in_specs=(
            P(("dp", "seq"), None),
            P(("dp", "seq")),
            P(),
            P(),
            P(("dp", "seq"), None),
            P(),
            P(),
            P(),
            P(("dp", "seq"), None),
        ),
        out_specs=(P(("dp", "seq"), None), P(("dp", "seq"), None), P(), P(), P(), P(), P()),
        check_vma=False,
    )
```

```python
import functools

import jax
import jax.numpy as jnp
from jax import lax
from jax.experimental import pallas as pl
from jax.experimental.pallas import tpu as pltpu
from jax.sharding import PartitionSpec as P

HEADS = 80
HEAD_DIM = 64
STATE = 128
CONV = 4
INNER = 5120
CH = 5376

STREAMS = 2
TURNS = 2
PIECES = STREAMS * TURNS
PIECE_HEADS = HEADS // PIECES
WIDTH = PIECE_HEADS * HEAD_DIM
SPAN = STREAMS * WIDTH
PAIR = 2 * HEAD_DIM
CHUNK = 256
BC = 2 * STATE
BC_AT = INNER // BC
FAR = -1e30
CODE = 32766.0
PER = CHUNK // HEAD_DIM

F32 = jnp.float32
BF16 = jnp.bfloat16
I16 = jnp.int16
EXACT = lax.Precision.HIGHEST
ACROSS = ((1,), (1,))
ANY = pl.BlockSpec(memory_space=pl.ANY)
HBM = pl.BlockSpec(memory_space=pltpu.HBM)
SMEM = pl.BlockSpec(memory_space=pltpu.SMEM)
VMEM_LIMIT = 24 * 1024 * 1024

MASK, ENTRY, LEAVE, PULL, RATE, DECAY, RUN, FAR_AT, ROW, SMASK = range(0, 1280, 128)
SKIP = ROW + HEADS
TABLE = SMASK + 136


def iota(shape, dim):
    return lax.broadcasted_iota(jnp.int32, shape, dim)


def mm(a, b, contract=((1,), (0,))):
    return lax.dot_general(a, b, (contract, ((), ())), preferred_element_type=F32)


def halves(value):
    high = value.astype(BF16)
    return high, (value - high.astype(F32)).astype(BF16)


def lanes(*parts):
    return jnp.concatenate(parts, axis=1)


def rows(*parts):
    return jnp.concatenate(parts, axis=0)


def by_head(table, first, count):
    out = []
    for head in range(first, first + count, 2):
        shape = (table.shape[0], PAIR)
        left = jnp.broadcast_to(table[:, head : head + 1], shape)
        right = jnp.broadcast_to(table[:, head + 1 : head + 2], shape)
        out.append(jnp.where(iota(shape, 1) < HEAD_DIM, left, right))
    return lanes(*out)


def taps_of(ext_ref, cols, count, mask):
    taps = []
    for tap in range(CONV):
        back = CONV - 1 - tap
        value = ext_ref[8 - back : 8 - back + count, cols]
        taps.append(value if back == 0 else value * mask[back])
    return taps


def columns(table, width):
    shape = (table.shape[0], width)
    return [jnp.broadcast_to(table[:, i : i + 1], shape) for i in range(CONV)]


def activate(taps, cols, w_ref, b_ref):
    v = b_ref[:, cols] + w_ref[CONV - 1 : CONV, cols] * taps[CONV - 1]
    for tap in range(CONV - 2, -1, -1):
        v = v + w_ref[tap : tap + 1, cols] * taps[tap]
    gate = 1.0 / (1.0 + jnp.exp(-v))
    return v * gate, gate * (1.0 + v * (1.0 - gate))


class Flow:
    def __init__(self, sems):
        self.sems = sems
        self.used = 0

    def copy(self, source, target):
        made = pltpu.make_async_copy(source, target, self.sems.at[self.used])
        self.used += 1
        return made


def at(first, width=CHUNK):
    return slice(first, first + width)


def tail_kernel(x_ref, doc_ref, out_ref):
    count = doc_ref.shape[1]
    edge = x_ref.shape[0] - CONV + 1
    cut = jnp.zeros((1, 1), F32)
    for back in range(CONV - 1):
        row = edge + CONV - 2 - back
        if back:
            cut = cut + doc_ref[:, count - back : count - back + 1].astype(F32)
        keep = (cut == 0.0).astype(F32)
        value = x_ref[row : row + 1, :].astype(F32) * keep
        out_ref[CONV - 2 - back : CONV - 1 - back, :] = value.astype(BF16)


def edge_kernel(gin_ref, misc_ref, back_ref, doc_ref, out_ref):
    count = doc_ref.shape[1]
    size = gin_ref.shape[0]
    cut = jnp.zeros((1, 1), F32)
    keeps = []
    for back in range(CONV - 1):
        if back:
            cut = cut + doc_ref[:, count - back : count - back + 1].astype(F32)
        keeps.insert(0, (cut == 0.0).astype(F32))
    place = iota((8, 1), 0)
    value = misc_ref[...]
    for i in range(CONV - 1):
        row = 8 - CONV + 1 + i
        value = value + jnp.where(place == row, back_ref[i : i + 1, :] * keeps[i], 0.0)
    out_ref[...] = gin_ref[...]
    out_ref[size - 8 :, :] = value.astype(BF16)


def prep_kernel(doc_ref, raw_ref, dtb_ref, alog_ref, skip_ref, tab_ref):
    count = raw_ref.shape[0]
    resets = doc_ref[...].astype(F32)
    t, s = iota((count, count), 0), iota((count, count), 1)

    def total(keep, shape):
        return jnp.sum(jnp.where(keep, jnp.broadcast_to(resets, shape), 0.0), axis=1, keepdims=True)

    square = (count, count)
    lane = iota((count, 128), 1)
    table = jnp.ones((count, 128), F32)
    for back in range(1, CONV):
        fits = (total((s <= t) & (s > t - back), square) == 0.0).astype(F32)
        table = jnp.where(lane == back, fits, table)
    tab_ref[MASK : MASK + count, :] = table
    wide = (count + 8, count)
    at, s_wide = iota(wide, 0) - 8, iota(wide, 1)
    lane, place = iota((count + 8, 128), 1), iota((count + 8, 128), 0) - 8
    table = jnp.zeros((count + 8, 128), F32)
    for ahead in range(CONV):
        fits = (total((s_wide > at) & (s_wide <= at + ahead), wide) == 0.0).astype(F32)
        fits = jnp.where((place + ahead >= 0) & (place + ahead < count), fits, 0.0)
        table = jnp.where(lane == ahead, fits, table)
    tab_ref[SMASK : SMASK + count + 8, :] = table
    segment = total(s <= t, square)
    reset_col = total(s == t, square)
    segment_row = jnp.sum(
        jnp.where(t <= s, jnp.broadcast_to(reset_col, square), 0.0), axis=0, keepdims=True
    )
    causal = (s <= t) & (segment == segment_row)
    tab_ref[FAR_AT : FAR_AT + count, :] = jnp.where(causal, 0.0, FAR)
    v = raw_ref[...] + dtb_ref[...]
    dt = jnp.maximum(v, 0.0) + jnp.log1p(jnp.exp(-jnp.abs(v)))
    rate = -jnp.exp(alog_ref[...])
    decay = rate * dt
    run = jnp.dot((s <= t).astype(F32), decay, precision=EXACT, preferred_element_type=F32)
    end = run[count - 1 : count, :]
    last = segment == segment[count - 1 : count, :]
    gate = 1.0 / (1.0 + jnp.exp(-v))
    fill = jnp.zeros((count, 128 - HEADS), F32)

    def put(where, value):
        tab_ref[where : where + count, :] = lanes(value, fill)

    put(ENTRY, jnp.where(segment == 0.0, jnp.exp(run), 0.0))
    put(LEAVE, jnp.where(last, jnp.exp(end - run) * dt, 0.0))
    put(PULL, gate / dt)
    put(RATE, rate * gate)
    put(DECAY, decay)
    put(RUN, run)
    tab_ref[ROW : ROW + 128, :] = lanes(jnp.log(dt) - run, fill).T
    tab_ref[SKIP : SKIP + 1, :] = lanes(skip_ref[...], fill[:1])


def scores_of(act):
    keys, reads = act[:, :STATE], act[:, STATE:]
    return lax.dot_general(
        reads, keys, (ACROSS, ((), ())), precision=EXACT, preferred_element_type=F32
    )


def local_kernel(turn, flag_ref, x_ref, halo_ref, w_ref, b_ref, cot_ref, tab_ref, *refs):
    lead = turn == 0
    refs = list(refs)
    if lead:
        bch_ref, bcw_ref, bcb_ref = refs[:3]
        refs = refs[3:]
    else:
        turned_ref = refs.pop(0)
    act_ref, slope_ref = refs[:2]
    send_refs, mine_refs = refs[2 : 2 + STREAMS], refs[2 + STREAMS : 2 + 2 * STREAMS]
    if lead:
        bca_ref, bcs_ref, turned_ref, scores_ref = refs[2 + 2 * STREAMS : 6 + 2 * STREAMS]
    xb, cb, ab, sb, nb, mb, ext_ref, bx, in_sems, out_sems = refs[-10:]
    count = xb.shape[0]
    come, go = Flow(in_sems), Flow(out_sems)
    if lead:
        first = come.copy(x_ref.at[:, at(INNER, BC)], bx)
        first.start()
    arriving, leaving = [], []
    for stream in range(STREAMS):
        cols, whole_cols = at(stream * WIDTH, WIDTH), at(turn * SPAN + stream * WIDTH, WIDTH)
        pair = (
            come.copy(x_ref.at[:, whole_cols], xb.at[:, cols]),
            come.copy(cot_ref.at[:, whole_cols], cb.at[:, cols]),
        )
        for copy in pair:
            copy.start()
        arriving.append(pair)
    mask = columns(tab_ref[MASK : MASK + count, :], CHUNK)

    def load(cols, source, halo):
        ext_ref[8 : 8 + count, cols] = source.astype(F32)
        ext_ref[8 - CONV + 1 : 8, cols] = halo.astype(F32)
        return taps_of(ext_ref, cols, count, mask)

    if lead:
        first.wait()
        act, slope = activate(load(at(SPAN, BC), bx[...], bch_ref[...]), at(0), bcw_ref, bcb_ref)
        bca_ref[...] = act
        bcs_ref[...] = slope
        turned = rows(act[:, :STATE].T, act[:, STATE:].T)
        turned_ref[...] = turned
        scores_ref[...] = scores_of(act)
    else:
        turned = turned_ref[...]
    keys, reads = halves(turned[:STATE, :]), halves(turned[STATE:, :])
    keys_both, reads_both = lanes(*keys), lanes(*reads)
    entry, leave = tab_ref[ENTRY : ENTRY + count, :], tab_ref[LEAVE : LEAVE + count, :]
    first_core = flag_ref[0] == 0
    for stream in range(STREAMS):
        for copy in arriving[stream]:
            copy.wait()
        for start in range(stream * WIDTH, (stream + 1) * WIDTH, CHUNK):
            cols = at(start)
            head = (turn * SPAN + start) // HEAD_DIM
            taps = load(cols, xb[:, cols], halo_ref[:, cols])
            act, slope = activate(taps, cols, w_ref, b_ref)
            ab[:, cols] = act
            sb[:, cols] = slope
            e = by_head(entry, head, PER)
            lx_high, lx_low = halves(act * by_head(leave, head, PER))
            ey_high, ey_low = halves(cb[:, cols].astype(F32) * e)
            state = mm(keys_both, rows(lx_high, lx_high)) + mm(keys[0], lx_low)
            adjoint = mm(reads_both, rows(ey_high, ey_high)) + mm(reads[0], ey_low)
            nb[:STATE, cols] = jnp.where(first_core, state, adjoint)
            mb[:, cols] = jnp.where(first_core, adjoint, state)
            nb[STATE:, cols] = jnp.broadcast_to(e[count - 1 : count, :], (8, CHUNK))
        cols = at(stream * WIDTH, WIDTH)
        targets = (send_refs[stream], mine_refs[stream], act_ref.at[:, cols], slope_ref.at[:, cols])
        for source, target in zip((nb, mb, ab, sb), targets):
            copy = go.copy(source.at[:, cols], target)
            copy.start()
            leaving.append(copy)
    for copy in leaving:
        copy.wait()


def decode(codes):
    scale = jnp.exp2(codes[STATE : STATE + 1, :].astype(F32) * (1.0 / 256.0)) * (1.0 / CODE)
    return codes[:STATE, :].astype(F32) * scale


def encode(value):
    most = jnp.max(jnp.abs(value), axis=0, keepdims=True)
    power = jnp.ceil(jnp.log2(jnp.maximum(most, 1e-30)) * 256.0)
    scale = jnp.exp2(power * (1.0 / 256.0)) * (1.0 / CODE)
    codes = jnp.floor(value * (1.0 / scale) + 0.5).astype(jnp.int32)
    tail = jnp.broadcast_to(power.astype(jnp.int32), (16, value.shape[1]))
    return rows(codes, tail).astype(I16)


def chip_kernel(lead, mine_ref, met_ref, own_ref, *refs):
    chip_ref = refs[0]
    mb, eb, ob, sem = refs[-4:]
    come = Flow(sem)
    copies = [
        come.copy(mine_ref, mb),
        come.copy(met_ref, eb),
        come.copy(own_ref.at[pl.ds(STATE, 8), :], ob),
    ]
    for copy in copies:
        copy.start()
    for copy in copies:
        copy.wait()
    for start in range(0, WIDTH, CHUNK):
        cols = at(start)
        own = ob[0:1, cols]
        value = mb[:, cols] + own * eb[:STATE, cols]
        chip_ref[:STATE, cols] = value
        chip_ref[STATE:, cols] = own * eb[STATE:, cols]
        if lead:
            refs[1][:, cols] = encode(value)


def hop_kernel(pick_ref, previous_ref, *refs):
    chip_refs, out_ref = refs[:-1], refs[-1]
    for start in range(0, WIDTH, CHUNK):
        cols = at(start)
        chip = chip_refs[0][:, cols]
        for i, ref in enumerate(chip_refs[1:]):
            chip = jnp.where(pick_ref[0] > i, ref[:, cols], chip)
        before = jnp.where(pick_ref[1] == 0, 0.0, decode(previous_ref[:, cols]))
        out_ref[:, cols] = encode(chip[:STATE, :] + chip[STATE : STATE + 1, :] * before)


def within_kernel(piece, act_ref, cot_ref, tab_ref, scores_ref, y_ref, dx_ref, dscores_ref, *refs):
    ab, cb, yb, db, in_sems, out_sems = refs
    count = ab.shape[0]
    come, go = Flow(in_sems), Flow(out_sems)
    base = (piece % STREAMS) * WIDTH
    copies = (
        come.copy(act_ref.at[:, at(base, WIDTH)], ab),
        come.copy(cot_ref.at[:, at(piece * WIDTH, WIDTH)], cb),
    )
    for copy in copies:
        copy.start()
    for copy in copies:
        copy.wait()
    run = tab_ref[RUN : RUN + count, :]
    far, scores = tab_ref[FAR_AT : FAR_AT + count, :], scores_ref[...]
    left = iota((count, PAIR), 1) < HEAD_DIM
    total = jnp.zeros((count, count), F32)
    zero = jnp.zeros((count, PAIR), BF16)
    for pair in range(PIECE_HEADS // 2):
        cols = at(pair * PAIR, PAIR)
        x_high, x_low = halves(ab[:, cols])
        upstream = cb[:, cols]
        upstream_turned = upstream.astype(F32).T.astype(BF16)
        spread, weights = [], []
        for side in range(2):
            head = piece * PIECE_HEADS + 2 * pair + side
            row = tab_ref[ROW + head : ROW + head + 1, :]
            within = jnp.exp(run[:, head : head + 1] + row + far)
            spread.append(within)
            weights.append(lanes(*halves(within * scores)))
        out = mm(rows(*weights), rows(lanes(x_high, x_low), lanes(x_high, zero)))
        out = out[:, :PAIR] + out[:, PAIR:]
        yb[:, cols] = jnp.where(left, out[:count], out[count:])
        parts = []
        for side in range(2):
            mine = upstream_turned[side * HEAD_DIM : (side + 1) * HEAD_DIM, :]
            pushed = rows(weights[side][:, :count], weights[side][:, count:])
            parts.append(mm(lanes(mine, mine), pushed))
        db[:, cols] = rows(*parts).T
        up_left, up_right = jnp.where(left, upstream, zero), jnp.where(left, zero, upstream)
        lhs = rows(lanes(up_left, up_left), lanes(up_right, up_right))
        products = mm(lhs, lanes(x_high, x_low), ACROSS)
        total = total + spread[0] * products[:count] + spread[1] * products[count:]
    copies = (go.copy(yb, y_ref), go.copy(db, dx_ref))
    for copy in copies:
        copy.start()
    dscores_ref[...] = total
    for copy in copies:
        copy.wait()


def conv_back(dconv, taps, w, z_ref, z_cols, smask):
    count, width = dconv.shape
    z_ref[8 : 8 + count, z_cols] = dconv
    grad = jnp.zeros((count + 8, width), F32)
    for ahead in range(CONV):
        tap = CONV - 1 - ahead
        shifted = z_ref[ahead : ahead + count + 8, z_cols]
        grad = grad + w[tap : tap + 1, :] * (shifted * smask[ahead])
    sums = [jnp.sum(dconv * tap, axis=0, keepdims=True) for tap in taps]
    sums.append(jnp.sum(dconv, axis=0, keepdims=True))
    sums.append(jnp.zeros((3, width), F32))
    return grad[8:].astype(BF16), rows(grad[:8], grad[count:], *sums)


def clear_edges(z_ref, count):
    z_ref[0:8, :] = jnp.zeros((8, z_ref.shape[1]), F32)
    z_ref[8 + count : 16 + count, :] = jnp.zeros((8, z_ref.shape[1]), F32)


def finish_kernel(piece, hops, flag_ref, *refs):
    incs, exchs = refs[:hops], refs[hops : 2 * hops]
    refs = refs[2 * hops :]
    met_ref, act_ref, slope_ref, y_ref, dx_ref, cot_ref, x_ref, halo_ref, w_ref, tab_ref, bc_ref = refs[:11]
    out_ref, gin_ref, misc_ref, dreads_ref, dkeys_ref, scal_ref = refs[-22:-16]
    ib, hb, eb, ab, sb, yb, db, cb, xb, ob, gb, nb, ext_ref, z_ref, in_sems, out_sems = refs[-16:]
    count = xb.shape[0]
    come, go = Flow(in_sems), Flow(out_sems)
    within, base = (piece % STREAMS) * WIDTH, piece * WIDTH
    place = flag_ref[1]
    choices = []
    for here, sources, buffer in ((place, incs, ib), (hops - place, exchs, hb)):
        sem = come.used
        come.used += 1
        for i, source in enumerate(sources):
            choices.append((here == i + 1, pltpu.make_async_copy(source, buffer, come.sems.at[sem])))

        @pl.when(here == 0)
        def _():
            buffer[...] = jnp.zeros(buffer.shape, I16)

    for chosen, copy in choices:
        pl.when(chosen)(copy.start)
    arriving, leaving = [], []
    for start, width in ((0, CHUNK), (CHUNK, WIDTH - CHUNK)):
        cols = at(start, width)
        stream_cols, whole_cols = at(within + start, width), at(base + start, width)
        group = [
            come.copy(met_ref.at[:, cols], eb.at[:, cols]),
            come.copy(act_ref.at[:, stream_cols], ab.at[:, cols]),
            come.copy(slope_ref.at[:, stream_cols], sb.at[:, cols]),
            come.copy(y_ref.at[:, cols], yb.at[:, cols]),
            come.copy(dx_ref.at[:, cols], db.at[:, cols]),
            come.copy(cot_ref.at[:, whole_cols], cb.at[:, cols]),
            come.copy(x_ref.at[:, whole_cols], xb.at[:, cols]),
        ]
        for copy in group:
            copy.start()
        arriving.append(group)
    clear_edges(z_ref, count)
    keys, reads = halves(bc_ref[:, :STATE]), halves(bc_ref[:, STATE:])
    keys_both, reads_both = lanes(*keys), lanes(*reads)
    entry, leave = tab_ref[ENTRY : ENTRY + count, :], tab_ref[LEAVE : LEAVE + count, :]
    skip = tab_ref[SKIP : SKIP + 1, :]
    first_core = flag_ref[0] == 0
    mask = columns(tab_ref[MASK : MASK + count, :], CHUNK)
    smask = columns(tab_ref[SMASK : SMASK + count + 8, :], CHUNK)
    dreads = jnp.zeros((count, STATE), F32)
    dkeys = jnp.zeros((count, STATE), F32)
    sums = jnp.zeros((4 * count + 16, 128), F32)
    for chosen, copy in choices:
        pl.when(chosen)(copy.wait)
    for start in range(0, WIDTH, CHUNK):
        cols, whole_cols = at(start), at(base + start)
        head = (base + start) // HEAD_DIM
        if start <= CHUNK:
            for copy in arriving[start // CHUNK]:
                copy.wait()
        inc, exch = decode(ib[:, cols]), decode(hb[:, cols])
        mine = eb[STATE : STATE + 1, cols] * inc + eb[:STATE, cols]
        state = jnp.where(first_core, exch, mine)
        adjoint = jnp.where(first_core, mine, exch)
        s_high, s_low = halves(state)
        a_high, a_low = halves(adjoint)
        e, leaves = by_head(entry, head, PER), by_head(leave, head, PER)
        act, up = ab[:, cols], cb[:, cols].astype(F32)
        carried = mm(reads_both, rows(s_high, s_high)) + mm(reads[0], s_low)
        y = yb[:, cols] + e * carried
        back = mm(keys_both, rows(a_high, a_high)) + mm(keys[0], a_low)
        back = leaves * back
        dx = db[:, cols] + back
        gain = by_head(skip, head, PER)
        ob[:, cols] = (y + gain * act).astype(BF16)
        ey_high, ey_low = halves(up * e)
        lx_high, lx_low = halves(act * leaves)
        dreads = dreads + mm(lanes(ey_high, ey_high, ey_low), lanes(s_high, s_low, s_high), ACROSS)
        dkeys = dkeys + mm(lanes(lx_high, lx_high, lx_low), lanes(a_high, a_low, a_high), ACROSS)
        through = e[count - 1 : count, :]
        end = jnp.sum(act * back, axis=0, keepdims=True)
        end = end + through * jnp.sum(state * adjoint, axis=0, keepdims=True)
        direct = jnp.sum(up * act, axis=0, keepdims=True)
        received = act * dx
        small = halves(rows(end, direct, jnp.zeros((6, CHUNK), F32)))
        stack = halves(up * y - received) + halves(received)
        pick = (iota((CHUNK, 128), 1) == head + iota((CHUNK, 128), 0) // HEAD_DIM).astype(BF16)
        sums = sums + mm(rows(*stack, rows(*small)), pick)
        dconv = (dx + gain * up) * sb[:, cols]
        ext_ref[8 : 8 + count, cols] = xb[:, cols].astype(F32)
        ext_ref[8 - CONV + 1 : 8, cols] = halo_ref[:, whole_cols].astype(F32)
        taps = taps_of(ext_ref, cols, count, mask)
        gb[:, cols], nb[:, cols] = conv_back(dconv, taps, w_ref[:, whole_cols], z_ref, cols, smask)
    for source, target in ((ob, out_ref), (gb, gin_ref), (nb, misc_ref)):
        copy = go.copy(source, target.at[:, at(base, WIDTH)])
        copy.start()
        leaving.append(copy)
    dreads_ref[...] = dreads
    dkeys_ref[...] = dkeys
    drun = sums[:count] + sums[count : 2 * count]
    received = sums[2 * count : 3 * count] + sums[3 * count : 4 * count]
    small = sums[4 * count : 4 * count + 8] + sums[4 * count + 8 :]
    drun = drun + jnp.where(iota((count, 128), 0) == count - 1, small[0:1, :], 0.0)
    later = (iota((count, count), 1) >= iota((count, count), 0)).astype(F32)
    ddecay = jnp.dot(later, drun, precision=EXACT, preferred_element_type=F32)
    pull, rate = tab_ref[PULL : PULL + count, :], tab_ref[RATE : RATE + count, :]
    ddtb = jnp.sum(received * pull + ddecay * rate, axis=0, keepdims=True)
    dalog = jnp.sum(ddecay * tab_ref[DECAY : DECAY + count, :], axis=0, keepdims=True)
    scal_ref[...] = rows(ddtb, dalog, small[1:2, :], jnp.zeros((5, 128), F32))
    for copy in leaving:
        copy.wait()


def final_kernel(x_ref, halo_ref, w_ref, tab_ref, bc_ref, slope_ref, *refs):
    gin_ref, misc_ref, ext_ref, z_ref = refs[-4:]
    parts = refs[: 4 * PIECES]
    count = x_ref.shape[0]
    ext_ref[8 : 8 + count, :] = x_ref[...].astype(F32)
    ext_ref[8 - CONV + 1 : 8, :] = halo_ref[...].astype(F32)
    clear_edges(z_ref, count)
    total = []
    for kind in range(4):
        value = parts[kind * PIECES][...]
        for piece in range(1, PIECES):
            value = value + parts[kind * PIECES + piece][...]
        total.append(value)
    dreads, dkeys, dscores, scal = total
    keys, reads = bc_ref[:, :STATE], bc_ref[:, STATE:]
    dreads = dreads + jnp.dot(dscores, keys, precision=EXACT, preferred_element_type=F32)
    dkeys = dkeys + jnp.dot(dscores.T, reads, precision=EXACT, preferred_element_type=F32)
    cols = slice(0, BC)
    dconv = lanes(dkeys, dreads) * slope_ref[...]
    taps = taps_of(ext_ref, cols, count, columns(tab_ref[MASK : MASK + count, :], BC))
    smask = columns(tab_ref[SMASK : SMASK + count + 8, :], BC)
    gin_ref[...], misc = conv_back(dconv, taps, w_ref[...], z_ref, cols, smask)
    misc_ref[...] = misc
    misc_ref[16 + CONV + 1 : 24, :128] = scal[:3, :]


def cost(us):
    return pl.CostEstimate(flops=int(us * 1.1e9), bytes_accessed=1000, transcendentals=0)


def whole(shape):
    return pl.BlockSpec(shape, lambda *_: (0,) * len(shape))


def part(shape, *index):
    return pl.BlockSpec(shape, lambda *_: index)


def full(*arrays):
    return [whole(a.shape) for a in arrays]


def call(kernel, ins, specs, outs, out_specs, scratch=(), aliases=None, us=1.0):
    return pl.pallas_call(
        kernel,
        grid=(1,),
        in_specs=specs,
        out_specs=out_specs,
        out_shape=[jax.ShapeDtypeStruct(shape, dtype) for shape, dtype in outs],
        scratch_shapes=list(scratch),
        input_output_aliases=aliases or {},
        compiler_params=pltpu.CompilerParams(vmem_limit_bytes=VMEM_LIMIT),
        cost_estimate=cost(us),
    )(*ins)


def vmem(rows_, cols, dtype=F32):
    return pltpu.VMEM((rows_, cols), dtype)


def sems(count):
    return pltpu.SemaphoreType.DMA((count,))


def permute(value, axis, target):
    size = lax.axis_size(axis)
    return lax.ppermute(value, axis, [(i, target(i)) for i in range(size)])


def other_core(value):
    return permute(value, "seq", lambda i: i ^ 1)


def along(size):
    def target(i):
        if i % 2 == 1:
            return i + 2 if i + 2 < size else i - 1
        return i - 2 if i >= 2 else i + 1

    return target


def xor_sum(value, axis, low):
    size = lax.axis_size(axis)
    bit = low
    while bit < size:
        if 2 * bit < size:
            one = permute(value, axis, lambda i: i ^ bit)
            two = permute(value, axis, lambda i: i ^ (2 * bit))
            three = permute(value, axis, lambda i: i ^ (3 * bit))
            value = (value + one) + (two + three)
            bit *= 4
        else:
            value = value + permute(value, axis, lambda i: i ^ bit)
            bit *= 2
    return value


def chip_of(lead, mine, met, own):
    state = (STATE + 8, WIDTH)
    payload = (STATE + 16, WIDTH)
    outs = [(state, F32)] + [(payload, I16)] * lead
    return call(
        functools.partial(chip_kernel, lead),
        (mine, met, own),
        [HBM] * 3,
        outs,
        [whole(s) for s, _ in outs],
        [vmem(STATE, WIDTH), vmem(*state), vmem(8, WIDTH), sems(3)],
        us=1.5,
    )


def hop(pick, previous, chips):
    payload = (STATE + 16, WIDTH)
    return call(
        hop_kernel,
        (pick, previous, *chips),
        [SMEM, *full(previous, *chips)],
        [(payload, I16)],
        [whole(payload)],
        us=0.8,
    )[0]


def on_device(
    conv_input, doc_start, conv_weight, conv_bias, dt_raw, dt_bias, a_log, skip_gain, cotangent
):
    count = conv_input.shape[0]
    size = lax.axis_size("seq")
    index = lax.axis_index("seq")
    core = lax.rem(index, 2)
    chip = lax.div(index, 2)
    hops = size // 2 - 1
    place = jnp.where(core == 1, chip, hops - chip)
    flag = jnp.stack([core, place]).astype(jnp.int32)
    docs = doc_start[None, :]
    edge = part((16, CH), count // 16 - 1, 0)

    tail_out = call(
        tail_kernel, (conv_input, docs), [edge, whole(docs.shape)],
        [((CONV - 1, CH), BF16)], [whole((CONV - 1, CH))],
    )[0]
    halo = lax.ppermute(tail_out, "seq", [(i, i + 1) for i in range(size - 1)])

    bias = conv_bias[None, :]
    prep_in = (docs, dt_raw, dt_bias[None, :], a_log[None, :], skip_gain[None, :])
    table = (TABLE, 128)
    tab = call(prep_kernel, prep_in, full(*prep_in), [(table, F32)], [whole(table)])[0]

    square = (count, count)
    payload = (STATE + 16, WIDTH)
    shape = (count, WIDTH)
    acts, slopes, chips, sent = [], [], [], []
    mets = []
    given = tab
    for turn in range(TURNS):
        lead = turn == 0
        here = [part((height, SPAN), 0, turn) for height in (CONV - 1, CONV, 1)]
        ins = [flag, conv_input, halo, conv_weight, bias, cotangent, given]
        specs = [SMEM, HBM, *here, HBM, whole(table)]
        outs = [(count, SPAN)] * 2 + [(STATE + 8, WIDTH)] * STREAMS + [(STATE, WIDTH)] * STREAMS
        out_specs = [HBM] * len(outs)
        if lead:
            ins += [halo, conv_weight, bias]
            specs += [part((height, BC), 0, BC_AT) for height in (CONV - 1, CONV, 1)]
            bc_out = [(count, BC), (count, BC), (BC, count), square]
            outs += bc_out
            out_specs += [whole(s) for s in bc_out]
        else:
            ins.append(turned)
            specs.append(whole(turned.shape))
        got = call(
            functools.partial(local_kernel, turn),
            ins,
            specs,
            [(s, F32) for s in outs],
            out_specs,
            [
                vmem(count, SPAN, BF16), vmem(count, SPAN, BF16), vmem(count, SPAN),
                vmem(count, SPAN), vmem(STATE + 8, SPAN), vmem(STATE, SPAN),
                vmem(count + 8, SPAN + BC), vmem(count, BC, BF16),
                sems(2 * STREAMS + 1), sems(4 * STREAMS),
            ],
            us=5.0,
        )
        act, slope, *got = got
        if lead:
            bc_act, bc_slope, turned, scores = got[2 * STREAMS :]
        acts.append(act)
        slopes.append(slope)
        for stream in range(STREAMS):
            send, mine = got[stream], got[STREAMS + stream]
            met = other_core(send)
            mets.append(met)
            chip, *first = chip_of(lead, mine, met, send)
            chips.append(chip)
            sent += first
        if lead:
            given, *sent = lax.optimization_barrier((given, *sent))

    received = [[] for _ in range(STREAMS)]
    swapped = [[] for _ in range(STREAMS)]
    for turn in range(TURNS + hops - 1):
        if turn:
            piece = jnp.clip(turn - place, 0, TURNS - 1)
            pick = jnp.stack([piece, place]).astype(jnp.int32)
            sent = [
                hop(pick, received[stream][-1], chips[stream::STREAMS]) for stream in range(STREAMS)
            ]
        for stream in range(STREAMS):
            got = permute(sent[stream], "seq", along(size))
            received[stream].append(got)
            swapped[stream].append(other_core(got))

    withins = []
    for j in range(PIECES):
        ins = (acts[j // STREAMS], cotangent, tab, scores)
        withins.append(
            call(
                functools.partial(within_kernel, j),
                ins,
                [HBM, HBM, *full(tab, scores)],
                [(shape, F32), (shape, F32), (square, F32)],
                [HBM, HBM, whole(square)],
                [vmem(*shape), vmem(*shape, BF16), vmem(*shape), vmem(*shape), sems(2), sems(2)],
                us=3.0,
            )
        )

    shared = None
    dreads, dkeys, scals = [None] * PIECES, [None] * PIECES, [None] * PIECES
    shared_out = [((count, INNER), BF16), ((count, CH), BF16), ((24, CH), F32)]
    small_out = [((count, STATE), F32), ((count, STATE), F32), ((8, 128), F32)]
    for j in range(PIECES):
        turn, stream = j // STREAMS, j % STREAMS
        y, dx, _ = withins[j]
        ins = [flag, *received[stream][turn : turn + hops], *swapped[stream][turn : turn + hops]]
        specs = [SMEM] + [ANY] * (2 * hops)
        ins += [mets[j], acts[turn], slopes[turn], y, dx, cotangent, conv_input]
        specs += [HBM] * 7 + full(halo, conv_weight, tab, bc_act)
        ins += [halo, conv_weight, tab, bc_act]
        aliases = None
        if shared is not None:
            aliases = {len(ins) + i: i for i in range(3)}
            ins += shared
            specs += [HBM] * 3
        *shared, dreads[j], dkeys[j], scals[j] = call(
            functools.partial(finish_kernel, j, hops),
            ins,
            specs,
            shared_out + small_out,
            [HBM] * 3 + [whole(s) for s, _ in small_out],
            [
                vmem(*payload, I16), vmem(*payload, I16), vmem(STATE + 8, WIDTH),
                vmem(*shape), vmem(*shape), vmem(*shape), vmem(*shape), vmem(*shape, BF16),
                vmem(*shape, BF16), vmem(*shape, BF16), vmem(*shape, BF16), vmem(24, WIDTH),
                vmem(count + 8, WIDTH), vmem(count + 16, WIDTH), sems(2 + 14), sems(3),
            ],
            aliases,
            us=5.0,
        )
    output, gin, misc = shared

    dscores = [group[2] for group in withins]
    small = (tab, bc_act, bc_slope, *dreads, *dkeys, *dscores, *scals)
    ins = (conv_input, halo, conv_weight) + small + (gin, misc)
    bc_common = [part((count, BC), 0, BC_AT), part((CONV - 1, BC), 0, BC_AT), part((CONV, BC), 0, BC_AT)]
    gin, misc = call(
        final_kernel,
        ins,
        bc_common + full(*small) + [ANY] * 2,
        shared_out[1:],
        [part((count, BC), 0, BC_AT), part((24, BC), 0, BC_AT)],
        [vmem(count + 8, BC), vmem(count + 16, BC)],
        {len(ins) - 2: 0, len(ins) - 1: 1},
    )

    returned = lax.ppermute(
        misc[8 - CONV + 1 : 8], "seq", [(i, i - 1) for i in range(1, size)]
    )
    grad_input = call(
        edge_kernel,
        (gin, misc, returned, docs),
        [edge, part((8, CH), 1, 0), *full(returned, docs)],
        [((count, CH), BF16)],
        [edge],
        aliases={0: 0},
    )[0]

    half = CH // 2
    lower, upper = misc[16:24, :half], misc[16:24, half:]
    first = core == 0
    value = jnp.where(first, lower, upper)
    value = value + other_core(jnp.where(first, upper, lower))
    value = xor_sum(value, "dp", 1)
    value = xor_sum(value, "seq", 2)
    value = value * float(lax.axis_size("dp") * size * count) ** (-0.5)
    other = other_core(value)
    lower = jnp.where(first, value, other)
    upper = jnp.where(first, other, value)
    summed = jnp.concatenate([lower, upper], axis=1)
    scal = summed[CONV + 1 :, INNER : INNER + HEADS]
    return (output, grad_input, summed[:CONV], summed[CONV], scal[0], scal[1], scal[2])


def solution(mesh):
    return jax.shard_map(
        on_device,
        mesh=mesh,
        in_specs=(
            P(("dp", "seq"), None),
            P(("dp", "seq")),
            P(),
            P(),
            P(("dp", "seq"), None),
            P(),
            P(),
            P(),
            P(("dp", "seq"), None),
        ),
        out_specs=(P(("dp", "seq"), None), P(("dp", "seq"), None), P(), P(), P(), P(), P()),
        check_vma=False,
    )
```

```python
import functools

import jax
import jax.numpy as jnp
from jax import lax
from jax.experimental import pallas as pl
from jax.experimental.pallas import tpu as pltpu
from jax.sharding import PartitionSpec as P

HEADS = 80
HEAD_DIM = 64
STATE = 128
CONV = 4
INNER = 5120
CH = 5376

STREAMS = 2
TURNS = 2
PIECES = STREAMS * TURNS
PIECE_HEADS = HEADS // PIECES
WIDTH = PIECE_HEADS * HEAD_DIM
SPAN = STREAMS * WIDTH
PAIR = 2 * HEAD_DIM
CHUNK = 256
BC = 2 * STATE
BC_AT = INNER // BC
FAR = -1e30
CODE = 32766.0
PER = CHUNK // HEAD_DIM

F32 = jnp.float32
BF16 = jnp.bfloat16
I16 = jnp.int16
EXACT = lax.Precision.HIGHEST
ACROSS = ((1,), (1,))
ANY = pl.BlockSpec(memory_space=pl.ANY)
HBM = pl.BlockSpec(memory_space=pltpu.HBM)
SMEM = pl.BlockSpec(memory_space=pltpu.SMEM)
VMEM_LIMIT = 24 * 1024 * 1024

MASK, ENTRY, LEAVE, PULL, RATE, DECAY, RUN, FAR_AT, ROW, SMASK = range(0, 1280, 128)
SKIP = ROW + HEADS
TABLE = SMASK + 136


def iota(shape, dim):
    return lax.broadcasted_iota(jnp.int32, shape, dim)


def mm(a, b, contract=((1,), (0,))):
    return lax.dot_general(a, b, (contract, ((), ())), preferred_element_type=F32)


def halves(value):
    high = value.astype(BF16)
    return high, (value - high.astype(F32)).astype(BF16)


def lanes(*parts):
    return jnp.concatenate(parts, axis=1)


def rows(*parts):
    return jnp.concatenate(parts, axis=0)


def by_head(table, first, count):
    out = []
    for head in range(first, first + count, 2):
        shape = (table.shape[0], PAIR)
        left = jnp.broadcast_to(table[:, head : head + 1], shape)
        right = jnp.broadcast_to(table[:, head + 1 : head + 2], shape)
        out.append(jnp.where(iota(shape, 1) < HEAD_DIM, left, right))
    return lanes(*out)


def taps_of(ext_ref, cols, count, mask):
    taps = []
    for tap in range(CONV):
        back = CONV - 1 - tap
        value = ext_ref[8 - back : 8 - back + count, cols]
        taps.append(value if back == 0 else value * mask[back])
    return taps


def columns(table, width):
    shape = (table.shape[0], width)
    return [jnp.broadcast_to(table[:, i : i + 1], shape) for i in range(CONV)]


def activate(taps, cols, w_ref, b_ref):
    v = b_ref[:, cols] + w_ref[CONV - 1 : CONV, cols] * taps[CONV - 1]
    for tap in range(CONV - 2, -1, -1):
        v = v + w_ref[tap : tap + 1, cols] * taps[tap]
    gate = 1.0 / (1.0 + jnp.exp(-v))
    return v * gate, gate * (1.0 + v * (1.0 - gate))


class Flow:
    def __init__(self, sems):
        self.sems = sems
        self.used = 0

    def copy(self, source, target):
        made = pltpu.make_async_copy(source, target, self.sems.at[self.used])
        self.used += 1
        return made


def at(first, width=CHUNK):
    return slice(first, first + width)


def tail_kernel(x_ref, doc_ref, out_ref):
    count = doc_ref.shape[1]
    edge = x_ref.shape[0] - CONV + 1
    cut = jnp.zeros((1, 1), F32)
    for back in range(CONV - 1):
        row = edge + CONV - 2 - back
        if back:
            cut = cut + doc_ref[:, count - back : count - back + 1].astype(F32)
        keep = (cut == 0.0).astype(F32)
        value = x_ref[row : row + 1, :].astype(F32) * keep
        out_ref[CONV - 2 - back : CONV - 1 - back, :] = value.astype(BF16)


def edge_kernel(gin_ref, misc_ref, back_ref, doc_ref, out_ref):
    count = doc_ref.shape[1]
    size = gin_ref.shape[0]
    cut = jnp.zeros((1, 1), F32)
    keeps = []
    for back in range(CONV - 1):
        if back:
            cut = cut + doc_ref[:, count - back : count - back + 1].astype(F32)
        keeps.insert(0, (cut == 0.0).astype(F32))
    place = iota((8, 1), 0)
    value = misc_ref[...]
    for i in range(CONV - 1):
        row = 8 - CONV + 1 + i
        value = value + jnp.where(place == row, back_ref[i : i + 1, :] * keeps[i], 0.0)
    out_ref[...] = gin_ref[...]
    out_ref[size - 8 :, :] = value.astype(BF16)


def prep_kernel(doc_ref, raw_ref, dtb_ref, alog_ref, skip_ref, tab_ref):
    count = raw_ref.shape[1]
    resets = doc_ref[...].astype(F32)
    t, s = iota((count, count), 0), iota((count, count), 1)

    def total(keep, shape):
        return jnp.sum(jnp.where(keep, jnp.broadcast_to(resets, shape), 0.0), axis=1, keepdims=True)

    square = (count, count)
    lane = iota((count, 128), 1)
    table = jnp.ones((count, 128), F32)
    for back in range(1, CONV):
        fits = (total((s <= t) & (s > t - back), square) == 0.0).astype(F32)
        table = jnp.where(lane == back, fits, table)
    tab_ref[MASK : MASK + count, :] = table
    wide = (count + 8, count)
    at, s_wide = iota(wide, 0) - 8, iota(wide, 1)
    lane, place = iota((count + 8, 128), 1), iota((count + 8, 128), 0) - 8
    table = jnp.zeros((count + 8, 128), F32)
    for ahead in range(CONV):
        fits = (total((s_wide > at) & (s_wide <= at + ahead), wide) == 0.0).astype(F32)
        fits = jnp.where((place + ahead >= 0) & (place + ahead < count), fits, 0.0)
        table = jnp.where(lane == ahead, fits, table)
    tab_ref[SMASK : SMASK + count + 8, :] = table
    segment = total(s <= t, square)
    reset_col = total(s == t, square)
    segment_row = jnp.sum(
        jnp.where(t <= s, jnp.broadcast_to(reset_col, square), 0.0), axis=0, keepdims=True
    )
    causal = (s <= t) & (segment == segment_row)
    tab_ref[FAR_AT : FAR_AT + count, :] = jnp.where(causal, 0.0, FAR)
    raw = rows(raw_ref[...], jnp.zeros((128 - HEADS, count), F32)).T[:, :HEADS]
    v = raw + dtb_ref[...]
    dt = jnp.maximum(v, 0.0) + jnp.log1p(jnp.exp(-jnp.abs(v)))
    rate = -jnp.exp(alog_ref[...])
    decay = rate * dt
    run = jnp.dot((s <= t).astype(F32), decay, precision=EXACT, preferred_element_type=F32)
    end = run[count - 1 : count, :]
    last = segment == segment[count - 1 : count, :]
    gate = 1.0 / (1.0 + jnp.exp(-v))
    fill = jnp.zeros((count, 128 - HEADS), F32)

    def put(where, value):
        tab_ref[where : where + count, :] = lanes(value, fill)

    put(ENTRY, jnp.where(segment == 0.0, jnp.exp(run), 0.0))
    put(LEAVE, jnp.where(last, jnp.exp(end - run) * dt, 0.0))
    put(PULL, gate / dt)
    put(RATE, rate * gate)
    put(DECAY, decay)
    put(RUN, run)
    tab_ref[ROW : ROW + 128, :] = lanes(jnp.log(dt) - run, fill).T
    tab_ref[SKIP : SKIP + 1, :] = lanes(skip_ref[...], fill[:1])


def scores_of(act):
    keys, reads = act[:, :STATE], act[:, STATE:]
    return lax.dot_general(
        reads, keys, (ACROSS, ((), ())), precision=EXACT, preferred_element_type=F32
    )


def local_kernel(turn, flag_ref, x_ref, halo_ref, w_ref, b_ref, cot_ref, tab_ref, *refs):
    lead = turn == 0
    refs = list(refs)
    if lead:
        bch_ref, bcw_ref, bcb_ref = refs[:3]
        refs = refs[3:]
    else:
        turned_ref = refs.pop(0)
    send_refs, mine_refs = refs[:STREAMS], refs[STREAMS : 2 * STREAMS]
    if lead:
        bca_ref, bcs_ref, turned_ref, scores_ref = refs[2 * STREAMS : 4 + 2 * STREAMS]
    xb, cb, nb, mb, ext_ref, bx, in_sems, out_sems = refs[-8:]
    count = xb.shape[0]
    come, go = Flow(in_sems), Flow(out_sems)
    if lead:
        first = come.copy(x_ref.at[:, at(INNER, BC)], bx)
        first.start()
    arriving, leaving = [], []
    for stream in range(STREAMS):
        cols, whole_cols = at(stream * WIDTH, WIDTH), at(turn * SPAN + stream * WIDTH, WIDTH)
        pair = (
            come.copy(x_ref.at[:, whole_cols], xb.at[:, cols]),
            come.copy(cot_ref.at[:, whole_cols], cb.at[:, cols]),
        )
        for copy in pair:
            copy.start()
        arriving.append(pair)
    mask = columns(tab_ref[MASK : MASK + count, :], CHUNK)

    def load(cols, source, halo):
        ext_ref[8 : 8 + count, cols] = source.astype(F32)
        ext_ref[8 - CONV + 1 : 8, cols] = halo.astype(F32)
        return taps_of(ext_ref, cols, count, mask)

    if lead:
        first.wait()
        act, slope = activate(load(at(SPAN, BC), bx[...], bch_ref[...]), at(0), bcw_ref, bcb_ref)
        bca_ref[...] = act
        bcs_ref[...] = slope
        turned = rows(act[:, :STATE].T, act[:, STATE:].T)
        turned_ref[...] = turned
        scores_ref[...] = scores_of(act)
    else:
        turned = turned_ref[...]
    keys, reads = halves(turned[:STATE, :]), halves(turned[STATE:, :])
    keys_both, reads_both = lanes(*keys), lanes(*reads)
    entry, leave = tab_ref[ENTRY : ENTRY + count, :], tab_ref[LEAVE : LEAVE + count, :]
    first_core = flag_ref[0] == 0
    for stream in range(STREAMS):
        for copy in arriving[stream]:
            copy.wait()
        for start in range(stream * WIDTH, (stream + 1) * WIDTH, CHUNK):
            cols = at(start)
            head = (turn * SPAN + start) // HEAD_DIM
            taps = load(cols, xb[:, cols], halo_ref[:, cols])
            act, _ = activate(taps, cols, w_ref, b_ref)
            e = by_head(entry, head, PER)
            lx_high, lx_low = halves(act * by_head(leave, head, PER))
            ey_high, ey_low = halves(cb[:, cols].astype(F32) * e)
            state = mm(keys_both, rows(lx_high, lx_high)) + mm(keys[0], lx_low)
            adjoint = mm(reads_both, rows(ey_high, ey_high)) + mm(reads[0], ey_low)
            nb[:STATE, cols] = jnp.where(first_core, state, adjoint)
            mb[:, cols] = jnp.where(first_core, adjoint, state)
            nb[STATE:, cols] = jnp.broadcast_to(e[count - 1 : count, :], (8, CHUNK))
        cols = at(stream * WIDTH, WIDTH)
        for source, target in ((nb, send_refs[stream]), (mb, mine_refs[stream])):
            copy = go.copy(source.at[:, cols], target)
            copy.start()
            leaving.append(copy)
    for copy in leaving:
        copy.wait()


def decode(codes):
    scale = jnp.exp2(codes[STATE : STATE + 1, :].astype(F32) * (1.0 / 256.0)) * (1.0 / CODE)
    return codes[:STATE, :].astype(F32) * scale


def encode(value):
    most = jnp.max(jnp.abs(value), axis=0, keepdims=True)
    power = jnp.ceil(jnp.log2(jnp.maximum(most, 1e-30)) * 256.0)
    scale = jnp.exp2(power * (1.0 / 256.0)) * (1.0 / CODE)
    codes = jnp.floor(value * (1.0 / scale) + 0.5).astype(jnp.int32)
    tail = jnp.broadcast_to(power.astype(jnp.int32), (16, value.shape[1]))
    return rows(codes, tail).astype(I16)


def chip_kernel(lead, mine_ref, met_ref, own_ref, *refs):
    chip_ref = refs[0]
    mb, eb, ob, sem = refs[-4:]
    come = Flow(sem)
    copies = [
        come.copy(mine_ref, mb),
        come.copy(met_ref, eb),
        come.copy(own_ref.at[pl.ds(STATE, 8), :], ob),
    ]
    for copy in copies:
        copy.start()
    for copy in copies:
        copy.wait()
    for start in range(0, WIDTH, CHUNK):
        cols = at(start)
        own = ob[0:1, cols]
        value = mb[:, cols] + own * eb[:STATE, cols]
        chip_ref[:STATE, cols] = value
        chip_ref[STATE:, cols] = own * eb[STATE:, cols]
        if lead:
            refs[1][:, cols] = encode(value)


def hop_kernel(pick_ref, previous_ref, *refs):
    chip_refs, out_ref = refs[:-1], refs[-1]
    for start in range(0, WIDTH, CHUNK):
        cols = at(start)
        chip = chip_refs[0][:, cols]
        for i, ref in enumerate(chip_refs[1:]):
            chip = jnp.where(pick_ref[0] > i, ref[:, cols], chip)
        before = jnp.where(pick_ref[1] == 0, 0.0, decode(previous_ref[:, cols]))
        out_ref[:, cols] = encode(chip[:STATE, :] + chip[STATE : STATE + 1, :] * before)


def within_kernel(
    piece, x_ref, cot_ref, halo_ref, w_ref, b_ref, tab_ref, scores_ref, y_ref, dx_ref, dscores_ref, *refs
):
    xb, cb, yb, db, ext_ref, in_sems, out_sems = refs
    count = xb.shape[0]
    come, go = Flow(in_sems), Flow(out_sems)
    copies = (
        come.copy(x_ref.at[:, at(piece * WIDTH, WIDTH)], xb),
        come.copy(cot_ref.at[:, at(piece * WIDTH, WIDTH)], cb),
    )
    for copy in copies:
        copy.start()
    mask = columns(tab_ref[MASK : MASK + count, :], PAIR)
    for copy in copies:
        copy.wait()
    run = tab_ref[RUN : RUN + count, :]
    far, scores = tab_ref[FAR_AT : FAR_AT + count, :], scores_ref[...]
    left = iota((count, PAIR), 1) < HEAD_DIM
    total = jnp.zeros((count, count), F32)
    zero = jnp.zeros((count, PAIR), BF16)
    for pair in range(PIECE_HEADS // 2):
        cols = at(pair * PAIR, PAIR)
        ext_ref[8 : 8 + count, cols] = xb[:, cols].astype(F32)
        ext_ref[8 - CONV + 1 : 8, cols] = halo_ref[:, cols].astype(F32)
        act, _ = activate(taps_of(ext_ref, cols, count, mask), cols, w_ref, b_ref)
        x_high, x_low = halves(act)
        upstream = cb[:, cols]
        upstream_turned = upstream.astype(F32).T.astype(BF16)
        spread, weights = [], []
        for side in range(2):
            head = piece * PIECE_HEADS + 2 * pair + side
            row = tab_ref[ROW + head : ROW + head + 1, :]
            within = jnp.exp(run[:, head : head + 1] + row + far)
            spread.append(within)
            weights.append(lanes(*halves(within * scores)))
        out = mm(rows(*weights), rows(lanes(x_high, x_low), lanes(x_high, zero)))
        out = out[:, :PAIR] + out[:, PAIR:]
        yb[:, cols] = jnp.where(left, out[:count], out[count:])
        parts = []
        for side in range(2):
            mine = upstream_turned[side * HEAD_DIM : (side + 1) * HEAD_DIM, :]
            pushed = rows(weights[side][:, :count], weights[side][:, count:])
            parts.append(mm(lanes(mine, mine), pushed))
        db[:, cols] = rows(*parts).T
        up_left, up_right = jnp.where(left, upstream, zero), jnp.where(left, zero, upstream)
        lhs = rows(lanes(up_left, up_left), lanes(up_right, up_right))
        products = mm(lhs, lanes(x_high, x_low), ACROSS)
        total = total + spread[0] * products[:count] + spread[1] * products[count:]
    copies = (go.copy(yb, y_ref), go.copy(db, dx_ref))
    for copy in copies:
        copy.start()
    dscores_ref[...] = total
    for copy in copies:
        copy.wait()


def conv_back(dconv, taps, w, z_ref, z_cols, smask):
    count, width = dconv.shape
    z_ref[8 : 8 + count, z_cols] = dconv
    grad = jnp.zeros((count + 8, width), F32)
    for ahead in range(CONV):
        tap = CONV - 1 - ahead
        shifted = z_ref[ahead : ahead + count + 8, z_cols]
        grad = grad + w[tap : tap + 1, :] * (shifted * smask[ahead])
    sums = [jnp.sum(dconv * tap, axis=0, keepdims=True) for tap in taps]
    sums.append(jnp.sum(dconv, axis=0, keepdims=True))
    sums.append(jnp.zeros((3, width), F32))
    return grad[8:].astype(BF16), rows(grad[:8], grad[count:], *sums)


def clear_edges(z_ref, count):
    z_ref[0:8, :] = jnp.zeros((8, z_ref.shape[1]), F32)
    z_ref[8 + count : 16 + count, :] = jnp.zeros((8, z_ref.shape[1]), F32)


def finish_kernel(piece, hops, flag_ref, *refs):
    incs, exchs = refs[:hops], refs[hops : 2 * hops]
    refs = refs[2 * hops :]
    met_ref, y_ref, dx_ref, cot_ref, x_ref, halo_ref, w_ref, b_ref, tab_ref, bc_ref = refs[:10]
    out_ref, gin_ref, misc_ref, dreads_ref, dkeys_ref, scal_ref = refs[-20:-14]
    ib, hb, eb, yb, db, cb, xb, ob, gb, nb, ext_ref, z_ref, in_sems, out_sems = refs[-14:]
    count = xb.shape[0]
    come, go = Flow(in_sems), Flow(out_sems)
    base = piece * WIDTH
    place = flag_ref[1]
    choices = []
    for here, sources, buffer in ((place, incs, ib), (hops - place, exchs, hb)):
        sem = come.used
        come.used += 1
        for i, source in enumerate(sources):
            choices.append((here == i + 1, pltpu.make_async_copy(source, buffer, come.sems.at[sem])))

        @pl.when(here == 0)
        def _():
            buffer[...] = jnp.zeros(buffer.shape, I16)

    for chosen, copy in choices:
        pl.when(chosen)(copy.start)
    arriving, leaving = [], []
    for start, width in ((0, CHUNK), (CHUNK, WIDTH - CHUNK)):
        cols = at(start, width)
        whole_cols = at(base + start, width)
        group = [
            come.copy(met_ref.at[:, cols], eb.at[:, cols]),
            come.copy(y_ref.at[:, cols], yb.at[:, cols]),
            come.copy(dx_ref.at[:, cols], db.at[:, cols]),
            come.copy(cot_ref.at[:, whole_cols], cb.at[:, cols]),
            come.copy(x_ref.at[:, whole_cols], xb.at[:, cols]),
        ]
        for copy in group:
            copy.start()
        arriving.append(group)
    clear_edges(z_ref, count)
    keys, reads = halves(bc_ref[:, :STATE]), halves(bc_ref[:, STATE:])
    keys_both, reads_both = lanes(*keys), lanes(*reads)
    entry, leave = tab_ref[ENTRY : ENTRY + count, :], tab_ref[LEAVE : LEAVE + count, :]
    skip = tab_ref[SKIP : SKIP + 1, :]
    first_core = flag_ref[0] == 0
    mask = columns(tab_ref[MASK : MASK + count, :], CHUNK)
    smask = columns(tab_ref[SMASK : SMASK + count + 8, :], CHUNK)
    dreads = jnp.zeros((count, STATE), F32)
    dkeys = jnp.zeros((count, STATE), F32)
    sums = jnp.zeros((4 * count + 16, 128), F32)
    for chosen, copy in choices:
        pl.when(chosen)(copy.wait)
    for start in range(0, WIDTH, CHUNK):
        cols = at(start)
        head = (base + start) // HEAD_DIM
        if start <= CHUNK:
            for copy in arriving[start // CHUNK]:
                copy.wait()
        inc, exch = decode(ib[:, cols]), decode(hb[:, cols])
        mine = eb[STATE : STATE + 1, cols] * inc + eb[:STATE, cols]
        state = jnp.where(first_core, exch, mine)
        adjoint = jnp.where(first_core, mine, exch)
        s_high, s_low = halves(state)
        a_high, a_low = halves(adjoint)
        e, leaves = by_head(entry, head, PER), by_head(leave, head, PER)
        ext_ref[8 : 8 + count, cols] = xb[:, cols].astype(F32)
        ext_ref[8 - CONV + 1 : 8, cols] = halo_ref[:, cols].astype(F32)
        taps = taps_of(ext_ref, cols, count, mask)
        act, slope = activate(taps, cols, w_ref, b_ref)
        up = cb[:, cols].astype(F32)
        carried = mm(reads_both, rows(s_high, s_high)) + mm(reads[0], s_low)
        y = yb[:, cols] + e * carried
        back = mm(keys_both, rows(a_high, a_high)) + mm(keys[0], a_low)
        back = leaves * back
        dx = db[:, cols] + back
        gain = by_head(skip, head, PER)
        ob[:, cols] = (y + gain * act).astype(BF16)
        ey_high, ey_low = halves(up * e)
        lx_high, lx_low = halves(act * leaves)
        dreads = dreads + mm(lanes(ey_high, ey_high, ey_low), lanes(s_high, s_low, s_high), ACROSS)
        dkeys = dkeys + mm(lanes(lx_high, lx_high, lx_low), lanes(a_high, a_low, a_high), ACROSS)
        through = e[count - 1 : count, :]
        end = jnp.sum(act * back, axis=0, keepdims=True)
        end = end + through * jnp.sum(state * adjoint, axis=0, keepdims=True)
        direct = jnp.sum(up * act, axis=0, keepdims=True)
        received = act * dx
        small = halves(rows(end, direct, jnp.zeros((6, CHUNK), F32)))
        stack = halves(up * y - received) + halves(received)
        pick = (iota((CHUNK, 128), 1) == head + iota((CHUNK, 128), 0) // HEAD_DIM).astype(BF16)
        sums = sums + mm(rows(*stack, rows(*small)), pick)
        dconv = (dx + gain * up) * slope
        gb[:, cols], nb[:, cols] = conv_back(dconv, taps, w_ref[:, cols], z_ref, cols, smask)
    for source, target in ((ob, out_ref), (gb, gin_ref), (nb, misc_ref)):
        copy = go.copy(source, target.at[:, at(base, WIDTH)])
        copy.start()
        leaving.append(copy)
    dreads_ref[...] = dreads
    dkeys_ref[...] = dkeys
    drun = sums[:count] + sums[count : 2 * count]
    received = sums[2 * count : 3 * count] + sums[3 * count : 4 * count]
    small = sums[4 * count : 4 * count + 8] + sums[4 * count + 8 :]
    drun = drun + jnp.where(iota((count, 128), 0) == count - 1, small[0:1, :], 0.0)
    later = (iota((count, count), 1) >= iota((count, count), 0)).astype(F32)
    ddecay = jnp.dot(later, drun, precision=EXACT, preferred_element_type=F32)
    pull, rate = tab_ref[PULL : PULL + count, :], tab_ref[RATE : RATE + count, :]
    ddtb = jnp.sum(received * pull + ddecay * rate, axis=0, keepdims=True)
    dalog = jnp.sum(ddecay * tab_ref[DECAY : DECAY + count, :], axis=0, keepdims=True)
    scal_ref[...] = rows(ddtb, dalog, small[1:2, :], jnp.zeros((5, 128), F32))
    for copy in leaving:
        copy.wait()


def final_kernel(x_ref, halo_ref, w_ref, tab_ref, bc_ref, slope_ref, *refs):
    gin_ref, misc_ref, ext_ref, z_ref = refs[-4:]
    parts = refs[: 4 * PIECES]
    count = x_ref.shape[0]
    ext_ref[8 : 8 + count, :] = x_ref[...].astype(F32)
    ext_ref[8 - CONV + 1 : 8, :] = halo_ref[...].astype(F32)
    clear_edges(z_ref, count)
    total = []
    for kind in range(4):
        value = parts[kind * PIECES][...]
        for piece in range(1, PIECES):
            value = value + parts[kind * PIECES + piece][...]
        total.append(value)
    dreads, dkeys, dscores, scal = total
    keys, reads = bc_ref[:, :STATE], bc_ref[:, STATE:]
    dreads = dreads + jnp.dot(dscores, keys, precision=EXACT, preferred_element_type=F32)
    dkeys = dkeys + jnp.dot(dscores.T, reads, precision=EXACT, preferred_element_type=F32)
    cols = slice(0, BC)
    dconv = lanes(dkeys, dreads) * slope_ref[...]
    taps = taps_of(ext_ref, cols, count, columns(tab_ref[MASK : MASK + count, :], BC))
    smask = columns(tab_ref[SMASK : SMASK + count + 8, :], BC)
    gin_ref[...], misc = conv_back(dconv, taps, w_ref[...], z_ref, cols, smask)
    misc_ref[...] = misc
    misc_ref[16 + CONV + 1 : 24, :128] = scal[:3, :]


def cost(us):
    return pl.CostEstimate(flops=int(us * 1.1e9), bytes_accessed=1000, transcendentals=0)


def whole(shape):
    return pl.BlockSpec(shape, lambda *_: (0,) * len(shape))


def part(shape, *index):
    return pl.BlockSpec(shape, lambda *_: index)


def full(*arrays):
    return [whole(a.shape) for a in arrays]


def call(kernel, ins, specs, outs, out_specs, scratch=(), aliases=None, us=1.0):
    return pl.pallas_call(
        kernel,
        grid=(1,),
        in_specs=specs,
        out_specs=out_specs,
        out_shape=[jax.ShapeDtypeStruct(shape, dtype) for shape, dtype in outs],
        scratch_shapes=list(scratch),
        input_output_aliases=aliases or {},
        compiler_params=pltpu.CompilerParams(vmem_limit_bytes=VMEM_LIMIT),
        cost_estimate=cost(us),
    )(*ins)


def vmem(rows_, cols, dtype=F32):
    return pltpu.VMEM((rows_, cols), dtype)


def sems(count):
    return pltpu.SemaphoreType.DMA((count,))


def permute(value, axis, target):
    size = lax.axis_size(axis)
    return lax.ppermute(value, axis, [(i, target(i)) for i in range(size)])


def other_core(value):
    return permute(value, "seq", lambda i: i ^ 1)


def along(size):
    def target(i):
        if i % 2 == 1:
            return i + 2 if i + 2 < size else i - 1
        return i - 2 if i >= 2 else i + 1

    return target


def xor_sum(value, axis, low):
    size = lax.axis_size(axis)
    bit = low
    while bit < size:
        if 2 * bit < size:
            one = permute(value, axis, lambda i: i ^ bit)
            two = permute(value, axis, lambda i: i ^ (2 * bit))
            three = permute(value, axis, lambda i: i ^ (3 * bit))
            value = (value + one) + (two + three)
            bit *= 4
        else:
            value = value + permute(value, axis, lambda i: i ^ bit)
            bit *= 2
    return value


def chip_of(lead, mine, met, own):
    state = (STATE + 8, WIDTH)
    payload = (STATE + 16, WIDTH)
    outs = [(state, F32)] + [(payload, I16)] * lead
    return call(
        functools.partial(chip_kernel, lead),
        (mine, met, own),
        [HBM] * 3,
        outs,
        [whole(s) for s, _ in outs],
        [vmem(STATE, WIDTH), vmem(*state), vmem(8, WIDTH), sems(3)],
        us=1.5,
    )


def hop(pick, previous, chips):
    payload = (STATE + 16, WIDTH)
    return call(
        hop_kernel,
        (pick, previous, *chips),
        [SMEM, *full(previous, *chips)],
        [(payload, I16)],
        [whole(payload)],
        us=0.8,
    )[0]


def on_device(
    conv_input, doc_start, conv_weight, conv_bias, dt_raw, dt_bias, a_log, skip_gain, cotangent
):
    count = conv_input.shape[0]
    size = lax.axis_size("seq")
    index = lax.axis_index("seq")
    core = lax.rem(index, 2)
    chip = lax.div(index, 2)
    hops = size // 2 - 1
    place = jnp.where(core == 1, chip, hops - chip)
    flag = jnp.stack([core, place]).astype(jnp.int32)
    docs = doc_start[None, :]
    edge = part((16, CH), count // 16 - 1, 0)

    tail_out = call(
        tail_kernel, (conv_input, docs), [edge, whole(docs.shape)],
        [((CONV - 1, CH), BF16)], [whole((CONV - 1, CH))],
    )[0]
    halo = lax.ppermute(tail_out, "seq", [(i, i + 1) for i in range(size - 1)])

    bias = conv_bias[None, :]
    prep_in = (docs, dt_raw.T, dt_bias[None, :], a_log[None, :], skip_gain[None, :])
    table = (TABLE, 128)
    tab = call(prep_kernel, prep_in, full(*prep_in), [(table, F32)], [whole(table)])[0]

    square = (count, count)
    payload = (STATE + 16, WIDTH)
    shape = (count, WIDTH)
    chips, sent, mets = [], [], []
    given = tab
    for turn in range(TURNS):
        lead = turn == 0
        here = [part((height, SPAN), 0, turn) for height in (CONV - 1, CONV, 1)]
        ins = [flag, conv_input, halo, conv_weight, bias, cotangent, given]
        specs = [SMEM, HBM, *here, HBM, whole(table)]
        outs = [(STATE + 8, WIDTH)] * STREAMS + [(STATE, WIDTH)] * STREAMS
        out_specs = [HBM] * len(outs)
        if lead:
            ins += [halo, conv_weight, bias]
            specs += [part((height, BC), 0, BC_AT) for height in (CONV - 1, CONV, 1)]
            bc_out = [(count, BC), (count, BC), (BC, count), square]
            outs += bc_out
            out_specs += [whole(s) for s in bc_out]
        else:
            ins.append(turned)
            specs.append(whole(turned.shape))
        got = call(
            functools.partial(local_kernel, turn),
            ins,
            specs,
            [(s, F32) for s in outs],
            out_specs,
            [
                vmem(count, SPAN, BF16), vmem(count, SPAN, BF16), vmem(STATE + 8, SPAN),
                vmem(STATE, SPAN), vmem(count + 8, SPAN + BC), vmem(count, BC, BF16),
                sems(2 * STREAMS + 1), sems(2 * STREAMS),
            ],
            us=5.0,
        )
        if lead:
            bc_act, bc_slope, turned, scores = got[2 * STREAMS :]
        for stream in range(STREAMS):
            send, mine = got[stream], got[STREAMS + stream]
            met = other_core(send)
            mets.append(met)
            chip, *first = chip_of(lead, mine, met, send)
            chips.append(chip)
            sent += first

    withins = []
    for j in range(PIECES):
        here = [part((height, WIDTH), 0, j) for height in (CONV - 1, CONV, 1)]
        withins.append(
            call(
                functools.partial(within_kernel, j),
                (conv_input, cotangent, halo, conv_weight, bias, tab, scores),
                [HBM, HBM, *here, *full(tab, scores)],
                [(shape, F32), (shape, F32), (square, F32)],
                [HBM, HBM, whole(square)],
                [
                    vmem(*shape, BF16), vmem(*shape, BF16), vmem(*shape), vmem(*shape),
                    vmem(count + 8, WIDTH), sems(2), sems(2),
                ],
                us=2.0,
            )
        )

    dreads, dkeys, scals = [None] * PIECES, [None] * PIECES, [None] * PIECES
    shared_out = [((count, INNER), BF16), ((count, CH), BF16), ((24, CH), F32)]
    small_out = [((count, STATE), F32), ((count, STATE), F32), ((8, 128), F32)]

    def finish(j, shared):
        turn, stream = j // STREAMS, j % STREAMS
        here = [part((height, WIDTH), 0, j) for height in (CONV - 1, CONV, 1)]
        y, dx, _ = withins[j]
        ins = [flag, *received[stream][turn : turn + hops], *swapped[stream][turn : turn + hops]]
        specs = [SMEM] + [ANY] * (2 * hops)
        ins += [mets[j], y, dx, cotangent, conv_input, halo, conv_weight, bias, tab, bc_act]
        specs += [HBM] * 5 + here + full(tab, bc_act)
        aliases = None
        if shared is not None:
            aliases = {len(ins) + i: i for i in range(3)}
            ins += shared
            specs += [HBM] * 3
        *shared, dreads[j], dkeys[j], scals[j] = call(
            functools.partial(finish_kernel, j, hops),
            ins,
            specs,
            shared_out + small_out,
            [HBM] * 3 + [whole(s) for s, _ in small_out],
            [
                vmem(*payload, I16), vmem(*payload, I16), vmem(STATE + 8, WIDTH),
                vmem(*shape), vmem(*shape), vmem(*shape, BF16), vmem(*shape, BF16),
                vmem(*shape, BF16), vmem(*shape, BF16), vmem(24, WIDTH),
                vmem(count + 8, WIDTH), vmem(count + 16, WIDTH), sems(2 + 10), sems(3),
            ],
            aliases,
            us=5.0,
        )
        return shared

    received = [[] for _ in range(STREAMS)]
    swapped = [[] for _ in range(STREAMS)]
    shared = None
    turns = TURNS + hops - 1
    for turn in range(turns):
        if turn:
            piece = jnp.clip(turn - place, 0, TURNS - 1)
            pick = jnp.stack([piece, place]).astype(jnp.int32)
            sent = [
                hop(pick, received[stream][-1], chips[stream::STREAMS]) for stream in range(STREAMS)
            ]
        arrived = [permute(value, "seq", along(size)) for value in sent]
        for stream in range(STREAMS):
            got = arrived[stream]
            if turn == turns - 1:
                shared = finish(stream, shared)
                got, shared = lax.optimization_barrier((got, shared))
            received[stream].append(got)
            swapped[stream].append(other_core(got))
    for j in range(STREAMS, PIECES):
        shared = finish(j, shared)
    output, gin, misc = shared

    dscores = [group[2] for group in withins]
    small = (tab, bc_act, bc_slope, *dreads, *dkeys, *dscores, *scals)
    ins = (conv_input, halo, conv_weight) + small + (gin, misc)
    bc_common = [part((count, BC), 0, BC_AT), part((CONV - 1, BC), 0, BC_AT), part((CONV, BC), 0, BC_AT)]
    gin, misc = call(
        final_kernel,
        ins,
        bc_common + full(*small) + [ANY] * 2,
        shared_out[1:],
        [part((count, BC), 0, BC_AT), part((24, BC), 0, BC_AT)],
        [vmem(count + 8, BC), vmem(count + 16, BC)],
        {len(ins) - 2: 0, len(ins) - 1: 1},
    )

    returned = lax.ppermute(
        misc[8 - CONV + 1 : 8], "seq", [(i, i - 1) for i in range(1, size)]
    )
    grad_input = call(
        edge_kernel,
        (gin, misc, returned, docs),
        [edge, part((8, CH), 1, 0), *full(returned, docs)],
        [((count, CH), BF16)],
        [edge],
        aliases={0: 0},
    )[0]

    half = CH // 2
    lower, upper = misc[16:24, :half], misc[16:24, half:]
    first = core == 0
    value = jnp.where(first, lower, upper)
    value = value + other_core(jnp.where(first, upper, lower))
    value = xor_sum(value, "dp", 1)
    value = xor_sum(value, "seq", 2)
    value = value * float(lax.axis_size("dp") * size * count) ** (-0.5)
    other = other_core(value)
    lower = jnp.where(first, value, other)
    upper = jnp.where(first, other, value)
    summed = jnp.concatenate([lower, upper], axis=1)
    scal = summed[CONV + 1 :, INNER : INNER + HEADS]
    return (output, grad_input, summed[:CONV], summed[CONV], scal[0], scal[1], scal[2])


def solution(mesh):
    return jax.shard_map(
        on_device,
        mesh=mesh,
        in_specs=(
            P(("dp", "seq"), None),
            P(("dp", "seq")),
            P(),
            P(),
            P(("dp", "seq"), None),
            P(),
            P(),
            P(),
            P(("dp", "seq"), None),
        ),
        out_specs=(P(("dp", "seq"), None), P(("dp", "seq"), None), P(), P(), P(), P(), P()),
        check_vma=False,
    )
```

```python
import functools

import jax
import jax.numpy as jnp
from jax import lax
from jax.experimental import pallas as pl
from jax.experimental.pallas import tpu as pltpu
from jax.sharding import PartitionSpec as P

HEADS = 80
HEAD_DIM = 64
STATE = 128
CONV = 4
INNER = 5120
CH = 5376

STREAMS = 2
TURNS = 2
PIECES = STREAMS * TURNS
PIECE_HEADS = HEADS // PIECES
WIDTH = PIECE_HEADS * HEAD_DIM
SPAN = STREAMS * WIDTH
PAIR = 2 * HEAD_DIM
CHUNK = 256
BC = 2 * STATE
BC_AT = INNER // BC
FAR = -1e30
STATES, SMALL = 0, 256
BC_ACT, BC_SLOPE, SCORES, SMALLS = 0, 256, 512, 640
WORK_ROWS = 3328
CODE = 32766.0
THIRD = CH // 3
PER = CHUNK // HEAD_DIM

F32 = jnp.float32
BF16 = jnp.bfloat16
I16 = jnp.int16
EXACT = lax.Precision.HIGHEST
ACROSS = ((1,), (1,))
ANY = pl.BlockSpec(memory_space=pl.ANY)
HBM = pl.BlockSpec(memory_space=pltpu.HBM)
VMEM_LIMIT = 24 * 1024 * 1024

MASK, ENTRY, LEAVE, PULL, RATE, DECAY, RUN, FAR_AT, ROW, SMASK = range(0, 1280, 128)
SKIP = ROW + HEADS
TABLE = SMASK + 136


def iota(shape, dim):
    return lax.broadcasted_iota(jnp.int32, shape, dim)


def mm(a, b, contract=((1,), (0,))):
    return lax.dot_general(a, b, (contract, ((), ())), preferred_element_type=F32)


def halves(value):
    high = value.astype(BF16)
    return high, (value - high.astype(F32)).astype(BF16)


def lanes(*parts):
    return jnp.concatenate(parts, axis=1)


def rows(*parts):
    return jnp.concatenate(parts, axis=0)


def by_head(table, first, count):
    out = []
    for head in range(first, first + count, 2):
        shape = (table.shape[0], PAIR)
        left = jnp.broadcast_to(table[:, head : head + 1], shape)
        right = jnp.broadcast_to(table[:, head + 1 : head + 2], shape)
        out.append(jnp.where(iota(shape, 1) < HEAD_DIM, left, right))
    return lanes(*out)


def taps_of(ext_ref, cols, count, mask):
    taps = []
    for tap in range(CONV):
        back = CONV - 1 - tap
        value = ext_ref[8 - back : 8 - back + count, cols]
        taps.append(value if back == 0 else value * mask[back])
    return taps


def columns(table, width):
    shape = (table.shape[0], width)
    return [jnp.broadcast_to(table[:, i : i + 1], shape) for i in range(CONV)]


def activate(taps, cols, w_ref, b_ref):
    v = b_ref[:, cols] + w_ref[CONV - 1 : CONV, cols] * taps[CONV - 1]
    for tap in range(CONV - 2, -1, -1):
        v = v + w_ref[tap : tap + 1, cols] * taps[tap]
    gate = 1.0 / (1.0 + jnp.exp(-v))
    return v * gate, gate * (1.0 + v * (1.0 - gate))


class Flow:
    def __init__(self, sems):
        self.sems = sems
        self.used = 0

    def copy(self, source, target):
        made = pltpu.make_async_copy(source, target, self.sems.at[self.used])
        self.used += 1
        return made


def position(hops):
    index = lax.axis_index("seq")
    core = lax.rem(index, 2)
    chip = lax.div(index, 2)
    return core, jnp.where(core == 1, chip, hops - chip)


def at(first, width=CHUNK):
    return slice(first, first + width)


def tail_kernel(x_ref, doc_ref, out_ref):
    count = doc_ref.shape[1]
    edge = x_ref.shape[0] - CONV + 1
    cut = jnp.zeros((1, 1), F32)
    for back in range(CONV - 1):
        row = edge + CONV - 2 - back
        if back:
            cut = cut + doc_ref[:, count - back : count - back + 1].astype(F32)
        keep = (cut == 0.0).astype(F32)
        value = x_ref[row : row + 1, :].astype(F32) * keep
        out_ref[CONV - 2 - back : CONV - 1 - back, :] = value.astype(BF16)


def edge_kernel(gin_ref, misc_ref, back_ref, doc_ref, out_ref):
    count = doc_ref.shape[1]
    size = gin_ref.shape[0]
    cut = jnp.zeros((1, 1), F32)
    keeps = []
    for back in range(CONV - 1):
        if back:
            cut = cut + doc_ref[:, count - back : count - back + 1].astype(F32)
        keeps.insert(0, (cut == 0.0).astype(F32))
    place = iota((8, 1), 0)
    value = misc_ref[...]
    for i in range(CONV - 1):
        row = 8 - CONV + 1 + i
        value = value + jnp.where(place == row, back_ref[i : i + 1, :] * keeps[i], 0.0)
    out_ref[...] = gin_ref[...]
    out_ref[size - 8 :, :] = value.astype(BF16)


def prep_kernel(doc_ref, raw_ref, dtb_ref, alog_ref, skip_ref, tab_ref):
    count = raw_ref.shape[1]
    resets = doc_ref[...].astype(F32)
    t, s = iota((count, count), 0), iota((count, count), 1)

    def total(keep, shape):
        return jnp.sum(jnp.where(keep, jnp.broadcast_to(resets, shape), 0.0), axis=1, keepdims=True)

    square = (count, count)
    lane = iota((count, 128), 1)
    table = jnp.ones((count, 128), F32)
    for back in range(1, CONV):
        fits = (total((s <= t) & (s > t - back), square) == 0.0).astype(F32)
        table = jnp.where(lane == back, fits, table)
    tab_ref[MASK : MASK + count, :] = table
    wide = (count + 8, count)
    at, s_wide = iota(wide, 0) - 8, iota(wide, 1)
    lane, place = iota((count + 8, 128), 1), iota((count + 8, 128), 0) - 8
    table = jnp.zeros((count + 8, 128), F32)
    for ahead in range(CONV):
        fits = (total((s_wide > at) & (s_wide <= at + ahead), wide) == 0.0).astype(F32)
        fits = jnp.where((place + ahead >= 0) & (place + ahead < count), fits, 0.0)
        table = jnp.where(lane == ahead, fits, table)
    tab_ref[SMASK : SMASK + count + 8, :] = table
    segment = total(s <= t, square)
    reset_col = total(s == t, square)
    segment_row = jnp.sum(
        jnp.where(t <= s, jnp.broadcast_to(reset_col, square), 0.0), axis=0, keepdims=True
    )
    causal = (s <= t) & (segment == segment_row)
    tab_ref[FAR_AT : FAR_AT + count, :] = jnp.where(causal, 0.0, FAR)
    raw = rows(raw_ref[...], jnp.zeros((128 - HEADS, count), F32)).T[:, :HEADS]
    v = raw + dtb_ref[...]
    dt = jnp.maximum(v, 0.0) + jnp.log1p(jnp.exp(-jnp.abs(v)))
    rate = -jnp.exp(alog_ref[...])
    decay = rate * dt
    run = jnp.dot((s <= t).astype(F32), decay, precision=EXACT, preferred_element_type=F32)
    end = run[count - 1 : count, :]
    last = segment == segment[count - 1 : count, :]
    gate = 1.0 / (1.0 + jnp.exp(-v))
    fill = jnp.zeros((count, 128 - HEADS), F32)

    def put(where, value):
        tab_ref[where : where + count, :] = lanes(value, fill)

    put(ENTRY, jnp.where(segment == 0.0, jnp.exp(run), 0.0))
    put(LEAVE, jnp.where(last, jnp.exp(end - run) * dt, 0.0))
    put(PULL, gate / dt)
    put(RATE, rate * gate)
    put(DECAY, decay)
    put(RUN, run)
    tab_ref[ROW : ROW + 128, :] = lanes(jnp.log(dt) - run, fill).T
    tab_ref[SKIP : SKIP + 1, :] = lanes(skip_ref[...], fill[:1])


def scores_of(act):
    keys, reads = act[:, :STATE], act[:, STATE:]
    return lax.dot_general(
        reads, keys, (ACROSS, ((), ())), precision=EXACT, preferred_element_type=F32
    )


def local_kernel(x_ref, halo_ref, w_ref, b_ref, cot_ref, tab_ref, *refs):
    send_refs = refs[:PIECES]
    work_ref = refs[PIECES]
    xb, cb, nb, mb, sb, ext_ref, in_sems, out_sems = refs[-8:]
    count = xb.shape[0]
    come, go = Flow(in_sems), Flow(out_sems)
    first = come.copy(x_ref.at[:, at(INNER, BC)], xb.at[:, at(INNER, BC)])
    first.start()
    arriving, leaving = [], []
    for piece in range(PIECES):
        cols = at(piece * WIDTH, WIDTH)
        pair = (
            come.copy(x_ref.at[:, cols], xb.at[:, cols]),
            come.copy(cot_ref.at[:, cols], cb.at[:, cols]),
        )
        for copy in pair:
            copy.start()
        arriving.append(pair)
    mask = columns(tab_ref[MASK : MASK + count, :], CHUNK)

    def act_of(cols):
        ext_ref[8 : 8 + count, cols] = xb[:, cols].astype(F32)
        ext_ref[8 - CONV + 1 : 8, cols] = halo_ref[:, cols].astype(F32)
        return activate(taps_of(ext_ref, cols, count, mask), cols, w_ref, b_ref)

    first.wait()
    act, slope = act_of(at(INNER, BC))
    sb[:, at(BC_ACT)] = act
    sb[:, at(BC_SLOPE)] = slope
    sb[:, at(SCORES, 128)] = scores_of(act)
    copy = go.copy(sb, work_ref.at[at(SMALL, count), at(0, SMALLS)])
    copy.start()
    leaving.append(copy)
    turned = rows(act[:, :STATE].T, act[:, STATE:].T)
    keys, reads = halves(turned[:STATE, :]), halves(turned[STATE:, :])
    keys_both, reads_both = lanes(*keys), lanes(*reads)
    entry, leave = tab_ref[ENTRY : ENTRY + count, :], tab_ref[LEAVE : LEAVE + count, :]
    first_core = lax.rem(lax.axis_index("seq"), 2) == 0
    for piece in range(PIECES):
        for copy in arriving[piece]:
            copy.wait()
        for start in range(piece * WIDTH, (piece + 1) * WIDTH, CHUNK):
            cols = at(start)
            head = start // HEAD_DIM
            act, _ = act_of(cols)
            e = by_head(entry, head, PER)
            lx_high, lx_low = halves(act * by_head(leave, head, PER))
            ey_high, ey_low = halves(cb[:, cols].astype(F32) * e)
            state = mm(keys_both, rows(lx_high, lx_high)) + mm(keys[0], lx_low)
            adjoint = mm(reads_both, rows(ey_high, ey_high)) + mm(reads[0], ey_low)
            nb[:STATE, cols] = jnp.where(first_core, state, adjoint)
            mb[:STATE, cols] = jnp.where(first_core, adjoint, state)
            through = jnp.broadcast_to(e[count - 1 : count, :], (8, CHUNK))
            nb[STATE:, cols] = through
            mb[STATE:, cols] = through
        cols = at(piece * WIDTH, WIDTH)
        for source, target in ((nb, send_refs[piece]), (mb, work_ref.at[at(STATES, STATE + 8), cols])):
            copy = go.copy(source.at[:, cols], target)
            copy.start()
            leaving.append(copy)
    for copy in leaving:
        copy.wait()


def decode(codes):
    scale = jnp.exp2(codes[STATE : STATE + 1, :].astype(F32) * (1.0 / 256.0)) * (1.0 / CODE)
    return codes[:STATE, :].astype(F32) * scale


def encode(value):
    most = jnp.max(jnp.abs(value), axis=0, keepdims=True)
    power = jnp.ceil(jnp.log2(jnp.maximum(most, 1e-30)) * 256.0)
    scale = jnp.exp2(power * (1.0 / 256.0)) * (1.0 / CODE)
    codes = jnp.floor(value * (1.0 / scale) + 0.5).astype(jnp.int32)
    tail = jnp.broadcast_to(power.astype(jnp.int32), (16, value.shape[1]))
    return rows(codes, tail).astype(I16)


def chip_kernel(piece, work_ref, met_ref, *refs):
    chip_ref = refs[0]
    mb, eb, sem = refs[-3:]
    come = Flow(sem)
    mine = work_ref.at[at(STATES, STATE + 8), at(piece * WIDTH, WIDTH)]
    copies = [come.copy(mine, mb), come.copy(met_ref, eb)]
    for copy in copies:
        copy.start()
    for copy in copies:
        copy.wait()
    for start in range(0, WIDTH, CHUNK):
        cols = at(start)
        own = mb[STATE : STATE + 1, cols]
        value = mb[:STATE, cols] + own * eb[:STATE, cols]
        chip_ref[:STATE, cols] = value
        chip_ref[STATE:, cols] = own * eb[STATE:, cols]
        if piece < STREAMS:
            refs[1][:, cols] = encode(value)


def hop_kernel(turn, hops, previous_ref, *refs):
    chip_refs, out_ref = refs[:-1], refs[-1]
    _, place = position(hops)
    for start in range(0, WIDTH, CHUNK):
        cols = at(start)
        chip = chip_refs[0][:, cols]
        for i, ref in enumerate(chip_refs[1:]):
            chip = jnp.where(turn - place > i, ref[:, cols], chip)
        before = jnp.where(place == 0, 0.0, decode(previous_ref[:, cols]))
        out_ref[:, cols] = encode(chip[:STATE, :] + chip[STATE : STATE + 1, :] * before)


def within_kernel(
    piece, x_ref, cot_ref, work_ref, halo_ref, w_ref, b_ref, tab_ref, y_ref, dx_ref, dscores_ref, *refs
):
    xb, cb, sb, yb, db, ext_ref, in_sems, out_sems = refs
    count = xb.shape[0]
    come, go = Flow(in_sems), Flow(out_sems)
    copies = (
        come.copy(x_ref.at[:, at(piece * WIDTH, WIDTH)], xb),
        come.copy(cot_ref.at[:, at(piece * WIDTH, WIDTH)], cb),
        come.copy(work_ref.at[at(SMALL, count), at(SCORES, count)], sb),
    )
    for copy in copies:
        copy.start()
    mask = columns(tab_ref[MASK : MASK + count, :], PAIR)
    for copy in copies:
        copy.wait()
    run = tab_ref[RUN : RUN + count, :]
    far, scores = tab_ref[FAR_AT : FAR_AT + count, :], sb[...]
    left = iota((count, PAIR), 1) < HEAD_DIM
    total = jnp.zeros((count, count), F32)
    zero = jnp.zeros((count, PAIR), BF16)
    for pair in range(PIECE_HEADS // 2):
        cols = at(pair * PAIR, PAIR)
        ext_ref[8 : 8 + count, cols] = xb[:, cols].astype(F32)
        ext_ref[8 - CONV + 1 : 8, cols] = halo_ref[:, cols].astype(F32)
        act, _ = activate(taps_of(ext_ref, cols, count, mask), cols, w_ref, b_ref)
        x_high, x_low = halves(act)
        upstream = cb[:, cols]
        upstream_turned = upstream.astype(F32).T.astype(BF16)
        spread, weights = [], []
        for side in range(2):
            head = piece * PIECE_HEADS + 2 * pair + side
            row = tab_ref[ROW + head : ROW + head + 1, :]
            within = jnp.exp(run[:, head : head + 1] + row + far)
            spread.append(within)
            weights.append(lanes(*halves(within * scores)))
        out = mm(rows(*weights), rows(lanes(x_high, x_low), lanes(x_high, zero)))
        out = out[:, :PAIR] + out[:, PAIR:]
        yb[:, cols] = jnp.where(left, out[:count], out[count:])
        parts = []
        for side in range(2):
            mine = upstream_turned[side * HEAD_DIM : (side + 1) * HEAD_DIM, :]
            pushed = rows(weights[side][:, :count], weights[side][:, count:])
            parts.append(mm(lanes(mine, mine), pushed))
        db[:, cols] = rows(*parts).T
        up_left, up_right = jnp.where(left, upstream, zero), jnp.where(left, zero, upstream)
        lhs = rows(lanes(up_left, up_left), lanes(up_right, up_right))
        products = mm(lhs, lanes(x_high, x_low), ACROSS)
        total = total + spread[0] * products[:count] + spread[1] * products[count:]
    copies = (go.copy(yb, y_ref), go.copy(db, dx_ref))
    for copy in copies:
        copy.start()
    dscores_ref[...] = total
    for copy in copies:
        copy.wait()


def conv_back(dconv, taps, w, z_ref, z_cols, smask):
    count, width = dconv.shape
    z_ref[8 : 8 + count, z_cols] = dconv
    grad = jnp.zeros((count + 8, width), F32)
    for ahead in range(CONV):
        tap = CONV - 1 - ahead
        shifted = z_ref[ahead : ahead + count + 8, z_cols]
        grad = grad + w[tap : tap + 1, :] * (shifted * smask[ahead])
    sums = [jnp.sum(dconv * tap, axis=0, keepdims=True) for tap in taps]
    sums.append(jnp.sum(dconv, axis=0, keepdims=True))
    sums.append(jnp.zeros((3, width), F32))
    return grad[8:].astype(BF16), rows(grad[:8], grad[count:], *sums)


def clear_edges(z_ref, count):
    z_ref[0:8, :] = jnp.zeros((8, z_ref.shape[1]), F32)
    z_ref[8 + count : 16 + count, :] = jnp.zeros((8, z_ref.shape[1]), F32)


def finish_kernel(piece, hops, *refs):
    incs, exchs = refs[:hops], refs[hops : 2 * hops]
    refs = refs[2 * hops :]
    met_ref, work_ref, y_ref, dx_ref, cot_ref, x_ref, halo_ref, w_ref, b_ref, tab_ref = refs[:10]
    out_ref, gin_ref, misc_ref, dreads_ref, dkeys_ref, scal_ref = refs[-21:-15]
    ib, hb, eb, bc, yb, db, cb, xb, ob, gb, nb, ext_ref, z_ref, in_sems, out_sems = refs[-15:]
    count = xb.shape[0]
    come, go = Flow(in_sems), Flow(out_sems)
    base = piece * WIDTH
    core, place = position(hops)
    first = come.copy(work_ref.at[at(SMALL, count), at(BC_ACT)], bc)
    first.start()
    choices = []
    for here, sources, buffer in ((place, incs, ib), (hops - place, exchs, hb)):
        sem = come.used
        come.used += 1
        for i, source in enumerate(sources):
            choices.append((here == i + 1, pltpu.make_async_copy(source, buffer, come.sems.at[sem])))

        @pl.when(here == 0)
        def _():
            buffer[...] = jnp.zeros(buffer.shape, I16)

    for chosen, copy in choices:
        pl.when(chosen)(copy.start)
    arriving, leaving = [], []
    for start, width in ((0, CHUNK), (CHUNK, WIDTH - CHUNK)):
        cols = at(start, width)
        whole_cols = at(base + start, width)
        group = [
            come.copy(met_ref.at[:, cols], eb.at[:, cols]),
            come.copy(y_ref.at[:, cols], yb.at[:, cols]),
            come.copy(dx_ref.at[:, cols], db.at[:, cols]),
            come.copy(cot_ref.at[:, whole_cols], cb.at[:, cols]),
            come.copy(x_ref.at[:, whole_cols], xb.at[:, cols]),
        ]
        for copy in group:
            copy.start()
        arriving.append(group)
    clear_edges(z_ref, count)
    first.wait()
    keys, reads = halves(bc[:, :STATE]), halves(bc[:, STATE:])
    keys_both, reads_both = lanes(*keys), lanes(*reads)
    entry, leave = tab_ref[ENTRY : ENTRY + count, :], tab_ref[LEAVE : LEAVE + count, :]
    skip = tab_ref[SKIP : SKIP + 1, :]
    first_core = core == 0
    mask = columns(tab_ref[MASK : MASK + count, :], CHUNK)
    smask = columns(tab_ref[SMASK : SMASK + count + 8, :], CHUNK)
    dreads = jnp.zeros((count, STATE), F32)
    dkeys = jnp.zeros((count, STATE), F32)
    sums = jnp.zeros((4 * count + 16, 128), F32)
    for chosen, copy in choices:
        pl.when(chosen)(copy.wait)
    for start in range(0, WIDTH, CHUNK):
        cols = at(start)
        head = (base + start) // HEAD_DIM
        if start <= CHUNK:
            for copy in arriving[start // CHUNK]:
                copy.wait()
        inc, exch = decode(ib[:, cols]), decode(hb[:, cols])
        mine = eb[STATE : STATE + 1, cols] * inc + eb[:STATE, cols]
        state = jnp.where(first_core, exch, mine)
        adjoint = jnp.where(first_core, mine, exch)
        s_high, s_low = halves(state)
        a_high, a_low = halves(adjoint)
        e, leaves = by_head(entry, head, PER), by_head(leave, head, PER)
        ext_ref[8 : 8 + count, cols] = xb[:, cols].astype(F32)
        ext_ref[8 - CONV + 1 : 8, cols] = halo_ref[:, cols].astype(F32)
        taps = taps_of(ext_ref, cols, count, mask)
        act, slope = activate(taps, cols, w_ref, b_ref)
        up = cb[:, cols].astype(F32)
        carried = mm(reads_both, rows(s_high, s_high)) + mm(reads[0], s_low)
        y = yb[:, cols] + e * carried
        back = mm(keys_both, rows(a_high, a_high)) + mm(keys[0], a_low)
        back = leaves * back
        dx = db[:, cols] + back
        gain = by_head(skip, head, PER)
        ob[:, cols] = (y + gain * act).astype(BF16)
        ey_high, ey_low = halves(up * e)
        lx_high, lx_low = halves(act * leaves)
        dreads = dreads + mm(lanes(ey_high, ey_high, ey_low), lanes(s_high, s_low, s_high), ACROSS)
        dkeys = dkeys + mm(lanes(lx_high, lx_high, lx_low), lanes(a_high, a_low, a_high), ACROSS)
        through = e[count - 1 : count, :]
        end = jnp.sum(act * back, axis=0, keepdims=True)
        end = end + through * jnp.sum(state * adjoint, axis=0, keepdims=True)
        direct = jnp.sum(up * act, axis=0, keepdims=True)
        received = act * dx
        small = halves(rows(end, direct, jnp.zeros((6, CHUNK), F32)))
        stack = halves(up * y - received) + halves(received)
        pick = (iota((CHUNK, 128), 1) == head + iota((CHUNK, 128), 0) // HEAD_DIM).astype(BF16)
        sums = sums + mm(rows(*stack, rows(*small)), pick)
        dconv = (dx + gain * up) * slope
        gb[:, cols], nb[:, cols] = conv_back(dconv, taps, w_ref[:, cols], z_ref, cols, smask)
    for source, target in ((ob, out_ref), (gb, gin_ref), (nb, misc_ref)):
        copy = go.copy(source, target.at[:, at(base, WIDTH)])
        copy.start()
        leaving.append(copy)
    dreads_ref[...] = dreads
    dkeys_ref[...] = dkeys
    drun = sums[:count] + sums[count : 2 * count]
    received = sums[2 * count : 3 * count] + sums[3 * count : 4 * count]
    small = sums[4 * count : 4 * count + 8] + sums[4 * count + 8 :]
    drun = drun + jnp.where(iota((count, 128), 0) == count - 1, small[0:1, :], 0.0)
    later = (iota((count, count), 1) >= iota((count, count), 0)).astype(F32)
    ddecay = jnp.dot(later, drun, precision=EXACT, preferred_element_type=F32)
    pull, rate = tab_ref[PULL : PULL + count, :], tab_ref[RATE : RATE + count, :]
    ddtb = jnp.sum(received * pull + ddecay * rate, axis=0, keepdims=True)
    dalog = jnp.sum(ddecay * tab_ref[DECAY : DECAY + count, :], axis=0, keepdims=True)
    scal_ref[...] = rows(ddtb, dalog, small[1:2, :], jnp.zeros((5, 128), F32))
    for copy in leaving:
        copy.wait()


def final_kernel(x_ref, halo_ref, w_ref, tab_ref, work_ref, *refs):
    gin_ref, misc_ref, packed_ref, ext_ref, z_ref, sb, gb, sem = refs[-8:]
    gathered = pltpu.make_async_copy(refs[-9].at[at(16, 8), at(0, INNER)], gb, sem.at[1])
    gathered.start()
    parts = refs[: 4 * PIECES]
    count = x_ref.shape[0]
    copy = pltpu.make_async_copy(work_ref.at[at(SMALL, count), at(0, SCORES)], sb, sem.at[0])
    copy.start()
    ext_ref[8 : 8 + count, :] = x_ref[...].astype(F32)
    ext_ref[8 - CONV + 1 : 8, :] = halo_ref[...].astype(F32)
    clear_edges(z_ref, count)
    total = []
    for kind in range(4):
        value = parts[kind * PIECES][...]
        for piece in range(1, PIECES):
            value = value + parts[kind * PIECES + piece][...]
        total.append(value)
    dreads, dkeys, dscores, scal = total
    copy.wait()
    keys, reads = sb[:, at(BC_ACT, STATE)], sb[:, at(BC_ACT + STATE, STATE)]
    dreads = dreads + jnp.dot(dscores, keys, precision=EXACT, preferred_element_type=F32)
    dkeys = dkeys + jnp.dot(dscores.T, reads, precision=EXACT, preferred_element_type=F32)
    cols = slice(0, BC)
    dconv = lanes(dkeys, dreads) * sb[:, at(BC_SLOPE)]
    taps = taps_of(ext_ref, cols, count, columns(tab_ref[MASK : MASK + count, :], BC))
    smask = columns(tab_ref[SMASK : SMASK + count + 8, :], BC)
    gin_ref[...], misc = conv_back(dconv, taps, w_ref[...], z_ref, cols, smask)
    misc_ref[...] = misc
    gathered.wait()
    grads = lanes(gb[...], misc[16:, :])
    thirds = [grads[:, at(i * THIRD, THIRD)] for i in range(3)]
    packed_ref[0:8, :] = rows(thirds[0][:CONV], thirds[1][:CONV])
    fill = jnp.zeros((1, THIRD - 384), F32)
    params = lanes(scal[0:1, :], scal[1:2, :], scal[2:3, :], fill)
    last = [third[CONV : CONV + 1] for third in thirds]
    packed_ref[8:16, :] = rows(thirds[2][:CONV], *last, params)


def cost(us):
    return pl.CostEstimate(flops=int(us * 1.1e9), bytes_accessed=1000, transcendentals=0)


def whole(shape):
    return pl.BlockSpec(shape, lambda *_: (0,) * len(shape))


def part(shape, *index):
    return pl.BlockSpec(shape, lambda *_: index)


def full(*arrays):
    return [whole(a.shape) for a in arrays]


def call(kernel, ins, specs, outs, out_specs, scratch=(), aliases=None, us=1.0):
    return pl.pallas_call(
        kernel,
        grid=(1,),
        in_specs=specs,
        out_specs=out_specs,
        out_shape=[jax.ShapeDtypeStruct(shape, dtype) for shape, dtype in outs],
        scratch_shapes=list(scratch),
        input_output_aliases=aliases or {},
        compiler_params=pltpu.CompilerParams(vmem_limit_bytes=VMEM_LIMIT),
        cost_estimate=cost(us),
    )(*ins)


def vmem(rows_, cols, dtype=F32):
    return pltpu.VMEM((rows_, cols), dtype)


def sems(count):
    return pltpu.SemaphoreType.DMA((count,))


def permute(value, axis, target):
    size = lax.axis_size(axis)
    return lax.ppermute(value, axis, [(i, target(i)) for i in range(size)])


def other_core(value):
    return permute(value, "seq", lambda i: i ^ 1)


def along(size):
    def target(i):
        if i % 2 == 1:
            return i + 2 if i + 2 < size else i - 1
        return i - 2 if i >= 2 else i + 1

    return target


def xor_sum(value, axis, low):
    size = lax.axis_size(axis)
    bit = low
    while bit < size:
        if 2 * bit < size:
            one = permute(value, axis, lambda i: i ^ bit)
            two = permute(value, axis, lambda i: i ^ (2 * bit))
            three = permute(value, axis, lambda i: i ^ (3 * bit))
            value = (value + one) + (two + three)
            bit *= 4
        else:
            value = value + permute(value, axis, lambda i: i ^ bit)
            bit *= 2
    return value


def chip_of(piece, work, met):
    state = (STATE + 8, WIDTH)
    payload = (STATE + 16, WIDTH)
    outs = [(state, F32)] + [(payload, I16)] * (piece < STREAMS)
    return call(
        functools.partial(chip_kernel, piece),
        (work, met),
        [HBM] * 2,
        outs,
        [whole(s) for s, _ in outs],
        [vmem(*state), vmem(*state), sems(2)],
        us=1.5,
    )


def hop(turn, hops, previous, chips):
    payload = (STATE + 16, WIDTH)
    return call(
        functools.partial(hop_kernel, turn, hops),
        (previous, *chips),
        full(previous, *chips),
        [(payload, I16)],
        [whole(payload)],
        us=0.8,
    )[0]


def on_device(
    conv_input, doc_start, conv_weight, conv_bias, dt_raw, dt_bias, a_log, skip_gain, cotangent
):
    count = conv_input.shape[0]
    size = lax.axis_size("seq")
    core = lax.rem(lax.axis_index("seq"), 2)
    hops = size // 2 - 1
    docs = doc_start[None, :]
    edge = part((16, CH), count // 16 - 1, 0)

    tail_out = call(
        tail_kernel, (conv_input, docs), [edge, whole(docs.shape)],
        [((CONV - 1, CH), BF16)], [whole((CONV - 1, CH))],
    )[0]
    halo = lax.ppermute(tail_out, "seq", [(i, i + 1) for i in range(size - 1)])

    bias = conv_bias[None, :]
    prep_in = (docs, dt_raw.T, dt_bias[None, :], a_log[None, :], skip_gain[None, :])
    table = (TABLE, 128)
    tab = call(prep_kernel, prep_in, full(*prep_in), [(table, F32)], [whole(table)])[0]

    square = (count, count)
    payload = (STATE + 16, WIDTH)
    shape = (count, WIDTH)
    ins = (conv_input, halo, conv_weight, bias, cotangent, tab)
    outs = [(STATE + 8, WIDTH)] * PIECES + [(WORK_ROWS, INNER)]
    got = call(
        local_kernel,
        ins,
        [HBM, *full(halo, conv_weight, bias), HBM, whole(table)],
        [(s, F32) for s in outs],
        [HBM] * len(outs),
        [
            vmem(count, CH, BF16), vmem(count, INNER, BF16), vmem(STATE + 8, INNER),
            vmem(STATE + 8, INNER), vmem(count, SMALLS), vmem(count + 8, CH),
            sems(2 * PIECES + 1), sems(2 * PIECES + 1),
        ],
        us=8.0,
    )
    *sends, work = got
    mets = [other_core(send) for send in sends]
    chips, sent = [], []
    for j in range(PIECES):
        chip, *first = chip_of(j, work, mets[j])
        chips.append(chip)
        sent += first

    withins = []
    for j in range(PIECES):
        here = [part((height, WIDTH), 0, j) for height in (CONV - 1, CONV, 1)]
        withins.append(
            call(
                functools.partial(within_kernel, j),
                (conv_input, cotangent, work, halo, conv_weight, bias, tab),
                [HBM, HBM, HBM, *here, whole(table)],
                [(shape, F32), (shape, F32), (square, F32)],
                [HBM, HBM, whole(square)],
                [
                    vmem(*shape, BF16), vmem(*shape, BF16), vmem(*square), vmem(*shape),
                    vmem(*shape), vmem(count + 8, WIDTH), sems(3), sems(2),
                ],
                us=2.0,
            )
        )

    dreads, dkeys, scals = [None] * PIECES, [None] * PIECES, [None] * PIECES
    shared_out = [((count, INNER), BF16), ((count, CH), BF16), ((24, CH), F32)]
    small_out = [((count, STATE), F32), ((count, STATE), F32), ((8, 128), F32)]

    def finish(j, shared):
        turn, stream = j // STREAMS, j % STREAMS
        here = [part((height, WIDTH), 0, j) for height in (CONV - 1, CONV, 1)]
        y, dx, _ = withins[j]
        ins = [*received[stream][turn : turn + hops], *swapped[stream][turn : turn + hops]]
        specs = [ANY] * (2 * hops)
        ins += [mets[j], work, y, dx, cotangent, conv_input, halo, conv_weight, bias, tab]
        specs += [HBM] * 6 + here + [whole(table)]
        aliases = None
        if shared is not None:
            aliases = {len(ins) + i: i for i in range(3)}
            ins += shared
            specs += [HBM] * 3
        *shared, dreads[j], dkeys[j], scals[j] = call(
            functools.partial(finish_kernel, j, hops),
            ins,
            specs,
            shared_out + small_out,
            [HBM] * 3 + [whole(s) for s, _ in small_out],
            [
                vmem(*payload, I16), vmem(*payload, I16), vmem(STATE + 8, WIDTH), vmem(count, BC),
                vmem(*shape), vmem(*shape), vmem(*shape, BF16), vmem(*shape, BF16),
                vmem(*shape, BF16), vmem(*shape, BF16), vmem(24, WIDTH),
                vmem(count + 8, WIDTH), vmem(count + 16, WIDTH), sems(3 + 10), sems(3),
            ],
            aliases,
            us=5.0,
        )
        return shared

    received = [[] for _ in range(STREAMS)]
    swapped = [[] for _ in range(STREAMS)]
    shared = None
    turns = TURNS + hops - 1
    for turn in range(turns):
        if turn:
            sent = [
                hop(turn, hops, received[stream][-1], chips[stream::STREAMS])
                for stream in range(STREAMS)
            ]
        arrived = [permute(value, "seq", along(size)) for value in sent]
        for stream in range(STREAMS):
            got = arrived[stream]
            if turn == turns - 1:
                shared = finish(stream, shared)
                got, shared = lax.optimization_barrier((got, shared))
            received[stream].append(got)
            swapped[stream].append(other_core(got))
    for j in range(STREAMS, PIECES):
        shared = finish(j, shared)
    output, gin, misc = shared

    dscores = [group[2] for group in withins]
    small = (*dreads, *dkeys, *dscores, *scals)
    ins = (conv_input, halo, conv_weight, tab, work) + small + (gin, misc)
    bc_common = [part((count, BC), 0, BC_AT), part((CONV - 1, BC), 0, BC_AT), part((CONV, BC), 0, BC_AT)]
    gin, misc, packed = call(
        final_kernel,
        ins,
        bc_common + [whole(table), HBM] + full(*small) + [HBM] * 2,
        shared_out[1:] + [((16, THIRD), F32)],
        [part((count, BC), 0, BC_AT), part((24, BC), 0, BC_AT), whole((16, THIRD))],
        [
            vmem(count + 8, BC), vmem(count + 16, BC), vmem(count, SCORES), vmem(8, INNER), sems(2),
        ],
        {len(ins) - 2: 0, len(ins) - 1: 1},
    )

    returned = lax.ppermute(
        misc[8 - CONV + 1 : 8], "seq", [(i, i - 1) for i in range(1, size)]
    )
    lower, upper = packed[:8], packed[8:]
    first = core == 0
    value = jnp.where(first, lower, upper)
    value = value + other_core(jnp.where(first, upper, lower))
    value = xor_sum(value, "dp", 1)
    value, returned = lax.optimization_barrier((value, returned))
    grad_input = call(
        edge_kernel,
        (gin, misc, returned, docs),
        [edge, part((8, CH), 1, 0), *full(returned, docs)],
        [((count, CH), BF16)],
        [edge],
        aliases={0: 0},
    )[0]
    value = xor_sum(value, "seq", 2)
    value, grad_input = lax.optimization_barrier((value, grad_input))
    value = value * float(lax.axis_size("dp") * size * count) ** (-0.5)
    other = other_core(value)
    lower = jnp.where(first, value, other)
    upper = jnp.where(first, other, value)
    grad_weight = jnp.concatenate([lower[:CONV], lower[CONV:], upper[:CONV]], axis=1)
    grad_bias = upper[CONV : CONV + 3].reshape(CH)
    params = [upper[CONV + 3, i : i + HEADS] for i in (0, 128, 256)]
    return (output, grad_input, grad_weight, grad_bias, *params)


def solution(mesh):
    return jax.shard_map(
        on_device,
        mesh=mesh,
        in_specs=(
            P(("dp", "seq"), None),
            P(("dp", "seq")),
            P(),
            P(),
            P(("dp", "seq"), None),
            P(),
            P(),
            P(),
            P(("dp", "seq"), None),
        ),
        out_specs=(P(("dp", "seq"), None), P(("dp", "seq"), None), P(), P(), P(), P(), P()),
        check_vma=False,
    )
```

```python
import functools

import jax
import jax.numpy as jnp
from jax import lax
from jax.experimental import pallas as pl
from jax.experimental.pallas import tpu as pltpu
from jax.sharding import PartitionSpec as P

HEADS = 80
HEAD_DIM = 64
STATE = 128
CONV = 4
INNER = 5120
CH = 5376

STREAMS = 2
TURNS = 2
PIECES = STREAMS * TURNS
PIECE_HEADS = HEADS // PIECES
WIDTH = PIECE_HEADS * HEAD_DIM
SPAN = STREAMS * WIDTH
PAIR = 2 * HEAD_DIM
CHUNK = 256
BC = 2 * STATE
BC_AT = INNER // BC
FAR = -1e30
STATES, SMALL = 0, 256
BC_ACT, BC_SLOPE, SCORES, SMALLS = 0, 256, 512, 640
WORK_ROWS = 3328
CODE = 32766.0
THIRD = CH // 3
PER = CHUNK // HEAD_DIM

F32 = jnp.float32
BF16 = jnp.bfloat16
I16 = jnp.int16
EXACT = lax.Precision.HIGHEST
ACROSS = ((1,), (1,))
ANY = pl.BlockSpec(memory_space=pl.ANY)
HBM = pl.BlockSpec(memory_space=pltpu.HBM)
VMEM_LIMIT = 24 * 1024 * 1024

MASK, ENTRY, LEAVE, PULL, RATE, DECAY, RUN, FAR_AT, ROW, SMASK = range(0, 1280, 128)
SKIP = ROW + HEADS
TABLE = SMASK + 136


def iota(shape, dim):
    return lax.broadcasted_iota(jnp.int32, shape, dim)


def mm(a, b, contract=((1,), (0,))):
    return lax.dot_general(a, b, (contract, ((), ())), preferred_element_type=F32)


def halves(value):
    high = value.astype(BF16)
    return high, (value - high.astype(F32)).astype(BF16)


def lanes(*parts):
    return jnp.concatenate(parts, axis=1)


def rows(*parts):
    return jnp.concatenate(parts, axis=0)


def by_head(table, first, count):
    out = []
    for head in range(first, first + count, 2):
        shape = (table.shape[0], PAIR)
        left = jnp.broadcast_to(table[:, head : head + 1], shape)
        right = jnp.broadcast_to(table[:, head + 1 : head + 2], shape)
        out.append(jnp.where(iota(shape, 1) < HEAD_DIM, left, right))
    return lanes(*out)


def taps_of(ext_ref, cols, count, mask):
    taps = []
    for tap in range(CONV):
        back = CONV - 1 - tap
        value = ext_ref[8 - back : 8 - back + count, cols]
        taps.append(value if back == 0 else value * mask[back])
    return taps


def columns(table, width):
    shape = (table.shape[0], width)
    return [jnp.broadcast_to(table[:, i : i + 1], shape) for i in range(CONV)]


def activate(taps, cols, w_ref, b_ref):
    v = b_ref[:, cols] + w_ref[CONV - 1 : CONV, cols] * taps[CONV - 1]
    for tap in range(CONV - 2, -1, -1):
        v = v + w_ref[tap : tap + 1, cols] * taps[tap]
    gate = 1.0 / (1.0 + jnp.exp(-v))
    return v * gate, gate * (1.0 + v * (1.0 - gate))


class Flow:
    def __init__(self, sems):
        self.sems = sems
        self.used = 0

    def copy(self, source, target):
        made = pltpu.make_async_copy(source, target, self.sems.at[self.used])
        self.used += 1
        return made


def position(hops):
    index = lax.axis_index("seq")
    core = lax.rem(index, 2)
    chip = lax.div(index, 2)
    return core, jnp.where(core == 1, chip, hops - chip)


def at(first, width=CHUNK):
    return slice(first, first + width)


def tail_kernel(x_ref, doc_ref, out_ref):
    count = doc_ref.shape[1]
    edge = x_ref.shape[0] - CONV + 1
    cut = jnp.zeros((1, 1), F32)
    for back in range(CONV - 1):
        row = edge + CONV - 2 - back
        if back:
            cut = cut + doc_ref[:, count - back : count - back + 1].astype(F32)
        keep = (cut == 0.0).astype(F32)
        value = x_ref[row : row + 1, :].astype(F32) * keep
        out_ref[CONV - 2 - back : CONV - 1 - back, :] = value.astype(BF16)


def edge_kernel(gin_ref, misc_ref, back_ref, doc_ref, out_ref):
    count = doc_ref.shape[1]
    size = gin_ref.shape[0]
    cut = jnp.zeros((1, 1), F32)
    keeps = []
    for back in range(CONV - 1):
        if back:
            cut = cut + doc_ref[:, count - back : count - back + 1].astype(F32)
        keeps.insert(0, (cut == 0.0).astype(F32))
    place = iota((8, 1), 0)
    value = misc_ref[...]
    for i in range(CONV - 1):
        row = 8 - CONV + 1 + i
        value = value + jnp.where(place == row, back_ref[i : i + 1, :] * keeps[i], 0.0)
    out_ref[...] = gin_ref[...]
    out_ref[size - 8 :, :] = value.astype(BF16)


def prep_kernel(doc_ref, raw_ref, dtb_ref, alog_ref, skip_ref, tab_ref):
    count = raw_ref.shape[1]
    resets = doc_ref[...].astype(F32)
    t, s = iota((count, count), 0), iota((count, count), 1)

    def total(keep, shape):
        return jnp.sum(jnp.where(keep, jnp.broadcast_to(resets, shape), 0.0), axis=1, keepdims=True)

    square = (count, count)
    lane = iota((count, 128), 1)
    table = jnp.ones((count, 128), F32)
    for back in range(1, CONV):
        fits = (total((s <= t) & (s > t - back), square) == 0.0).astype(F32)
        table = jnp.where(lane == back, fits, table)
    tab_ref[MASK : MASK + count, :] = table
    wide = (count + 8, count)
    at, s_wide = iota(wide, 0) - 8, iota(wide, 1)
    lane, place = iota((count + 8, 128), 1), iota((count + 8, 128), 0) - 8
    table = jnp.zeros((count + 8, 128), F32)
    for ahead in range(CONV):
        fits = (total((s_wide > at) & (s_wide <= at + ahead), wide) == 0.0).astype(F32)
        fits = jnp.where((place + ahead >= 0) & (place + ahead < count), fits, 0.0)
        table = jnp.where(lane == ahead, fits, table)
    tab_ref[SMASK : SMASK + count + 8, :] = table
    segment = total(s <= t, square)
    reset_col = total(s == t, square)
    segment_row = jnp.sum(
        jnp.where(t <= s, jnp.broadcast_to(reset_col, square), 0.0), axis=0, keepdims=True
    )
    causal = (s <= t) & (segment == segment_row)
    tab_ref[FAR_AT : FAR_AT + count, :] = jnp.where(causal, 0.0, FAR)
    raw = rows(raw_ref[...], jnp.zeros((128 - HEADS, count), F32)).T[:, :HEADS]
    v = raw + dtb_ref[...]
    dt = jnp.maximum(v, 0.0) + jnp.log1p(jnp.exp(-jnp.abs(v)))
    rate = -jnp.exp(alog_ref[...])
    decay = rate * dt
    run = jnp.dot((s <= t).astype(F32), decay, precision=EXACT, preferred_element_type=F32)
    end = run[count - 1 : count, :]
    last = segment == segment[count - 1 : count, :]
    gate = 1.0 / (1.0 + jnp.exp(-v))
    fill = jnp.zeros((count, 128 - HEADS), F32)

    def put(where, value):
        tab_ref[where : where + count, :] = lanes(value, fill)

    put(ENTRY, jnp.where(segment == 0.0, jnp.exp(run), 0.0))
    put(LEAVE, jnp.where(last, jnp.exp(end - run) * dt, 0.0))
    put(PULL, gate / dt)
    put(RATE, rate * gate)
    put(DECAY, decay)
    put(RUN, run)
    tab_ref[ROW : ROW + 128, :] = lanes(jnp.log(dt) - run, fill).T
    tab_ref[SKIP : SKIP + 1, :] = lanes(skip_ref[...], fill[:1])


def scores_of(act):
    keys, reads = act[:, :STATE], act[:, STATE:]
    return lax.dot_general(
        reads, keys, (ACROSS, ((), ())), precision=EXACT, preferred_element_type=F32
    )


def local_kernel(x_ref, halo_ref, w_ref, b_ref, cot_ref, tab_ref, *refs):
    send_refs = refs[:PIECES]
    work_ref = refs[PIECES]
    xb, cb, nb, mb, sb, ext_ref, in_sems, out_sems = refs[-8:]
    count = xb.shape[0]
    come, go = Flow(in_sems), Flow(out_sems)
    first = come.copy(x_ref.at[:, at(INNER, BC)], xb.at[:, at(INNER, BC)])
    first.start()
    arriving, leaving = [], []
    for piece in range(PIECES):
        cols = at(piece * WIDTH, WIDTH)
        pair = (
            come.copy(x_ref.at[:, cols], xb.at[:, cols]),
            come.copy(cot_ref.at[:, cols], cb.at[:, cols]),
        )
        for copy in pair:
            copy.start()
        arriving.append(pair)
    mask = columns(tab_ref[MASK : MASK + count, :], CHUNK)

    def act_of(cols):
        ext_ref[8 : 8 + count, cols] = xb[:, cols].astype(F32)
        ext_ref[8 - CONV + 1 : 8, cols] = halo_ref[:, cols].astype(F32)
        return activate(taps_of(ext_ref, cols, count, mask), cols, w_ref, b_ref)

    first.wait()
    act, slope = act_of(at(INNER, BC))
    sb[:, at(BC_ACT)] = act
    sb[:, at(BC_SLOPE)] = slope
    sb[:, at(SCORES, 128)] = scores_of(act)
    copy = go.copy(sb, work_ref.at[at(SMALL, count), at(0, SMALLS)])
    copy.start()
    leaving.append(copy)
    turned = rows(act[:, :STATE].T, act[:, STATE:].T)
    keys, reads = halves(turned[:STATE, :]), halves(turned[STATE:, :])
    keys_both, reads_both = lanes(*keys), lanes(*reads)
    entry, leave = tab_ref[ENTRY : ENTRY + count, :], tab_ref[LEAVE : LEAVE + count, :]
    first_core = lax.rem(lax.axis_index("seq"), 2) == 0
    for piece in range(PIECES):
        for copy in arriving[piece]:
            copy.wait()
        for start in range(piece * WIDTH, (piece + 1) * WIDTH, CHUNK):
            cols = at(start)
            head = start // HEAD_DIM
            act, _ = act_of(cols)
            e = by_head(entry, head, PER)
            lx_high, lx_low = halves(act * by_head(leave, head, PER))
            ey_high, ey_low = halves(cb[:, cols].astype(F32) * e)
            state = mm(keys_both, rows(lx_high, lx_high)) + mm(keys[0], lx_low)
            adjoint = mm(reads_both, rows(ey_high, ey_high)) + mm(reads[0], ey_low)
            nb[:STATE, cols] = jnp.where(first_core, state, adjoint)
            mb[:STATE, cols] = jnp.where(first_core, adjoint, state)
            through = jnp.broadcast_to(e[count - 1 : count, :], (8, CHUNK))
            nb[STATE:, cols] = through
            mb[STATE:, cols] = through
        cols = at(piece * WIDTH, WIDTH)
        for source, target in ((nb, send_refs[piece]), (mb, work_ref.at[at(STATES, STATE + 8), cols])):
            copy = go.copy(source.at[:, cols], target)
            copy.start()
            leaving.append(copy)
    for copy in leaving:
        copy.wait()


def decode(codes):
    scale = jnp.exp2(codes[STATE : STATE + 1, :].astype(F32) * (1.0 / 256.0)) * (1.0 / CODE)
    return codes[:STATE, :].astype(F32) * scale


def encode(value):
    most = jnp.max(jnp.abs(value), axis=0, keepdims=True)
    power = jnp.ceil(jnp.log2(jnp.maximum(most, 1e-30)) * 256.0)
    scale = jnp.exp2(power * (1.0 / 256.0)) * (1.0 / CODE)
    codes = jnp.floor(value * (1.0 / scale) + 0.5).astype(jnp.int32)
    tail = jnp.broadcast_to(power.astype(jnp.int32), (16, value.shape[1]))
    return rows(codes, tail).astype(I16)


def chip_kernel(piece, work_ref, met_ref, *refs):
    chip_ref = refs[0]
    mb, eb, sem = refs[-3:]
    come = Flow(sem)
    mine = work_ref.at[at(STATES, STATE + 8), at(piece * WIDTH, WIDTH)]
    copies = [come.copy(mine, mb), come.copy(met_ref, eb)]
    for copy in copies:
        copy.start()
    for copy in copies:
        copy.wait()
    for start in range(0, WIDTH, CHUNK):
        cols = at(start)
        own = mb[STATE : STATE + 1, cols]
        value = mb[:STATE, cols] + own * eb[:STATE, cols]
        chip_ref[:STATE, cols] = value
        chip_ref[STATE:, cols] = own * eb[STATE:, cols]
        if piece < STREAMS:
            refs[1][:, cols] = encode(value)


def hop_kernel(turn, hops, previous_ref, *refs):
    chip_refs, out_ref = refs[:-1], refs[-1]
    _, place = position(hops)
    for start in range(0, WIDTH, CHUNK):
        cols = at(start)
        chip = chip_refs[0][:, cols]
        for i, ref in enumerate(chip_refs[1:]):
            chip = jnp.where(turn - place > i, ref[:, cols], chip)
        before = jnp.where(place == 0, 0.0, decode(previous_ref[:, cols]))
        out_ref[:, cols] = encode(chip[:STATE, :] + chip[STATE : STATE + 1, :] * before)


def within_kernel(
    piece, x_ref, cot_ref, work_ref, halo_ref, w_ref, b_ref, tab_ref, y_ref, dx_ref, dscores_ref, *refs
):
    xb, cb, sb, yb, db, ext_ref, in_sems, out_sems = refs
    count = xb.shape[0]
    come, go = Flow(in_sems), Flow(out_sems)
    copies = (
        come.copy(x_ref.at[:, at(piece * WIDTH, WIDTH)], xb),
        come.copy(cot_ref.at[:, at(piece * WIDTH, WIDTH)], cb),
        come.copy(work_ref.at[at(SMALL, count), at(SCORES, count)], sb),
    )
    for copy in copies:
        copy.start()
    mask = columns(tab_ref[MASK : MASK + count, :], PAIR)
    for copy in copies:
        copy.wait()
    run = tab_ref[RUN : RUN + count, :]
    far, scores = tab_ref[FAR_AT : FAR_AT + count, :], sb[...]
    left = iota((count, PAIR), 1) < HEAD_DIM
    total = jnp.zeros((count, count), F32)
    zero = jnp.zeros((count, PAIR), BF16)
    for pair in range(PIECE_HEADS // 2):
        cols = at(pair * PAIR, PAIR)
        ext_ref[8 : 8 + count, cols] = xb[:, cols].astype(F32)
        ext_ref[8 - CONV + 1 : 8, cols] = halo_ref[:, cols].astype(F32)
        act, _ = activate(taps_of(ext_ref, cols, count, mask), cols, w_ref, b_ref)
        x_high, x_low = halves(act)
        upstream = cb[:, cols]
        upstream_turned = upstream.astype(F32).T.astype(BF16)
        spread, weights = [], []
        for side in range(2):
            head = piece * PIECE_HEADS + 2 * pair + side
            row = tab_ref[ROW + head : ROW + head + 1, :]
            within = jnp.exp(run[:, head : head + 1] + row + far)
            spread.append(within)
            weights.append(lanes(*halves(within * scores)))
        out = mm(rows(*weights), rows(lanes(x_high, x_low), lanes(x_high, zero)))
        out = out[:, :PAIR] + out[:, PAIR:]
        yb[:, cols] = jnp.where(left, out[:count], out[count:])
        parts = []
        for side in range(2):
            mine = upstream_turned[side * HEAD_DIM : (side + 1) * HEAD_DIM, :]
            pushed = rows(weights[side][:, :count], weights[side][:, count:])
            parts.append(mm(lanes(mine, mine), pushed))
        db[:, cols] = rows(*parts).T
        up_left, up_right = jnp.where(left, upstream, zero), jnp.where(left, zero, upstream)
        lhs = rows(lanes(up_left, up_left), lanes(up_right, up_right))
        products = mm(lhs, lanes(x_high, x_low), ACROSS)
        total = total + spread[0] * products[:count] + spread[1] * products[count:]
    copies = (go.copy(yb, y_ref), go.copy(db, dx_ref))
    for copy in copies:
        copy.start()
    dscores_ref[...] = total
    for copy in copies:
        copy.wait()


def conv_back(dconv, taps, w, z_ref, z_cols, smask):
    count, width = dconv.shape
    z_ref[8 : 8 + count, z_cols] = dconv
    grad = jnp.zeros((count + 8, width), F32)
    for ahead in range(CONV):
        tap = CONV - 1 - ahead
        shifted = z_ref[ahead : ahead + count + 8, z_cols]
        grad = grad + w[tap : tap + 1, :] * (shifted * smask[ahead])
    sums = [jnp.sum(dconv * tap, axis=0, keepdims=True) for tap in taps]
    sums.append(jnp.sum(dconv, axis=0, keepdims=True))
    sums.append(jnp.zeros((3, width), F32))
    return grad[8:].astype(BF16), rows(grad[:8], grad[count:], *sums)


def clear_edges(z_ref, count):
    z_ref[0:8, :] = jnp.zeros((8, z_ref.shape[1]), F32)
    z_ref[8 + count : 16 + count, :] = jnp.zeros((8, z_ref.shape[1]), F32)


def finish_kernel(piece, hops, *refs):
    incs, exchs = refs[:hops], refs[hops : 2 * hops]
    refs = refs[2 * hops :]
    met_ref, work_ref, y_ref, dx_ref, cot_ref, x_ref, halo_ref, w_ref, b_ref, tab_ref = refs[:10]
    out_ref, gin_ref, misc_ref, dreads_ref, dkeys_ref, scal_ref = refs[-21:-15]
    ib, hb, eb, bc, yb, db, cb, xb, ob, gb, nb, ext_ref, z_ref, in_sems, out_sems = refs[-15:]
    count = xb.shape[0]
    come, go = Flow(in_sems), Flow(out_sems)
    base = piece * WIDTH
    core, place = position(hops)
    first = come.copy(work_ref.at[at(SMALL, count), at(BC_ACT)], bc)
    first.start()
    choices = []
    for here, sources, buffer in ((place, incs, ib), (hops - place, exchs, hb)):
        sem = come.used
        come.used += 1
        for i, source in enumerate(sources):
            choices.append((here == i + 1, pltpu.make_async_copy(source, buffer, come.sems.at[sem])))

        @pl.when(here == 0)
        def _():
            buffer[...] = jnp.zeros(buffer.shape, I16)

    for chosen, copy in choices:
        pl.when(chosen)(copy.start)
    arriving, leaving = [], []
    for start, width in ((0, CHUNK), (CHUNK, WIDTH - CHUNK)):
        cols = at(start, width)
        whole_cols = at(base + start, width)
        group = [
            come.copy(met_ref.at[:, cols], eb.at[:, cols]),
            come.copy(y_ref.at[:, cols], yb.at[:, cols]),
            come.copy(dx_ref.at[:, cols], db.at[:, cols]),
            come.copy(cot_ref.at[:, whole_cols], cb.at[:, cols]),
            come.copy(x_ref.at[:, whole_cols], xb.at[:, cols]),
        ]
        for copy in group:
            copy.start()
        arriving.append(group)
    clear_edges(z_ref, count)
    first.wait()
    keys, reads = halves(bc[:, :STATE]), halves(bc[:, STATE:])
    keys_both, reads_both = lanes(*keys), lanes(*reads)
    entry, leave = tab_ref[ENTRY : ENTRY + count, :], tab_ref[LEAVE : LEAVE + count, :]
    skip = tab_ref[SKIP : SKIP + 1, :]
    first_core = core == 0
    mask = columns(tab_ref[MASK : MASK + count, :], CHUNK)
    smask = columns(tab_ref[SMASK : SMASK + count + 8, :], CHUNK)
    dreads = jnp.zeros((count, STATE), F32)
    dkeys = jnp.zeros((count, STATE), F32)
    sums = jnp.zeros((4 * count + 16, 128), F32)
    for chosen, copy in choices:
        pl.when(chosen)(copy.wait)
    for start in range(0, WIDTH, CHUNK):
        cols = at(start)
        head = (base + start) // HEAD_DIM
        if start <= CHUNK:
            for copy in arriving[start // CHUNK]:
                copy.wait()
        inc, exch = decode(ib[:, cols]), decode(hb[:, cols])
        mine = eb[STATE : STATE + 1, cols] * inc + eb[:STATE, cols]
        state = jnp.where(first_core, exch, mine)
        adjoint = jnp.where(first_core, mine, exch)
        s_high, s_low = halves(state)
        a_high, a_low = halves(adjoint)
        e, leaves = by_head(entry, head, PER), by_head(leave, head, PER)
        ext_ref[8 : 8 + count, cols] = xb[:, cols].astype(F32)
        ext_ref[8 - CONV + 1 : 8, cols] = halo_ref[:, cols].astype(F32)
        taps = taps_of(ext_ref, cols, count, mask)
        act, slope = activate(taps, cols, w_ref, b_ref)
        up = cb[:, cols].astype(F32)
        carried = mm(reads_both, rows(s_high, s_high)) + mm(reads[0], s_low)
        y = yb[:, cols] + e * carried
        back = mm(keys_both, rows(a_high, a_high)) + mm(keys[0], a_low)
        back = leaves * back
        dx = db[:, cols] + back
        gain = by_head(skip, head, PER)
        ob[:, cols] = (y + gain * act).astype(BF16)
        ey_high, ey_low = halves(up * e)
        lx_high, lx_low = halves(act * leaves)
        dreads = dreads + mm(lanes(ey_high, ey_high, ey_low), lanes(s_high, s_low, s_high), ACROSS)
        dkeys = dkeys + mm(lanes(lx_high, lx_high, lx_low), lanes(a_high, a_low, a_high), ACROSS)
        through = e[count - 1 : count, :]
        end = jnp.sum(act * back, axis=0, keepdims=True)
        end = end + through * jnp.sum(state * adjoint, axis=0, keepdims=True)
        direct = jnp.sum(up * act, axis=0, keepdims=True)
        received = act * dx
        small = halves(rows(end, direct, jnp.zeros((6, CHUNK), F32)))
        stack = halves(up * y - received) + halves(received)
        pick = (iota((CHUNK, 128), 1) == head + iota((CHUNK, 128), 0) // HEAD_DIM).astype(BF16)
        sums = sums + mm(rows(*stack, rows(*small)), pick)
        dconv = (dx + gain * up) * slope
        gb[:, cols], nb[:, cols] = conv_back(dconv, taps, w_ref[:, cols], z_ref, cols, smask)
    for source, target in ((ob, out_ref), (gb, gin_ref), (nb, misc_ref)):
        copy = go.copy(source, target.at[:, at(base, WIDTH)])
        copy.start()
        leaving.append(copy)
    dreads_ref[...] = dreads
    dkeys_ref[...] = dkeys
    drun = sums[:count] + sums[count : 2 * count]
    received = sums[2 * count : 3 * count] + sums[3 * count : 4 * count]
    small = sums[4 * count : 4 * count + 8] + sums[4 * count + 8 :]
    drun = drun + jnp.where(iota((count, 128), 0) == count - 1, small[0:1, :], 0.0)
    later = (iota((count, count), 1) >= iota((count, count), 0)).astype(F32)
    ddecay = jnp.dot(later, drun, precision=EXACT, preferred_element_type=F32)
    pull, rate = tab_ref[PULL : PULL + count, :], tab_ref[RATE : RATE + count, :]
    ddtb = jnp.sum(received * pull + ddecay * rate, axis=0, keepdims=True)
    dalog = jnp.sum(ddecay * tab_ref[DECAY : DECAY + count, :], axis=0, keepdims=True)
    scal_ref[...] = rows(ddtb, dalog, small[1:2, :], jnp.zeros((5, 128), F32))
    for copy in leaving:
        copy.wait()


def final_kernel(x_ref, halo_ref, w_ref, tab_ref, work_ref, *refs):
    gin_ref, misc_ref, packed_ref, ext_ref, z_ref, sb, gb, sem = refs[-8:]
    gathered = pltpu.make_async_copy(refs[-9].at[at(16, 8), at(0, INNER)], gb, sem.at[1])
    gathered.start()
    parts = refs[: 4 * PIECES]
    count = x_ref.shape[0]
    copy = pltpu.make_async_copy(work_ref.at[at(SMALL, count), at(0, SCORES)], sb, sem.at[0])
    copy.start()
    ext_ref[8 : 8 + count, :] = x_ref[...].astype(F32)
    ext_ref[8 - CONV + 1 : 8, :] = halo_ref[...].astype(F32)
    clear_edges(z_ref, count)
    total = []
    for kind in range(4):
        value = parts[kind * PIECES][...]
        for piece in range(1, PIECES):
            value = value + parts[kind * PIECES + piece][...]
        total.append(value)
    dreads, dkeys, dscores, scal = total
    copy.wait()
    keys, reads = sb[:, at(BC_ACT, STATE)], sb[:, at(BC_ACT + STATE, STATE)]
    dreads = dreads + jnp.dot(dscores, keys, precision=EXACT, preferred_element_type=F32)
    dkeys = dkeys + jnp.dot(dscores.T, reads, precision=EXACT, preferred_element_type=F32)
    cols = slice(0, BC)
    dconv = lanes(dkeys, dreads) * sb[:, at(BC_SLOPE)]
    taps = taps_of(ext_ref, cols, count, columns(tab_ref[MASK : MASK + count, :], BC))
    smask = columns(tab_ref[SMASK : SMASK + count + 8, :], BC)
    gin_ref[...], misc = conv_back(dconv, taps, w_ref[...], z_ref, cols, smask)
    misc_ref[...] = misc
    gathered.wait()
    grads = lanes(gb[...], misc[16:, :])
    thirds = [grads[:, at(i * THIRD, THIRD)] for i in range(3)]
    packed_ref[0:8, :] = rows(thirds[0][:CONV], thirds[1][:CONV])
    fill = jnp.zeros((1, THIRD - 384), F32)
    params = lanes(scal[0:1, :], scal[1:2, :], scal[2:3, :], fill)
    last = [third[CONV : CONV + 1] for third in thirds]
    packed_ref[8:16, :] = rows(thirds[2][:CONV], *last, params)


def cost(us):
    return pl.CostEstimate(flops=int(us * 1.1e9), bytes_accessed=1000, transcendentals=0)


def whole(shape):
    return pl.BlockSpec(shape, lambda *_: (0,) * len(shape))


def part(shape, *index):
    return pl.BlockSpec(shape, lambda *_: index)


def full(*arrays):
    return [whole(a.shape) for a in arrays]


def call(kernel, ins, specs, outs, out_specs, scratch=(), aliases=None, us=1.0):
    return pl.pallas_call(
        kernel,
        grid=(1,),
        in_specs=specs,
        out_specs=out_specs,
        out_shape=[jax.ShapeDtypeStruct(shape, dtype) for shape, dtype in outs],
        scratch_shapes=list(scratch),
        input_output_aliases=aliases or {},
        compiler_params=pltpu.CompilerParams(vmem_limit_bytes=VMEM_LIMIT),
        cost_estimate=cost(us),
    )(*ins)


def vmem(rows_, cols, dtype=F32):
    return pltpu.VMEM((rows_, cols), dtype)


def sems(count):
    return pltpu.SemaphoreType.DMA((count,))


def permute(value, axis, target):
    size = lax.axis_size(axis)
    return lax.ppermute(value, axis, [(i, target(i)) for i in range(size)])


def other_core(value):
    return permute(value, "seq", lambda i: i ^ 1)


def along(size):
    def target(i):
        if i % 2 == 1:
            return i + 2 if i + 2 < size else i - 1
        return i - 2 if i >= 2 else i + 1

    return target


def xor_sum(value, axis, low):
    size = lax.axis_size(axis)
    bit = low
    while bit < size:
        if 2 * bit < size:
            one = permute(value, axis, lambda i: i ^ bit)
            two = permute(value, axis, lambda i: i ^ (2 * bit))
            three = permute(value, axis, lambda i: i ^ (3 * bit))
            value = (value + one) + (two + three)
            bit *= 4
        else:
            value = value + permute(value, axis, lambda i: i ^ bit)
            bit *= 2
    return value


def chip_of(piece, work, met):
    state = (STATE + 8, WIDTH)
    payload = (STATE + 16, WIDTH)
    outs = [(state, F32)] + [(payload, I16)] * (piece < STREAMS)
    return call(
        functools.partial(chip_kernel, piece),
        (work, met),
        [HBM] * 2,
        outs,
        [whole(s) for s, _ in outs],
        [vmem(*state), vmem(*state), sems(2)],
        us=1.5,
    )


def hop(turn, hops, previous, chips):
    payload = (STATE + 16, WIDTH)
    return call(
        functools.partial(hop_kernel, turn, hops),
        (previous, *chips),
        full(previous, *chips),
        [(payload, I16)],
        [whole(payload)],
        us=0.8,
    )[0]


def on_device(
    conv_input, doc_start, conv_weight, conv_bias, dt_raw, dt_bias, a_log, skip_gain, cotangent
):
    count = conv_input.shape[0]
    size = lax.axis_size("seq")
    core = lax.rem(lax.axis_index("seq"), 2)
    hops = size // 2 - 1
    docs = doc_start[None, :]
    edge = part((16, CH), count // 16 - 1, 0)

    tail_out = call(
        tail_kernel, (conv_input, docs), [edge, whole(docs.shape)],
        [((CONV - 1, CH), BF16)], [whole((CONV - 1, CH))],
    )[0]
    halo = lax.ppermute(tail_out, "seq", [(i, i + 1) for i in range(size - 1)])

    bias = conv_bias[None, :]
    prep_in = (docs, dt_raw.T, dt_bias[None, :], a_log[None, :], skip_gain[None, :])
    table = (TABLE, 128)
    tab = call(prep_kernel, prep_in, full(*prep_in), [(table, F32)], [whole(table)])[0]

    square = (count, count)
    payload = (STATE + 16, WIDTH)
    shape = (count, WIDTH)
    ins = (conv_input, halo, conv_weight, bias, cotangent, tab)
    outs = [(STATE + 8, WIDTH)] * PIECES + [(WORK_ROWS, INNER)]
    got = call(
        local_kernel,
        ins,
        [HBM, *full(halo, conv_weight, bias), HBM, whole(table)],
        [(s, F32) for s in outs],
        [HBM] * len(outs),
        [
            vmem(count, CH, BF16), vmem(count, INNER, BF16), vmem(STATE + 8, INNER),
            vmem(STATE + 8, INNER), vmem(count, SMALLS), vmem(count + 8, CH),
            sems(2 * PIECES + 1), sems(2 * PIECES + 1),
        ],
        us=8.0,
    )
    *sends, work = got
    mets = [other_core(send) for send in sends]
    chips, sent = [], []
    for j in range(PIECES):
        chip, *first = chip_of(j, work, mets[j])
        chips.append(chip)
        sent += first

    def within(j, work):
        here = [part((height, WIDTH), 0, j) for height in (CONV - 1, CONV, 1)]
        return call(
            functools.partial(within_kernel, j),
            (conv_input, cotangent, work, halo, conv_weight, bias, tab),
            [HBM, HBM, HBM, *here, whole(table)],
            [(shape, F32), (shape, F32), (square, F32)],
            [HBM, HBM, whole(square)],
            [
                vmem(*shape, BF16), vmem(*shape, BF16), vmem(*square), vmem(*shape),
                vmem(*shape), vmem(count + 8, WIDTH), sems(3), sems(2),
            ],
            us=2.0,
        )

    withins = [within(j, work) for j in range(PIECES - 1)]
    dreads, dkeys, scals = [None] * PIECES, [None] * PIECES, [None] * PIECES
    shared_out = [((count, INNER), BF16), ((count, CH), BF16), ((24, CH), F32)]
    small_out = [((count, STATE), F32), ((count, STATE), F32), ((8, 128), F32)]

    def finish(j, shared):
        turn, stream = j // STREAMS, j % STREAMS
        here = [part((height, WIDTH), 0, j) for height in (CONV - 1, CONV, 1)]
        y, dx, _ = withins[j]
        ins = [*received[stream][turn : turn + hops], *swapped[stream][turn : turn + hops]]
        specs = [ANY] * (2 * hops)
        ins += [mets[j], work, y, dx, cotangent, conv_input, halo, conv_weight, bias, tab]
        specs += [HBM] * 6 + here + [whole(table)]
        aliases = None
        if shared is not None:
            aliases = {len(ins) + i: i for i in range(3)}
            ins += shared
            specs += [HBM] * 3
        *shared, dreads[j], dkeys[j], scals[j] = call(
            functools.partial(finish_kernel, j, hops),
            ins,
            specs,
            shared_out + small_out,
            [HBM] * 3 + [whole(s) for s, _ in small_out],
            [
                vmem(*payload, I16), vmem(*payload, I16), vmem(STATE + 8, WIDTH), vmem(count, BC),
                vmem(*shape), vmem(*shape), vmem(*shape, BF16), vmem(*shape, BF16),
                vmem(*shape, BF16), vmem(*shape, BF16), vmem(24, WIDTH),
                vmem(count + 8, WIDTH), vmem(count + 16, WIDTH), sems(3 + 10), sems(3),
            ],
            aliases,
            us=5.0,
        )
        return shared

    received = [[] for _ in range(STREAMS)]
    swapped = [[] for _ in range(STREAMS)]
    shared = None
    turns = TURNS + hops - 1
    for turn in range(turns):
        if turn:
            sent = [
                hop(turn, hops, received[stream][-1], chips[stream::STREAMS])
                for stream in range(STREAMS)
            ]
        if turn == turns - 1:
            *sent, late = lax.optimization_barrier((*sent, work))
            withins.append(within(PIECES - 1, late))
        arrived = [permute(value, "seq", along(size)) for value in sent]
        for stream in range(STREAMS):
            got = arrived[stream]
            if turn == turns - 1:
                shared = finish(stream, shared)
                got, shared = lax.optimization_barrier((got, shared))
            received[stream].append(got)
            swapped[stream].append(other_core(got))
    for j in range(STREAMS, PIECES):
        shared = finish(j, shared)
    output, gin, misc = shared

    dscores = [group[2] for group in withins]
    small = (*dreads, *dkeys, *dscores, *scals)
    ins = (conv_input, halo, conv_weight, tab, work) + small + (gin, misc)
    bc_common = [part((count, BC), 0, BC_AT), part((CONV - 1, BC), 0, BC_AT), part((CONV, BC), 0, BC_AT)]
    gin, misc, packed = call(
        final_kernel,
        ins,
        bc_common + [whole(table), HBM] + full(*small) + [HBM] * 2,
        shared_out[1:] + [((16, THIRD), F32)],
        [part((count, BC), 0, BC_AT), part((24, BC), 0, BC_AT), whole((16, THIRD))],
        [
            vmem(count + 8, BC), vmem(count + 16, BC), vmem(count, SCORES), vmem(8, INNER), sems(2),
        ],
        {len(ins) - 2: 0, len(ins) - 1: 1},
    )

    returned = lax.ppermute(
        misc[8 - CONV + 1 : 8], "seq", [(i, i - 1) for i in range(1, size)]
    )
    lower, upper = packed[:8], packed[8:]
    first = core == 0
    value = jnp.where(first, lower, upper)
    value = value + other_core(jnp.where(first, upper, lower))
    value = xor_sum(value, "dp", 1)
    value, returned = lax.optimization_barrier((value, returned))
    grad_input = call(
        edge_kernel,
        (gin, misc, returned, docs),
        [edge, part((8, CH), 1, 0), *full(returned, docs)],
        [((count, CH), BF16)],
        [edge],
        aliases={0: 0},
    )[0]
    value = xor_sum(value, "seq", 2)
    value, grad_input = lax.optimization_barrier((value, grad_input))
    value = value * float(lax.axis_size("dp") * size * count) ** (-0.5)
    other = other_core(value)
    lower = jnp.where(first, value, other)
    upper = jnp.where(first, other, value)
    grad_weight = jnp.concatenate([lower[:CONV], lower[CONV:], upper[:CONV]], axis=1)
    grad_bias = upper[CONV : CONV + 3].reshape(CH)
    params = [upper[CONV + 3, i : i + HEADS] for i in (0, 128, 256)]
    return (output, grad_input, grad_weight, grad_bias, *params)


def solution(mesh):
    return jax.shard_map(
        on_device,
        mesh=mesh,
        in_specs=(
            P(("dp", "seq"), None),
            P(("dp", "seq")),
            P(),
            P(),
            P(("dp", "seq"), None),
            P(),
            P(),
            P(),
            P(("dp", "seq"), None),
        ),
        out_specs=(P(("dp", "seq"), None), P(("dp", "seq"), None), P(), P(), P(), P(), P()),
        check_vma=False,
    )
```

```python
import functools

import jax
import jax.numpy as jnp
from jax import lax
from jax.experimental import pallas as pl
from jax.experimental.pallas import tpu as pltpu
from jax.sharding import PartitionSpec as P

HEADS = 80
HEAD_DIM = 64
STATE = 128
CONV = 4
INNER = 5120
CH = 5376

STREAMS = 2
TURNS = 2
PIECES = STREAMS * TURNS
PIECE_HEADS = HEADS // PIECES
WIDTH = PIECE_HEADS * HEAD_DIM
SPAN = STREAMS * WIDTH
PAIR = 2 * HEAD_DIM
CHUNK = 256
BC = 2 * STATE
BC_AT = INNER // BC
FAR = -1e30
STATES, SMALL = 0, 256
BC_ACT, BC_SLOPE, SCORES, SMALLS = 0, 256, 512, 640
WORK_ROWS = 3328
CODE = 32766.0
THIRD = CH // 3
PER = CHUNK // HEAD_DIM

F32 = jnp.float32
BF16 = jnp.bfloat16
I16 = jnp.int16
EXACT = lax.Precision.HIGHEST
ACROSS = ((1,), (1,))
ANY = pl.BlockSpec(memory_space=pl.ANY)
HBM = pl.BlockSpec(memory_space=pltpu.HBM)
VMEM_LIMIT = 40 * 1024 * 1024

MASK, ENTRY, LEAVE, PULL, RATE, DECAY, RUN, FAR_AT, ROW, SMASK = range(0, 1280, 128)
SKIP = ROW + HEADS
TABLE = SMASK + 136


def iota(shape, dim):
    return lax.broadcasted_iota(jnp.int32, shape, dim)


def mm(a, b, contract=((1,), (0,))):
    return lax.dot_general(a, b, (contract, ((), ())), preferred_element_type=F32)


def halves(value):
    high = value.astype(BF16)
    return high, (value - high.astype(F32)).astype(BF16)


def lanes(*parts):
    return jnp.concatenate(parts, axis=1)


def rows(*parts):
    return jnp.concatenate(parts, axis=0)


def by_head(table, first, count):
    out = []
    for head in range(first, first + count, 2):
        shape = (table.shape[0], PAIR)
        left = jnp.broadcast_to(table[:, head : head + 1], shape)
        right = jnp.broadcast_to(table[:, head + 1 : head + 2], shape)
        out.append(jnp.where(iota(shape, 1) < HEAD_DIM, left, right))
    return lanes(*out)


def taps_of(ext_ref, cols, count, mask):
    taps = []
    for tap in range(CONV):
        back = CONV - 1 - tap
        value = ext_ref[8 - back : 8 - back + count, cols]
        taps.append(value if back == 0 else value * mask[back])
    return taps


def columns(table, width):
    shape = (table.shape[0], width)
    return [jnp.broadcast_to(table[:, i : i + 1], shape) for i in range(CONV)]


def activate(taps, cols, w_ref, b_ref):
    v = b_ref[:, cols] + w_ref[CONV - 1 : CONV, cols] * taps[CONV - 1]
    for tap in range(CONV - 2, -1, -1):
        v = v + w_ref[tap : tap + 1, cols] * taps[tap]
    gate = 1.0 / (1.0 + jnp.exp(-v))
    return v * gate, gate * (1.0 + v * (1.0 - gate))


class Flow:
    def __init__(self, sems):
        self.sems = sems
        self.used = 0

    def copy(self, source, target):
        made = pltpu.make_async_copy(source, target, self.sems.at[self.used])
        self.used += 1
        return made


def position(hops):
    index = lax.axis_index("seq")
    core = lax.rem(index, 2)
    chip = lax.div(index, 2)
    return core, jnp.where(core == 1, chip, hops - chip)


def at(first, width=CHUNK):
    return slice(first, first + width)


def tail_kernel(x_ref, doc_ref, out_ref):
    count = doc_ref.shape[1]
    edge = x_ref.shape[0] - CONV + 1
    cut = jnp.zeros((1, 1), F32)
    for back in range(CONV - 1):
        row = edge + CONV - 2 - back
        if back:
            cut = cut + doc_ref[:, count - back : count - back + 1].astype(F32)
        keep = (cut == 0.0).astype(F32)
        value = x_ref[row : row + 1, :].astype(F32) * keep
        out_ref[CONV - 2 - back : CONV - 1 - back, :] = value.astype(BF16)


def edge_kernel(gin_ref, misc_ref, back_ref, doc_ref, out_ref):
    count = doc_ref.shape[1]
    size = gin_ref.shape[0]
    cut = jnp.zeros((1, 1), F32)
    keeps = []
    for back in range(CONV - 1):
        if back:
            cut = cut + doc_ref[:, count - back : count - back + 1].astype(F32)
        keeps.insert(0, (cut == 0.0).astype(F32))
    place = iota((8, 1), 0)
    value = misc_ref[...]
    for i in range(CONV - 1):
        row = 8 - CONV + 1 + i
        value = value + jnp.where(place == row, back_ref[i : i + 1, :] * keeps[i], 0.0)
    out_ref[...] = gin_ref[...]
    out_ref[size - 8 :, :] = value.astype(BF16)


def prep_kernel(doc_ref, raw_ref, dtb_ref, alog_ref, skip_ref, tab_ref):
    count = raw_ref.shape[1]
    resets = doc_ref[...].astype(F32)
    t, s = iota((count, count), 0), iota((count, count), 1)

    def total(keep, shape):
        return jnp.sum(jnp.where(keep, jnp.broadcast_to(resets, shape), 0.0), axis=1, keepdims=True)

    square = (count, count)
    lane = iota((count, 128), 1)
    table = jnp.ones((count, 128), F32)
    for back in range(1, CONV):
        fits = (total((s <= t) & (s > t - back), square) == 0.0).astype(F32)
        table = jnp.where(lane == back, fits, table)
    tab_ref[MASK : MASK + count, :] = table
    wide = (count + 8, count)
    at, s_wide = iota(wide, 0) - 8, iota(wide, 1)
    lane, place = iota((count + 8, 128), 1), iota((count + 8, 128), 0) - 8
    table = jnp.zeros((count + 8, 128), F32)
    for ahead in range(CONV):
        fits = (total((s_wide > at) & (s_wide <= at + ahead), wide) == 0.0).astype(F32)
        fits = jnp.where((place + ahead >= 0) & (place + ahead < count), fits, 0.0)
        table = jnp.where(lane == ahead, fits, table)
    tab_ref[SMASK : SMASK + count + 8, :] = table
    segment = total(s <= t, square)
    reset_col = total(s == t, square)
    segment_row = jnp.sum(
        jnp.where(t <= s, jnp.broadcast_to(reset_col, square), 0.0), axis=0, keepdims=True
    )
    causal = (s <= t) & (segment == segment_row)
    tab_ref[FAR_AT : FAR_AT + count, :] = jnp.where(causal, 0.0, FAR)
    raw = rows(raw_ref[...], jnp.zeros((128 - HEADS, count), F32)).T[:, :HEADS]
    v = raw + dtb_ref[...]
    dt = jnp.maximum(v, 0.0) + jnp.log1p(jnp.exp(-jnp.abs(v)))
    rate = -jnp.exp(alog_ref[...])
    decay = rate * dt
    run = jnp.dot((s <= t).astype(F32), decay, precision=EXACT, preferred_element_type=F32)
    end = run[count - 1 : count, :]
    last = segment == segment[count - 1 : count, :]
    gate = 1.0 / (1.0 + jnp.exp(-v))
    fill = jnp.zeros((count, 128 - HEADS), F32)

    def put(where, value):
        tab_ref[where : where + count, :] = lanes(value, fill)

    put(ENTRY, jnp.where(segment == 0.0, jnp.exp(run), 0.0))
    put(LEAVE, jnp.where(last, jnp.exp(end - run) * dt, 0.0))
    put(PULL, gate / dt)
    put(RATE, rate * gate)
    put(DECAY, decay)
    put(RUN, run)
    tab_ref[ROW : ROW + 128, :] = lanes(jnp.log(dt) - run, fill).T
    tab_ref[SKIP : SKIP + 1, :] = lanes(skip_ref[...], fill[:1])


def scores_of(act):
    keys, reads = act[:, :STATE], act[:, STATE:]
    return lax.dot_general(
        reads, keys, (ACROSS, ((), ())), precision=EXACT, preferred_element_type=F32
    )


def local_kernel(x_ref, halo_ref, w_ref, b_ref, cot_ref, tab_ref, *refs):
    send_refs = refs[:PIECES]
    work_ref = refs[PIECES]
    xb, cb, nb, mb, sb, ext_ref, in_sems, out_sems = refs[-8:]
    count = xb.shape[0]
    come, go = Flow(in_sems), Flow(out_sems)
    first = come.copy(x_ref.at[:, at(INNER, BC)], xb.at[:, at(INNER, BC)])
    first.start()
    arriving, leaving = [], []
    for piece in range(PIECES):
        cols = at(piece * WIDTH, WIDTH)
        pair = (
            come.copy(x_ref.at[:, cols], xb.at[:, cols]),
            come.copy(cot_ref.at[:, cols], cb.at[:, cols]),
        )
        for copy in pair:
            copy.start()
        arriving.append(pair)
    mask = columns(tab_ref[MASK : MASK + count, :], CHUNK)

    def act_of(cols):
        ext_ref[8 : 8 + count, cols] = xb[:, cols].astype(F32)
        ext_ref[8 - CONV + 1 : 8, cols] = halo_ref[:, cols].astype(F32)
        return activate(taps_of(ext_ref, cols, count, mask), cols, w_ref, b_ref)

    first.wait()
    act, slope = act_of(at(INNER, BC))
    sb[:, at(BC_ACT)] = act
    sb[:, at(BC_SLOPE)] = slope
    sb[:, at(SCORES, 128)] = scores_of(act)
    copy = go.copy(sb, work_ref.at[at(SMALL, count), at(0, SMALLS)])
    copy.start()
    leaving.append(copy)
    turned = rows(act[:, :STATE].T, act[:, STATE:].T)
    keys, reads = halves(turned[:STATE, :]), halves(turned[STATE:, :])
    keys_both, reads_both = lanes(*keys), lanes(*reads)
    entry, leave = tab_ref[ENTRY : ENTRY + count, :], tab_ref[LEAVE : LEAVE + count, :]
    first_core = lax.rem(lax.axis_index("seq"), 2) == 0
    for piece in range(PIECES):
        for copy in arriving[piece]:
            copy.wait()
        for start in range(piece * WIDTH, (piece + 1) * WIDTH, CHUNK):
            cols = at(start)
            head = start // HEAD_DIM
            act, _ = act_of(cols)
            e = by_head(entry, head, PER)
            lx_high, lx_low = halves(act * by_head(leave, head, PER))
            ey_high, ey_low = halves(cb[:, cols].astype(F32) * e)
            state = mm(keys_both, rows(lx_high, lx_high)) + mm(keys[0], lx_low)
            adjoint = mm(reads_both, rows(ey_high, ey_high)) + mm(reads[0], ey_low)
            nb[:STATE, cols] = jnp.where(first_core, state, adjoint)
            mb[:STATE, cols] = jnp.where(first_core, adjoint, state)
            through = jnp.broadcast_to(e[count - 1 : count, :], (8, CHUNK))
            nb[STATE:, cols] = through
            mb[STATE:, cols] = through
        cols = at(piece * WIDTH, WIDTH)
        for source, target in ((nb, send_refs[piece]), (mb, work_ref.at[at(STATES, STATE + 8), cols])):
            copy = go.copy(source.at[:, cols], target)
            copy.start()
            leaving.append(copy)
    for copy in leaving:
        copy.wait()


def decode(codes):
    scale = jnp.exp2(codes[STATE : STATE + 1, :].astype(F32) * (1.0 / 256.0)) * (1.0 / CODE)
    return codes[:STATE, :].astype(F32) * scale


def encode(value):
    most = jnp.max(jnp.abs(value), axis=0, keepdims=True)
    power = jnp.ceil(jnp.log2(jnp.maximum(most, 1e-30)) * 256.0)
    scale = jnp.exp2(power * (1.0 / 256.0)) * (1.0 / CODE)
    codes = jnp.floor(value * (1.0 / scale) + 0.5).astype(jnp.int32)
    tail = jnp.broadcast_to(power.astype(jnp.int32), (16, value.shape[1]))
    return rows(codes, tail).astype(I16)


def chip_kernel(piece, work_ref, met_ref, *refs):
    chip_ref = refs[0]
    mb, eb, sem = refs[-3:]
    come = Flow(sem)
    mine = work_ref.at[at(STATES, STATE + 8), at(piece * WIDTH, WIDTH)]
    copies = [come.copy(mine, mb), come.copy(met_ref, eb)]
    for copy in copies:
        copy.start()
    for copy in copies:
        copy.wait()
    for start in range(0, WIDTH, CHUNK):
        cols = at(start)
        own = mb[STATE : STATE + 1, cols]
        value = mb[:STATE, cols] + own * eb[:STATE, cols]
        chip_ref[:STATE, cols] = value
        chip_ref[STATE:, cols] = own * eb[STATE:, cols]
        if piece < STREAMS:
            refs[1][:, cols] = encode(value)


def hop_kernel(turn, hops, previous_ref, *refs):
    chip_refs, out_ref = refs[:-1], refs[-1]
    _, place = position(hops)
    for start in range(0, WIDTH, CHUNK):
        cols = at(start)
        chip = chip_refs[0][:, cols]
        for i, ref in enumerate(chip_refs[1:]):
            chip = jnp.where(turn - place > i, ref[:, cols], chip)
        before = jnp.where(place == 0, 0.0, decode(previous_ref[:, cols]))
        out_ref[:, cols] = encode(chip[:STATE, :] + chip[STATE : STATE + 1, :] * before)


def within_kernel(
    piece, x_ref, cot_ref, work_ref, halo_ref, w_ref, b_ref, tab_ref, y_ref, dx_ref, dscores_ref, *refs
):
    xb, cb, sb, yb, db, ext_ref, in_sems, out_sems = refs
    count = xb.shape[0]
    come, go = Flow(in_sems), Flow(out_sems)
    copies = (
        come.copy(x_ref.at[:, at(piece * WIDTH, WIDTH)], xb),
        come.copy(cot_ref.at[:, at(piece * WIDTH, WIDTH)], cb),
        come.copy(work_ref.at[at(SMALL, count), at(SCORES, count)], sb),
    )
    for copy in copies:
        copy.start()
    mask = columns(tab_ref[MASK : MASK + count, :], PAIR)
    for copy in copies:
        copy.wait()
    run = tab_ref[RUN : RUN + count, :]
    far, scores = tab_ref[FAR_AT : FAR_AT + count, :], sb[...]
    left = iota((count, PAIR), 1) < HEAD_DIM
    total = jnp.zeros((count, count), F32)
    zero = jnp.zeros((count, PAIR), BF16)
    for pair in range(PIECE_HEADS // 2):
        cols = at(pair * PAIR, PAIR)
        ext_ref[8 : 8 + count, cols] = xb[:, cols].astype(F32)
        ext_ref[8 - CONV + 1 : 8, cols] = halo_ref[:, cols].astype(F32)
        act, _ = activate(taps_of(ext_ref, cols, count, mask), cols, w_ref, b_ref)
        x_high, x_low = halves(act)
        upstream = cb[:, cols]
        upstream_turned = upstream.astype(F32).T.astype(BF16)
        spread, weights = [], []
        for side in range(2):
            head = piece * PIECE_HEADS + 2 * pair + side
            row = tab_ref[ROW + head : ROW + head + 1, :]
            within = jnp.exp(run[:, head : head + 1] + row + far)
            spread.append(within)
            weights.append(lanes(*halves(within * scores)))
        out = mm(rows(*weights), rows(lanes(x_high, x_low), lanes(x_high, zero)))
        out = out[:, :PAIR] + out[:, PAIR:]
        yb[:, cols] = jnp.where(left, out[:count], out[count:])
        parts = []
        for side in range(2):
            mine = upstream_turned[side * HEAD_DIM : (side + 1) * HEAD_DIM, :]
            pushed = rows(weights[side][:, :count], weights[side][:, count:])
            parts.append(mm(lanes(mine, mine), pushed))
        db[:, cols] = rows(*parts).T
        up_left, up_right = jnp.where(left, upstream, zero), jnp.where(left, zero, upstream)
        lhs = rows(lanes(up_left, up_left), lanes(up_right, up_right))
        products = mm(lhs, lanes(x_high, x_low), ACROSS)
        total = total + spread[0] * products[:count] + spread[1] * products[count:]
    copies = (go.copy(yb, y_ref), go.copy(db, dx_ref))
    for copy in copies:
        copy.start()
    dscores_ref[...] = total
    for copy in copies:
        copy.wait()


def conv_back(dconv, taps, w, z_ref, z_cols, smask):
    count, width = dconv.shape
    z_ref[8 : 8 + count, z_cols] = dconv
    grad = jnp.zeros((count + 8, width), F32)
    for ahead in range(CONV):
        tap = CONV - 1 - ahead
        shifted = z_ref[ahead : ahead + count + 8, z_cols]
        grad = grad + w[tap : tap + 1, :] * (shifted * smask[ahead])
    sums = [jnp.sum(dconv * tap, axis=0, keepdims=True) for tap in taps]
    sums.append(jnp.sum(dconv, axis=0, keepdims=True))
    sums.append(jnp.zeros((3, width), F32))
    return grad[8:].astype(BF16), rows(grad[:8], grad[count:], *sums)


def clear_edges(z_ref, count):
    z_ref[0:8, :] = jnp.zeros((8, z_ref.shape[1]), F32)
    z_ref[8 + count : 16 + count, :] = jnp.zeros((8, z_ref.shape[1]), F32)


def finish_kernel(piece, hops, *refs):
    incs, exchs = refs[:hops], refs[hops : 2 * hops]
    refs = refs[2 * hops :]
    met_ref, work_ref, y_ref, dx_ref, cot_ref, x_ref, halo_ref, w_ref, b_ref, tab_ref = refs[:10]
    out_ref, gin_ref, misc_ref, dreads_ref, dkeys_ref, scal_ref = refs[-21:-15]
    ib, hb, eb, bc, yb, db, cb, xb, ob, gb, nb, ext_ref, z_ref, in_sems, out_sems = refs[-15:]
    count = xb.shape[0]
    come, go = Flow(in_sems), Flow(out_sems)
    base = piece * WIDTH
    core, place = position(hops)
    first = come.copy(work_ref.at[at(SMALL, count), at(BC_ACT)], bc)
    first.start()
    choices = []
    for here, sources, buffer in ((place, incs, ib), (hops - place, exchs, hb)):
        sem = come.used
        come.used += 1
        for i, source in enumerate(sources):
            choices.append((here == i + 1, pltpu.make_async_copy(source, buffer, come.sems.at[sem])))

        @pl.when(here == 0)
        def _():
            buffer[...] = jnp.zeros(buffer.shape, I16)

    for chosen, copy in choices:
        pl.when(chosen)(copy.start)
    arriving, leaving = [], []
    for start, width in ((0, CHUNK), (CHUNK, WIDTH - CHUNK)):
        cols = at(start, width)
        whole_cols = at(base + start, width)
        group = [
            come.copy(met_ref.at[:, cols], eb.at[:, cols]),
            come.copy(y_ref.at[:, cols], yb.at[:, cols]),
            come.copy(dx_ref.at[:, cols], db.at[:, cols]),
            come.copy(cot_ref.at[:, whole_cols], cb.at[:, cols]),
            come.copy(x_ref.at[:, whole_cols], xb.at[:, cols]),
        ]
        for copy in group:
            copy.start()
        arriving.append(group)
    clear_edges(z_ref, count)
    first.wait()
    keys, reads = halves(bc[:, :STATE]), halves(bc[:, STATE:])
    keys_both, reads_both = lanes(*keys), lanes(*reads)
    entry, leave = tab_ref[ENTRY : ENTRY + count, :], tab_ref[LEAVE : LEAVE + count, :]
    skip = tab_ref[SKIP : SKIP + 1, :]
    first_core = core == 0
    mask = columns(tab_ref[MASK : MASK + count, :], CHUNK)
    smask = columns(tab_ref[SMASK : SMASK + count + 8, :], CHUNK)
    dreads = jnp.zeros((count, STATE), F32)
    dkeys = jnp.zeros((count, STATE), F32)
    sums = jnp.zeros((4 * count + 16, 128), F32)
    for chosen, copy in choices:
        pl.when(chosen)(copy.wait)
    for start in range(0, WIDTH, CHUNK):
        cols = at(start)
        head = (base + start) // HEAD_DIM
        if start <= CHUNK:
            for copy in arriving[start // CHUNK]:
                copy.wait()
        inc, exch = decode(ib[:, cols]), decode(hb[:, cols])
        mine = eb[STATE : STATE + 1, cols] * inc + eb[:STATE, cols]
        state = jnp.where(first_core, exch, mine)
        adjoint = jnp.where(first_core, mine, exch)
        s_high, s_low = halves(state)
        a_high, a_low = halves(adjoint)
        e, leaves = by_head(entry, head, PER), by_head(leave, head, PER)
        ext_ref[8 : 8 + count, cols] = xb[:, cols].astype(F32)
        ext_ref[8 - CONV + 1 : 8, cols] = halo_ref[:, cols].astype(F32)
        taps = taps_of(ext_ref, cols, count, mask)
        act, slope = activate(taps, cols, w_ref, b_ref)
        up = cb[:, cols].astype(F32)
        carried = mm(reads_both, rows(s_high, s_high)) + mm(reads[0], s_low)
        y = yb[:, cols] + e * carried
        back = mm(keys_both, rows(a_high, a_high)) + mm(keys[0], a_low)
        back = leaves * back
        dx = db[:, cols] + back
        gain = by_head(skip, head, PER)
        ob[:, cols] = (y + gain * act).astype(BF16)
        ey_high, ey_low = halves(up * e)
        lx_high, lx_low = halves(act * leaves)
        dreads = dreads + mm(lanes(ey_high, ey_high, ey_low), lanes(s_high, s_low, s_high), ACROSS)
        dkeys = dkeys + mm(lanes(lx_high, lx_high, lx_low), lanes(a_high, a_low, a_high), ACROSS)
        through = e[count - 1 : count, :]
        end = jnp.sum(act * back, axis=0, keepdims=True)
        end = end + through * jnp.sum(state * adjoint, axis=0, keepdims=True)
        direct = jnp.sum(up * act, axis=0, keepdims=True)
        received = act * dx
        small = halves(rows(end, direct, jnp.zeros((6, CHUNK), F32)))
        stack = halves(up * y - received) + halves(received)
        pick = (iota((CHUNK, 128), 1) == head + iota((CHUNK, 128), 0) // HEAD_DIM).astype(BF16)
        sums = sums + mm(rows(*stack, rows(*small)), pick)
        dconv = (dx + gain * up) * slope
        gb[:, cols], nb[:, cols] = conv_back(dconv, taps, w_ref[:, cols], z_ref, cols, smask)
    for source, target in ((ob, out_ref), (gb, gin_ref), (nb, misc_ref)):
        copy = go.copy(source, target.at[:, at(base, WIDTH)])
        copy.start()
        leaving.append(copy)
    dreads_ref[...] = dreads
    dkeys_ref[...] = dkeys
    drun = sums[:count] + sums[count : 2 * count]
    received = sums[2 * count : 3 * count] + sums[3 * count : 4 * count]
    small = sums[4 * count : 4 * count + 8] + sums[4 * count + 8 :]
    drun = drun + jnp.where(iota((count, 128), 0) == count - 1, small[0:1, :], 0.0)
    later = (iota((count, count), 1) >= iota((count, count), 0)).astype(F32)
    ddecay = jnp.dot(later, drun, precision=EXACT, preferred_element_type=F32)
    pull, rate = tab_ref[PULL : PULL + count, :], tab_ref[RATE : RATE + count, :]
    ddtb = jnp.sum(received * pull + ddecay * rate, axis=0, keepdims=True)
    dalog = jnp.sum(ddecay * tab_ref[DECAY : DECAY + count, :], axis=0, keepdims=True)
    scal_ref[...] = rows(ddtb, dalog, small[1:2, :], jnp.zeros((5, 128), F32))
    for copy in leaving:
        copy.wait()


def final_kernel(x_ref, halo_ref, w_ref, tab_ref, work_ref, *refs):
    gin_ref, misc_ref, packed_ref, ext_ref, z_ref, sb, gb, sem = refs[-8:]
    gathered = pltpu.make_async_copy(refs[-9].at[at(16, 8), at(0, INNER)], gb, sem.at[1])
    gathered.start()
    parts = refs[: 4 * PIECES]
    count = x_ref.shape[0]
    copy = pltpu.make_async_copy(work_ref.at[at(SMALL, count), at(0, SCORES)], sb, sem.at[0])
    copy.start()
    ext_ref[8 : 8 + count, :] = x_ref[...].astype(F32)
    ext_ref[8 - CONV + 1 : 8, :] = halo_ref[...].astype(F32)
    clear_edges(z_ref, count)
    total = []
    for kind in range(4):
        value = parts[kind * PIECES][...]
        for piece in range(1, PIECES):
            value = value + parts[kind * PIECES + piece][...]
        total.append(value)
    dreads, dkeys, dscores, scal = total
    copy.wait()
    keys, reads = sb[:, at(BC_ACT, STATE)], sb[:, at(BC_ACT + STATE, STATE)]
    dreads = dreads + jnp.dot(dscores, keys, precision=EXACT, preferred_element_type=F32)
    dkeys = dkeys + jnp.dot(dscores.T, reads, precision=EXACT, preferred_element_type=F32)
    cols = slice(0, BC)
    dconv = lanes(dkeys, dreads) * sb[:, at(BC_SLOPE)]
    taps = taps_of(ext_ref, cols, count, columns(tab_ref[MASK : MASK + count, :], BC))
    smask = columns(tab_ref[SMASK : SMASK + count + 8, :], BC)
    gin_ref[...], misc = conv_back(dconv, taps, w_ref[...], z_ref, cols, smask)
    misc_ref[...] = misc
    gathered.wait()
    grads = lanes(gb[...], misc[16:, :])
    thirds = [grads[:, at(i * THIRD, THIRD)] for i in range(3)]
    packed_ref[0:8, :] = rows(thirds[0][:CONV], thirds[1][:CONV])
    fill = jnp.zeros((1, THIRD - 384), F32)
    params = lanes(scal[0:1, :], scal[1:2, :], scal[2:3, :], fill)
    last = [third[CONV : CONV + 1] for third in thirds]
    packed_ref[8:16, :] = rows(thirds[2][:CONV], *last, params)


def cost(us):
    return pl.CostEstimate(flops=int(us * 1.1e9), bytes_accessed=1000, transcendentals=0)


def whole(shape):
    return pl.BlockSpec(shape, lambda *_: (0,) * len(shape))


def part(shape, *index):
    return pl.BlockSpec(shape, lambda *_: index)


def full(*arrays):
    return [whole(a.shape) for a in arrays]


def call(kernel, ins, specs, outs, out_specs, scratch=(), aliases=None, us=1.0):
    return pl.pallas_call(
        kernel,
        grid=(1,),
        in_specs=specs,
        out_specs=out_specs,
        out_shape=[jax.ShapeDtypeStruct(shape, dtype) for shape, dtype in outs],
        scratch_shapes=list(scratch),
        input_output_aliases=aliases or {},
        compiler_params=pltpu.CompilerParams(vmem_limit_bytes=VMEM_LIMIT),
        cost_estimate=cost(us),
    )(*ins)


def vmem(rows_, cols, dtype=F32):
    return pltpu.VMEM((rows_, cols), dtype)


def sems(count):
    return pltpu.SemaphoreType.DMA((count,))


def permute(value, axis, target):
    size = lax.axis_size(axis)
    return lax.ppermute(value, axis, [(i, target(i)) for i in range(size)])


def other_core(value):
    return permute(value, "seq", lambda i: i ^ 1)


def along(size):
    def target(i):
        if i % 2 == 1:
            return i + 2 if i + 2 < size else i - 1
        return i - 2 if i >= 2 else i + 1

    return target


def xor_sum(value, axis, low):
    size = lax.axis_size(axis)
    bit = low
    while bit < size:
        if 2 * bit < size:
            one = permute(value, axis, lambda i: i ^ bit)
            two = permute(value, axis, lambda i: i ^ (2 * bit))
            three = permute(value, axis, lambda i: i ^ (3 * bit))
            value = (value + one) + (two + three)
            bit *= 4
        else:
            value = value + permute(value, axis, lambda i: i ^ bit)
            bit *= 2
    return value


def chip_of(piece, work, met):
    state = (STATE + 8, WIDTH)
    payload = (STATE + 16, WIDTH)
    outs = [(state, F32)] + [(payload, I16)] * (piece < STREAMS)
    return call(
        functools.partial(chip_kernel, piece),
        (work, met),
        [HBM] * 2,
        outs,
        [whole(s) for s, _ in outs],
        [vmem(*state), vmem(*state), sems(2)],
        us=1.5,
    )


def hop(turn, hops, previous, chips):
    payload = (STATE + 16, WIDTH)
    return call(
        functools.partial(hop_kernel, turn, hops),
        (previous, *chips),
        full(previous, *chips),
        [(payload, I16)],
        [whole(payload)],
        us=0.8,
    )[0]


def on_device(
    conv_input, doc_start, conv_weight, conv_bias, dt_raw, dt_bias, a_log, skip_gain, cotangent
):
    count = conv_input.shape[0]
    size = lax.axis_size("seq")
    core = lax.rem(lax.axis_index("seq"), 2)
    hops = size // 2 - 1
    docs = doc_start[None, :]
    edge = part((16, CH), count // 16 - 1, 0)

    tail_out = call(
        tail_kernel, (conv_input, docs), [edge, whole(docs.shape)],
        [((CONV - 1, CH), BF16)], [whole((CONV - 1, CH))],
    )[0]
    halo = lax.ppermute(tail_out, "seq", [(i, i + 1) for i in range(size - 1)])

    bias = conv_bias[None, :]
    prep_in = (docs, dt_raw.T, dt_bias[None, :], a_log[None, :], skip_gain[None, :])
    table = (TABLE, 128)
    tab = call(prep_kernel, prep_in, full(*prep_in), [(table, F32)], [whole(table)])[0]

    square = (count, count)
    payload = (STATE + 16, WIDTH)
    shape = (count, WIDTH)
    ins = (conv_input, halo, conv_weight, bias, cotangent, tab)
    outs = [(STATE + 8, WIDTH)] * PIECES + [(WORK_ROWS, INNER)]
    got = call(
        local_kernel,
        ins,
        [HBM, *full(halo, conv_weight, bias), HBM, whole(table)],
        [(s, F32) for s in outs],
        [HBM] * len(outs),
        [
            vmem(count, CH, BF16), vmem(count, INNER, BF16), vmem(STATE + 8, INNER),
            vmem(STATE + 8, INNER), vmem(count, SMALLS), vmem(count + 8, CH),
            sems(2 * PIECES + 1), sems(2 * PIECES + 1),
        ],
        us=8.0,
    )
    *sends, work = got
    mets = [other_core(send) for send in sends]
    chips, sent = [], []
    for j in range(PIECES):
        chip, *first = chip_of(j, work, mets[j])
        chips.append(chip)
        sent += first

    def within(j, work):
        here = [part((height, WIDTH), 0, j) for height in (CONV - 1, CONV, 1)]
        return call(
            functools.partial(within_kernel, j),
            (conv_input, cotangent, work, halo, conv_weight, bias, tab),
            [HBM, HBM, HBM, *here, whole(table)],
            [(shape, F32), (shape, F32), (square, F32)],
            [HBM, HBM, whole(square)],
            [
                vmem(*shape, BF16), vmem(*shape, BF16), vmem(*square), vmem(*shape),
                vmem(*shape), vmem(count + 8, WIDTH), sems(3), sems(2),
            ],
            us=2.0,
        )

    withins = [within(j, work) for j in range(PIECES - 1)]
    dreads, dkeys, scals = [None] * PIECES, [None] * PIECES, [None] * PIECES
    shared_out = [((count, INNER), BF16), ((count, CH), BF16), ((24, CH), F32)]
    small_out = [((count, STATE), F32), ((count, STATE), F32), ((8, 128), F32)]

    def finish(j, shared):
        turn, stream = j // STREAMS, j % STREAMS
        here = [part((height, WIDTH), 0, j) for height in (CONV - 1, CONV, 1)]
        y, dx, _ = withins[j]
        ins = [*received[stream][turn : turn + hops], *swapped[stream][turn : turn + hops]]
        specs = [ANY] * (2 * hops)
        ins += [mets[j], work, y, dx, cotangent, conv_input, halo, conv_weight, bias, tab]
        specs += [HBM] * 6 + here + [whole(table)]
        aliases = None
        if shared is not None:
            aliases = {len(ins) + i: i for i in range(3)}
            ins += shared
            specs += [HBM] * 3
        *shared, dreads[j], dkeys[j], scals[j] = call(
            functools.partial(finish_kernel, j, hops),
            ins,
            specs,
            shared_out + small_out,
            [HBM] * 3 + [whole(s) for s, _ in small_out],
            [
                vmem(*payload, I16), vmem(*payload, I16), vmem(STATE + 8, WIDTH), vmem(count, BC),
                vmem(*shape), vmem(*shape), vmem(*shape, BF16), vmem(*shape, BF16),
                vmem(*shape, BF16), vmem(*shape, BF16), vmem(24, WIDTH),
                vmem(count + 8, WIDTH), vmem(count + 16, WIDTH), sems(3 + 10), sems(3),
            ],
            aliases,
            us=5.0,
        )
        return shared

    received = [[] for _ in range(STREAMS)]
    swapped = [[] for _ in range(STREAMS)]
    shared = None
    turns = TURNS + hops - 1
    for turn in range(turns):
        if turn:
            sent = [
                hop(turn, hops, received[stream][-1], chips[stream::STREAMS])
                for stream in range(STREAMS)
            ]
        if turn == turns - 1:
            *sent, late = lax.optimization_barrier((*sent, work))
            withins.append(within(PIECES - 1, late))
        arrived = [permute(value, "seq", along(size)) for value in sent]
        for stream in range(STREAMS):
            got = arrived[stream]
            if turn == turns - 1:
                shared = finish(stream, shared)
                got, shared = lax.optimization_barrier((got, shared))
            received[stream].append(got)
            swapped[stream].append(other_core(got))
    for j in range(STREAMS, PIECES):
        shared = finish(j, shared)
    output, gin, misc = shared

    dscores = [group[2] for group in withins]
    small = (*dreads, *dkeys, *dscores, *scals)
    ins = (conv_input, halo, conv_weight, tab, work) + small + (gin, misc)
    bc_common = [part((count, BC), 0, BC_AT), part((CONV - 1, BC), 0, BC_AT), part((CONV, BC), 0, BC_AT)]
    gin, misc, packed = call(
        final_kernel,
        ins,
        bc_common + [whole(table), HBM] + full(*small) + [HBM] * 2,
        shared_out[1:] + [((16, THIRD), F32)],
        [part((count, BC), 0, BC_AT), part((24, BC), 0, BC_AT), whole((16, THIRD))],
        [
            vmem(count + 8, BC), vmem(count + 16, BC), vmem(count, SCORES), vmem(8, INNER), sems(2),
        ],
        {len(ins) - 2: 0, len(ins) - 1: 1},
    )

    returned = lax.ppermute(
        misc[8 - CONV + 1 : 8], "seq", [(i, i - 1) for i in range(1, size)]
    )
    lower, upper = packed[:8], packed[8:]
    first = core == 0
    value = jnp.where(first, lower, upper)
    value = value + other_core(jnp.where(first, upper, lower))
    value = xor_sum(value, "dp", 1)
    value, returned = lax.optimization_barrier((value, returned))
    grad_input = call(
        edge_kernel,
        (gin, misc, returned, docs),
        [edge, part((8, CH), 1, 0), *full(returned, docs)],
        [((count, CH), BF16)],
        [edge],
        aliases={0: 0},
    )[0]
    value = xor_sum(value, "seq", 2)
    value, grad_input = lax.optimization_barrier((value, grad_input))
    value = value * float(lax.axis_size("dp") * size * count) ** (-0.5)
    other = other_core(value)
    lower = jnp.where(first, value, other)
    upper = jnp.where(first, other, value)
    grad_weight = jnp.concatenate([lower[:CONV], lower[CONV:], upper[:CONV]], axis=1)
    grad_bias = jnp.concatenate([upper[CONV + i] for i in range(3)])
    params = [upper[CONV + 3, i : i + HEADS] for i in (0, 128, 256)]
    return (output, grad_input, grad_weight, grad_bias, *params)


def solution(mesh):
    return jax.shard_map(
        on_device,
        mesh=mesh,
        in_specs=(
            P(("dp", "seq"), None),
            P(("dp", "seq")),
            P(),
            P(),
            P(("dp", "seq"), None),
            P(),
            P(),
            P(),
            P(("dp", "seq"), None),
        ),
        out_specs=(P(("dp", "seq"), None), P(("dp", "seq"), None), P(), P(), P(), P(), P()),
        check_vma=False,
    )
```
